32 devices in a mesh: dp: 4 (over y, x), fsdp: 8 (over z, core).
Axes of the slice: x: 2, y: 2, z: 4, core: 2. Of those that a mesh axis runs over, the one named last changes fastest.
Arguments:
- frames: bfloat16 [32768, 768], P(('dp', 'fsdp')), may hold values from -6 to 6
- cotangent: bfloat16 [32768, 768], P(('dp', 'fsdp')), may hold values from -6 to 6
- lengths: int32 [32, 7], P(('dp', 'fsdp')), may hold values from 0 to 780, as said below
- qkv_master: float32 [3, 768, 768], P(None, ('dp', 'fsdp')), may hold values from -0.21875 to 0.21875
- out_master: float32 [768, 768], P(('dp', 'fsdp')), may hold values from -1.5 to 1.5
- up_master: float32 [768, 3072], P(('dp', 'fsdp')), may hold values from -0.21875 to 0.21875
- down_master: float32 [3072, 768], P(('dp', 'fsdp')), may hold values from -0.109375 to 0.109375
- vector_master: float32 [9216], P(('dp', 'fsdp')), may hold values from -2 to 2, as said below
- qkv_first: float32 [3, 768, 768], P(None, ('dp', 'fsdp')), may hold values from -80 to 80
- qkv_second: float32 [3, 768, 768], P(None, ('dp', 'fsdp')), may hold values from 128.3457 to 2053.5312
- out_first: float32 [768, 768], P(('dp', 'fsdp')), may hold values from -14 to 14
- out_second: float32 [768, 768], P(('dp', 'fsdp')), may hold values from 4.5121536 to 72.19446
- up_first: float32 [768, 3072], P(('dp', 'fsdp')), may hold values from -56 to 56
- up_second: float32 [768, 3072], P(('dp', 'fsdp')), may hold values from 72.19446 to 1155.1113
- down_first: float32 [3072, 768], P(('dp', 'fsdp')), may hold values from -56 to 56
- down_second: float32 [3072, 768], P(('dp', 'fsdp')), may hold values from 72.19446 to 1155.1113
- vector_first: float32 [9216], P(('dp', 'fsdp')), may hold values from -96 to 96
- vector_second: float32 [9216], P(('dp', 'fsdp')), may hold values from 200.54016 to 3208.6426
Outputs:
- layer_output: bfloat16 [32768, 768], P(('dp', 'fsdp'))
- frames_grad: bfloat16 [32768, 768], P(('dp', 'fsdp'))
- layer_rms: float32 [4], replicated
- qkv_first_new: float32 [3, 768, 768], P(None, ('dp', 'fsdp'))
- qkv_second_new: float32 [3, 768, 768], P(None, ('dp', 'fsdp'))
- qkv_master_new: float32 [3, 768, 768], P(None, ('dp', 'fsdp'))
- qkv_weight_low: bfloat16 [3, 768, 768], P(None, ('dp', 'fsdp'))
- out_first_new: float32 [768, 768], P(('dp', 'fsdp'))
- out_second_new: float32 [768, 768], P(('dp', 'fsdp'))
- out_master_new: float32 [768, 768], P(('dp', 'fsdp'))
- out_weight_low: bfloat16 [768, 768], P(('dp', 'fsdp'))
- up_first_new: float32 [768, 3072], P(('dp', 'fsdp'))
- up_second_new: float32 [768, 3072], P(('dp', 'fsdp'))
- up_master_new: float32 [768, 3072], P(('dp', 'fsdp'))
- up_weight_low: bfloat16 [768, 3072], P(('dp', 'fsdp'))
- down_first_new: float32 [3072, 768], P(('dp', 'fsdp'))
- down_second_new: float32 [3072, 768], P(('dp', 'fsdp'))
- down_master_new: float32 [3072, 768], P(('dp', 'fsdp'))
- down_weight_low: bfloat16 [3072, 768], P(('dp', 'fsdp'))
- vector_first_new: float32 [9216], P(('dp', 'fsdp'))
- vector_second_new: float32 [9216], P(('dp', 'fsdp'))
- vector_master_new: float32 [9216], P(('dp', 'fsdp'))
- vector_weight_low: bfloat16 [9216], P(('dp', 'fsdp'))
The draws below stay inside these ranges and needn't reach their ends.
Inputs may be any that keep to these rules, and one draw needn't show every extreme that they name: Each row holds 780 or 0 in its first slot, then some entries 150, then zeros; it has at least one clip, and its lengths sum to at most 900, which some row reaches. `vector_master`: the gain entries (g_1, g_2) lie between 0.5 and 1.5.
All inputs are finite; a program needn't handle non-finite values.
Results may differ from the reference program's by a relative error of at most 0.015.
The reference program's roundings to bfloat16 on the way count: a program that leaves them out, or rounds other values in their place, can miss the bound.
Values may be sent and summed in bfloat16 or wider, within the bound.
No kernel may reach another device: no remote copies, remote signals or barrier semaphores. Data moves between devices by JAX's collectives and lax.ppermute only.
A program may use at most 256 MiB of HBM per device.

```python
import math
import jax
import jax.numpy as jnp
from jax import lax

D = 768
HEADS = 12
HD = 64
FF = 3072
FR_DEV = 1024
SHORT = 150
LONG = 780
QBLK = 512
STEP = 10
GROUPS = 32
FRAMES = 32768
PV = 9216
N_DP = 4
N_FSDP = 8


def draw_lengths(key, part):
    key = jax.random.fold_in(key, 2)
    subkeys = jax.random.split(key, 2)
    groups = N_DP * N_FSDP
    most_clips = FR_DEV // SHORT
    least_clips = max(1, most_clips // 3)
    device = jnp.arange(groups, dtype=jnp.int32)
    inner_index = device % N_FSDP
    outer_index = device // N_FSDP
    span_inner = max(N_FSDP - 1, 1)
    span_outer = max(N_DP - 1, 1)
    rise_rank = inner_index * span_outer + outer_index * span_inner
    clip_count = least_clips + (most_clips - least_clips) * rise_rank // (2 * span_inner * span_outer)
    jitter = jax.random.randint(subkeys[0], (groups,), 0, 2, dtype=jnp.int32)
    jitter = jnp.where(device == groups - 1, 0, jitter)
    clip_count = jnp.maximum(clip_count - jitter, 1)
    long_order = jax.random.permutation(subkeys[1], groups - 1)
    long_count = max(1, groups // 16)
    is_long = jnp.any(device[:, None] == long_order[None, :long_count], axis=1)
    long_room = (SHORT * most_clips - LONG) // SHORT
    short_count = jnp.where(is_long, jnp.minimum(clip_count, long_room), clip_count)
    slot_index = jnp.arange(1, most_clips + 1, dtype=jnp.int32)
    first_slot = jnp.where(is_long, LONG, 0).astype(jnp.int32)
    short_slots = jnp.where(slot_index[None, :] <= short_count[:, None], SHORT, 0).astype(jnp.int32)
    return jnp.concatenate([first_slot[:, None], short_slots], axis=1).astype(jnp.int32)


def draw_vector_master(key, part):
    key = jax.random.fold_in(key, 11)
    subkeys = jax.random.split(key, 4)
    biases = jnp.clip(0.5 * jax.random.normal(subkeys[0], (4 * D,), jnp.float32), -2.0, 2.0)
    gain_values = jax.random.uniform(subkeys[1], (2, D), jnp.float32, 0.7, 1.3)
    shifts = jnp.clip(0.3 * jax.random.normal(subkeys[2], (2, D), jnp.float32), -2.0, 2.0)
    up_bias = jnp.clip(0.5 * jax.random.normal(subkeys[3], (FF,), jnp.float32), -2.0, 2.0)
    return jnp.concatenate([biases, gain_values[0], shifts[0], gain_values[1], shifts[1], up_bias]).astype(jnp.float32)


def block_scale(own_key, dims, cuts, smallest, top_value):
    gain = 1.0
    for dim, shards_of in cuts:
        draws = jax.random.uniform(jax.random.fold_in(jax.random.fold_in(own_key, 6), dim), (shards_of,), jnp.float32, smallest / len(cuts), top_value / len(cuts))
        gain = gain * jnp.repeat(jnp.exp(draws), dims[dim] // shards_of).reshape((-1,) + (1,) * (len(dims) - 1 - dim))
    return gain


def normal_values(own_key, shape, spread, bound, cuts=(), kind=jnp.bfloat16):
    values = jax.random.normal(own_key, shape, jnp.float32) * spread
    if len(cuts) > 0:
        values = block_scale(own_key, shape, cuts, -0.22, 0.18) * values
    return jnp.clip(values, min=-bound, max=bound).astype(kind)


def setup_inputs(seed: int = 0) -> dict:
    arg_keys = jax.random.split(jax.random.key(seed), 19)
    return {
        "frames": normal_values(arg_keys[0], (FRAMES, D), 1.0, 6.0, ((0, 32),)),
        "cotangent": normal_values(arg_keys[1], (FRAMES, D), 1.0, 6.0, ((0, 32),)),
        "lengths": draw_lengths(jax.random.fold_in(arg_keys[18], 71), 0),
        "qkv_master": normal_values(arg_keys[3], (3, D, D), D ** -0.5, 0.21875, ((1, 32),), jnp.float32),
        "out_master": normal_values(arg_keys[4], (D, D), 16 ** -0.5, 1.5, ((0, 32),), jnp.float32),
        "up_master": normal_values(arg_keys[5], (D, FF), D ** -0.5, 0.21875, ((0, 32),), jnp.float32),
        "down_master": normal_values(arg_keys[6], (FF, D), FF ** -0.5, 0.109375, ((0, 32),), jnp.float32),
        "vector_master": draw_vector_master(jax.random.fold_in(arg_keys[18], 71), 0),
        "qkv_first": normal_values(arg_keys[8], (3, D, D), (0.111 * 0.8 * (0.6 * FR_DEV * GROUPS) ** 0.5), 80.0, ((1, 32),), jnp.float32),
        "qkv_second": jnp.clip(jnp.exp(math.log(2053.5312) - 2.7725887 * jax.random.uniform(arg_keys[9], (3, D, D), jnp.float32) ** block_scale(arg_keys[9], (3, D, D), ((1, 32),), -0.2, 0.2)), 128.3457, 2053.5312),
        "out_first": normal_values(arg_keys[10], (D, D), (0.111 * 0.15 * (0.6 * FR_DEV * GROUPS) ** 0.5), 14.0, ((0, 32),), jnp.float32),
        "out_second": jnp.clip(jnp.exp(math.log(72.19446) - 2.7725887 * jax.random.uniform(arg_keys[11], (D, D), jnp.float32) ** block_scale(arg_keys[11], (D, D), ((0, 32),), -0.2, 0.2)), 4.5121536, 72.19446),
        "up_first": normal_values(arg_keys[12], (D, FF), (0.111 * 0.6 * (0.6 * FR_DEV * GROUPS) ** 0.5), 56.0, ((0, 32),), jnp.float32),
        "up_second": jnp.clip(jnp.exp(math.log(1155.1113) - 2.7725887 * jax.random.uniform(arg_keys[13], (D, FF), jnp.float32) ** block_scale(arg_keys[13], (D, FF), ((0, 32),), -0.2, 0.2)), 72.19446, 1155.1113),
        "down_first": normal_values(arg_keys[14], (FF, D), (0.111 * 0.6 * (0.6 * FR_DEV * GROUPS) ** 0.5), 56.0, ((0, 32),), jnp.float32),
        "down_second": jnp.clip(jnp.exp(math.log(1155.1113) - 2.7725887 * jax.random.uniform(arg_keys[15], (FF, D), jnp.float32) ** block_scale(arg_keys[15], (FF, D), ((0, 32),), -0.2, 0.2)), 72.19446, 1155.1113),
        "vector_first": normal_values(arg_keys[16], (PV,), (0.111 * (0.6 * FR_DEV * GROUPS) ** 0.5), 96.0, ((0, 32),), jnp.float32),
        "vector_second": jnp.clip(jnp.exp(math.log(3208.6426) - 2.7725887 * jax.random.uniform(arg_keys[17], (PV,), jnp.float32) ** block_scale(arg_keys[17], (PV,), ((0, 32),), -0.2, 0.2)), 200.54016, 3208.6426),
    }


@jax.custom_vjp
def low(v):
    return lax.optimization_barrier(v.astype(jnp.bfloat16)).astype(jnp.float32)

@jax.custom_vjp
def low_back(v):
    return v

def low_keep(v):
    return (low(v), None)

def low_pass(kept, grad):
    return (grad,)

def back_keep(v):
    return (v, None)

def back_low(kept, grad):
    return (low(grad),)
low.defvjp(low_keep, low_pass)
low_back.defvjp(back_keep, back_low)
NEGATIVE = -1e+30
NORM_EPS = 1e-05
SCORE_SCALE = 0.125
BETA_FIRST = 0.9
BETA_SECOND = 0.98
ADAM_EPS = 1e-06
MATRIX_RATE = 0.05
VECTOR_RATE = 0.3
WEIGHT_DECAY = 0.01
HIGHEST_PRECISION = lax.Precision.HIGHEST

def clip_segments(length_row, frame_count):
    clip_ends = jnp.cumsum(length_row).astype(jnp.int32)
    position = jnp.arange(frame_count, dtype=jnp.int32)
    segment = lax.optimization_barrier(jnp.sum((clip_ends[None, :] <= position[:, None]).astype(jnp.int32), axis=1)).astype(jnp.int32)
    valid_rows = (position < clip_ends[-1]).astype(jnp.float32)
    return (segment, valid_rows)

def layer_norm(hidden, norm_gain, norm_bias):
    row_mean = lax.optimization_barrier(jnp.mean(hidden, axis=-1, keepdims=True))
    centred = hidden - row_mean
    variance = lax.optimization_barrier(jnp.mean(centred * centred, axis=-1, keepdims=True))
    return centred * lax.rsqrt(variance + NORM_EPS) * norm_gain + norm_bias

def split_vector(vector, model_width, hidden_width):
    pieces = [vector[piece_index * model_width:(piece_index + 1) * model_width] for piece_index in range(8)]
    return (pieces, vector[8 * model_width:8 * model_width + hidden_width])

def attention(queries, keys_heads, values_heads, segment):
    block_count = FR_DEV // QBLK

    def block_function(inputs):
        query_block, segment_block = inputs
        scores = jnp.einsum('qhd,khd->hqk', query_block, keys_heads, precision=HIGHEST_PRECISION) * SCORE_SCALE
        scores = low_back(scores)
        allowed = segment_block[None, :, None] == segment[None, None, :]
        scores = jnp.where(allowed, scores, NEGATIVE)
        maximum = lax.optimization_barrier(jnp.max(scores, axis=-1, keepdims=True))
        raised = jnp.exp(scores - maximum)
        probabilities = low(raised / lax.optimization_barrier(jnp.sum(raised, axis=-1, keepdims=True)))
        return jnp.einsum('hqk,khd->qhd', probabilities, values_heads, precision=HIGHEST_PRECISION)
    blocks = lax.map(jax.checkpoint(block_function), (queries.reshape(block_count, QBLK, HEADS, HD), segment.reshape(block_count, QBLK)))
    return blocks.reshape(FR_DEV, D)

def layer_forward(block_frames, segment, valid_rows, qkv_value, out_value, up_value, down_value, vector_value):
    qkv_value = low(qkv_value)
    out_value = low(out_value)
    up_value = low(up_value)
    down_value = low(down_value)
    vector_value = low(vector_value)
    pieces, bias_up = split_vector(vector_value, D, FF)
    bias_query, bias_value, bias_out, bias_down, gain_first, shift_first, gain_second, shift_second = pieces
    projected = jnp.einsum('fd,cde->cfe', block_frames, qkv_value, precision=HIGHEST_PRECISION)
    queries = low_back(low(projected[0] + bias_query)).reshape(FR_DEV, HEADS, HD)
    keys_heads = low_back(low(projected[1])).reshape(FR_DEV, HEADS, HD)
    values_heads = low_back(low(projected[2] + bias_value)).reshape(FR_DEV, HEADS, HD)
    context = low_back(low(attention(queries, keys_heads, values_heads, segment)))
    attended = low_back(jnp.dot(context, out_value, precision=HIGHEST_PRECISION) + bias_out)
    first_sum = block_frames + attended
    normed = low(layer_norm(first_sum, gain_first, shift_first))
    up_pre = low_back(jnp.dot(normed, up_value, precision=HIGHEST_PRECISION) + bias_up)
    activated = low(jax.nn.gelu(up_pre, approximate=False))
    down_out = low_back(jnp.dot(activated, down_value, precision=HIGHEST_PRECISION) + bias_down)
    second_sum = normed + down_out
    result = layer_norm(second_sum, gain_second, shift_second)
    valid_column = valid_rows[:, None]
    squares = jnp.stack([jnp.sum(valid_column * attended * attended), jnp.sum(valid_column * first_sum * first_sum), jnp.sum(valid_column * down_out * down_out), jnp.sum(valid_column * second_sum * second_sum)])
    return (result, squares)

def adam_update(master, first, second, gradient, step_rate, decay_rate):
    first_new = BETA_FIRST * first + (1.0 - BETA_FIRST) * gradient
    second_new = BETA_SECOND * second + (1.0 - BETA_SECOND) * gradient * gradient
    first_hat = first_new / (1.0 - BETA_FIRST ** STEP)
    second_hat = second_new / (1.0 - BETA_SECOND ** STEP)
    updated = master - step_rate * (first_hat / (jnp.sqrt(second_hat) + ADAM_EPS) + decay_rate * master)
    return (first_new, second_new, updated, updated.astype(jnp.bfloat16))

def reference(frames, cotangent, lengths, qkv_master, out_master, up_master, down_master, vector_master, qkv_first, qkv_second, out_first, out_second, up_first, up_second, down_first, down_second, vector_first, vector_second):
    frame_blocks = frames.astype(jnp.float32).reshape(GROUPS, FR_DEV, D)
    cotangent_blocks = cotangent.astype(jnp.float32).reshape(GROUPS, FR_DEV, D)
    masters = (qkv_master, out_master, up_master, down_master, vector_master)

    def device_step(running, inputs):
        gradient_totals, square_total = running
        block_frames, cotangent_block, length_row = inputs
        segment, valid_rows = clip_segments(length_row, FR_DEV)

        def closed(frame_value, qkv_value, out_value, up_value, down_value, vector_value):
            return layer_forward(frame_value, segment, valid_rows, qkv_value, out_value, up_value, down_value, vector_value)
        result, pullback, squares = jax.vjp(closed, block_frames, qkv_master, out_master, up_master, down_master, vector_master, has_aux=True)
        gradients = pullback(cotangent_block * valid_rows[:, None])
        gradient_totals = tuple((earlier + gradient for earlier, gradient in zip(gradient_totals, gradients[1:])))
        return ((gradient_totals, square_total + squares), (result.astype(jnp.bfloat16), gradients[0].astype(jnp.bfloat16)))
    start_totals = tuple((jnp.zeros_like(master) for master in masters))
    (gradient_totals, square_total), (results, frame_grads) = lax.scan(device_step, (start_totals, jnp.zeros((4,), jnp.float32)), (frame_blocks, cotangent_blocks, lengths))
    counted = jnp.sum(lengths).astype(jnp.float32) * D
    layer_rms = jnp.sqrt(square_total / counted)
    qkv_new = adam_update(qkv_master, qkv_first, qkv_second, gradient_totals[0], MATRIX_RATE, WEIGHT_DECAY)
    out_new = adam_update(out_master, out_first, out_second, gradient_totals[1], MATRIX_RATE, WEIGHT_DECAY)
    up_new = adam_update(up_master, up_first, up_second, gradient_totals[2], MATRIX_RATE, WEIGHT_DECAY)
    down_new = adam_update(down_master, down_first, down_second, gradient_totals[3], MATRIX_RATE, WEIGHT_DECAY)
    vector_new = adam_update(vector_master, vector_first, vector_second, gradient_totals[4], VECTOR_RATE, 0.0)
    return (results.reshape(FRAMES, D), frame_grads.reshape(FRAMES, D), layer_rms, qkv_new[0], qkv_new[1], qkv_new[2], qkv_new[3], out_new[0], out_new[1], out_new[2], out_new[3], up_new[0], up_new[1], up_new[2], up_new[3], down_new[0], down_new[1], down_new[2], down_new[3], vector_new[0], vector_new[1], vector_new[2], vector_new[3])
```

```python
from functools import partial

import jax
import jax.numpy as jnp
from jax import lax
from jax.experimental import pallas as pl
from jax.experimental.pallas import tpu as pltpu
from jax.sharding import PartitionSpec as P

HEADS = 12
STEP = 10
MOST_VALID = 900

MASKED = 1e30
NORM_EPS = 1e-05
SCORE_SCALE = 0.125
BETA_FIRST = 0.9
BETA_SECOND = 0.98
ADAM_EPS = 1e-06
MATRIX_RATE = 0.05
VECTOR_RATE = 0.3
WEIGHT_DECAY = 0.01
AXES = ("dp", "fsdp")
BF = jnp.bfloat16
F32 = jnp.float32
NT = (((1,), (1,)), ((), ()))
TN = (((0,), (0,)), ((), ()))
VMEM_LIMIT = 60 * 2**20
INV_SQRT2 = 0.7071067811865476
INV_SQRT_2PI = 0.3989422804014327


def struct(shape, dtype):
    return jax.ShapeDtypeStruct(shape, dtype)


def params(**more):
    return pltpu.CompilerParams(vmem_limit_bytes=VMEM_LIMIT, **more)


def cost(flops, bytes_accessed, transcendentals=0):
    return pl.CostEstimate(
        flops=int(flops), bytes_accessed=int(bytes_accessed), transcendentals=int(transcendentals)
    )


class Place:
    def __init__(self, n_dp, n_fsdp):
        self.n_dp = n_dp
        self.n_fsdp = n_fsdp
        self.depth = n_fsdp // 2
        self.count = n_dp * n_fsdp
        dp = lax.axis_index("dp")
        fsdp = lax.axis_index("fsdp")
        self.index = dp * n_fsdp + fsdp
        self.coords = jnp.stack([dp // 2, dp % 2, fsdp // 2, fsdp % 2]).astype(jnp.int32)

    def swap_x(self, value):
        return lax.ppermute(value, "dp", [(i, i ^ 1) for i in range(self.n_dp)])

    def swap_y(self, value):
        return lax.ppermute(value, "dp", [(i, i ^ 2) for i in range(self.n_dp)])

    def swap_core(self, value):
        return lax.ppermute(value, "fsdp", [(i, i ^ 1) for i in range(self.n_fsdp)])

    def shift_z(self, value, step):
        depth = self.depth
        pairs = [(i, ((i // 2 + step) % depth) * 2 + i % 2) for i in range(self.n_fsdp)]
        return lax.ppermute(value, "fsdp", pairs)

    def total(self, value):
        for axis, size in (("fsdp", self.n_fsdp), ("dp", self.n_dp)):
            bit = 1
            while bit < size:
                other = lax.ppermute(value, axis, [(i, i ^ bit) for i in range(size)])
                value = value + other
                bit *= 2
        return value


def gather_blocks(place, block):
    depth = place.depth
    column = [block] + [place.shift_z(block, step) for step in range(1, depth)]
    near = jnp.stack(column[: depth // 2])
    far = jnp.stack(column[depth // 2 :])
    near_x = place.swap_x(near)
    far_y = place.swap_y(far)
    halves = [
        [near, near_x, place.swap_y(near), place.swap_y(near_x)],
        [far, place.swap_x(far), far_y, place.swap_x(far_y)],
    ]
    own = halves[0] + halves[1]
    return own + [place.swap_core(value) for value in own]


def first_add_kernel(coords, *refs):
    (ka, kar, sa, sar, kb, kbr, sb, sbr, keep_a, send_a, keep_b, send_b) = refs
    for left, right, out in (
        (ka, kar, keep_a),
        (sa, sar, send_a),
        (kb, kbr, keep_b),
        (sb, sbr, send_b),
    ):
        out[0] = (left[0, 0].astype(F32) + right[0, 0].astype(F32)).astype(BF)


def first_add(place, mine, received, width):
    depth = place.depth
    half = depth // 2
    rows, columns = mine.shape[1:]
    shape = (2, 2, depth, rows, columns)
    mine = mine.reshape(shape)
    received = received.reshape(shape)
    block = (1, 1, half, rows, width)
    keep_a = pl.BlockSpec(block, lambda i, j, c: (i, c[1], 0, 0, j))
    send_a = pl.BlockSpec(block, lambda i, j, c: (i, 1 - c[1], 0, 0, j))
    keep_b = pl.BlockSpec(block, lambda i, j, c: (c[0], i, 1, 0, j))
    send_b = pl.BlockSpec(block, lambda i, j, c: (1 - c[0], i, 1, 0, j))
    out = pl.BlockSpec((1, half, rows, width), lambda i, j, c: (i, 0, 0, j))
    outs = struct((2, half, rows, columns), BF)
    return pl.pallas_call(
        first_add_kernel,
        grid_spec=pltpu.PrefetchScalarGridSpec(
            num_scalar_prefetch=1,
            grid=(2, columns // width),
            in_specs=[keep_a, keep_a, send_a, send_a, keep_b, keep_b, send_b, send_b],
            out_specs=[out] * 4,
        ),
        out_shape=[outs] * 4,
        compiler_params=params(),
        cost_estimate=cost(mine.size, 6 * mine.size),
        name="reduce_over_core",
    )(place.coords, mine, received, mine, received, mine, received, mine, received)


def second_add_kernel(coords, *refs):
    (ka, kar, sa, sar, kb, kbr, sb, sbr, keep_a, send_a, keep_b, send_b) = refs
    for left, right, out in (
        (ka, kar, keep_a),
        (sa, sar, send_a),
        (kb, kbr, keep_b),
        (sb, sbr, send_b),
    ):
        out[...] = (left[0].astype(F32) + right[0].astype(F32)).astype(BF)


def second_add(place, keep_a, got_a, keep_b, got_b, width):
    half, rows, columns = keep_a.shape[1:]
    block = (1, half, rows, width)
    spec_ka = pl.BlockSpec(block, lambda j, c: (c[0], 0, 0, j))
    spec_sa = pl.BlockSpec(block, lambda j, c: (1 - c[0], 0, 0, j))
    spec_kb = pl.BlockSpec(block, lambda j, c: (c[1], 0, 0, j))
    spec_sb = pl.BlockSpec(block, lambda j, c: (1 - c[1], 0, 0, j))
    out = pl.BlockSpec((half, rows, width), lambda j, c: (0, 0, j))
    outs = struct((half, rows, columns), BF)
    return pl.pallas_call(
        second_add_kernel,
        grid_spec=pltpu.PrefetchScalarGridSpec(
            num_scalar_prefetch=1,
            grid=(columns // width,),
            in_specs=[spec_ka, spec_ka, spec_sa, spec_sa, spec_kb, spec_kb, spec_sb, spec_sb],
            out_specs=[out] * 4,
        ),
        out_shape=[outs] * 4,
        compiler_params=params(),
        cost_estimate=cost(2 * keep_a.size, 12 * keep_a.size),
        name="reduce_over_first_link",
    )(place.coords, keep_a, got_a, keep_a, got_a, keep_b, got_b, keep_b, got_b)


def third_add_kernel(depth, coords, keep_a, got_a, keep_b, got_b, *outs):
    half = depth // 2
    for step in range(depth):
        target = lax.rem(coords[2] + step, depth)
        inner = lax.rem(target, half)
        near = keep_a[inner].astype(F32) + got_a[inner].astype(F32)
        far = keep_b[inner].astype(F32) + got_b[inner].astype(F32)
        outs[step][...] = jnp.where(target < half, near, far).astype(BF)


def third_add(place, keep_a, got_a, keep_b, got_b, width):
    depth = place.depth
    half, rows, columns = keep_a.shape
    spec = pl.BlockSpec((half, rows, width), lambda j, c: (0, 0, j))
    out = pl.BlockSpec((rows, width), lambda j, c: (0, j))
    return pl.pallas_call(
        partial(third_add_kernel, depth),
        grid_spec=pltpu.PrefetchScalarGridSpec(
            num_scalar_prefetch=1,
            grid=(columns // width,),
            in_specs=[spec] * 4,
            out_specs=[out] * depth,
        ),
        out_shape=[struct((rows, columns), BF)] * depth,
        compiler_params=params(),
        cost_estimate=cost(2 * keep_a.size, 12 * keep_a.size),
        name="reduce_over_second_link",
    )(place.coords, keep_a, got_a, keep_b, got_b)


class Reduction:
    def __init__(self, place, mine, theirs, width):
        self.place = place
        self.width = width
        self.mine = mine
        self.got = place.swap_core(theirs)

    def first(self):
        place = self.place
        self.keep_a, send_a, self.keep_b, send_b = first_add(
            place, self.mine, self.got, self.width
        )
        self.got_a = place.swap_x(send_a)
        self.got_b = place.swap_y(send_b)

    def second(self):
        place = self.place
        self.keep_a, send_a, self.keep_b, send_b = second_add(
            place, self.keep_a, self.got_a, self.keep_b, self.got_b, self.width
        )
        self.got_a = place.swap_y(send_a)
        self.got_b = place.swap_x(send_b)

    def third(self):
        place = self.place
        blocks = third_add(
            place, self.keep_a, self.got_a, self.keep_b, self.got_b, self.width
        )
        self.blocks = [blocks[0]] + [
            place.shift_z(blocks[step], step) for step in range(1, place.depth)
        ]

    def result(self):
        total = self.blocks[0].astype(F32)
        for block in self.blocks[1:]:
            total = total + block.astype(F32)
        return total


def pack_kernel(qkv, out, up, down, vector, qkv_low, wire, vector_low):
    rows, width = out.shape
    qkv_low[...] = qkv[...].astype(BF)
    vector_low[...] = vector[...].astype(BF)
    wire[:, 0:width] = down[...].astype(BF)
    pieces = [up[:, j * width : (j + 1) * width] for j in range(4)]
    wire[:, width : 2 * width] = jnp.concatenate(pieces, axis=0).astype(BF)
    pieces = [out[:, j * 256 : (j + 1) * 256] for j in range(3)]
    pieces.append(jnp.zeros((rows, 256), F32))
    wire[:, 2 * width : 2 * width + 256] = jnp.concatenate(pieces, axis=0).astype(BF)


def pack(qkv, out, up, down, vector):
    rows, width = out.shape
    return pl.pallas_call(
        pack_kernel,
        out_shape=(
            struct(qkv.shape, BF),
            struct((4 * rows, 2 * width + 256), BF),
            struct(vector.shape, BF),
        ),
        compiler_params=params(),
        name="round_masters",
    )(qkv, out, up, down, vector)


def qkv_kernel(depth, coords, frames, vector, *refs):
    blocks = refs[:16]
    q_ref, k_ref, v_ref, w_out, raw, weights, sems, out_sem = refs[16:]
    half = depth // 2
    chips = 4 * depth
    rows = raw.shape[2]
    width = raw.shape[3]
    outs = (q_ref, k_ref, v_ref)

    @pl.when(pl.program_id(0) == 0)
    def load():
        copies = []
        for number, block in enumerate(blocks):
            core = number // 8
            far = (number // 4) % 2
            dy = (number // 2) % 2
            dx = number % 2
            y = (coords[0] + dy) % 2
            x = (coords[1] + dx) % 2
            other = (coords[3] + core) % 2
            for j in range(half):
                z = (coords[2] + depth - (far * half + j)) % depth
                device = ((y * 2 + x) * depth + z) * 2 + other
                copies.append(
                    pltpu.make_async_copy(block.at[j], raw.at[device], sems.at[number, j])
                )
        for copy in copies:
            copy.start()
        for copy in copies:
            copy.wait()

        def place_rows(chip, carry):
            for which in range(3):
                pair = jnp.concatenate(
                    [raw[2 * chip, which].astype(F32), raw[2 * chip + 1, which].astype(F32)],
                    axis=0,
                )
                start = pl.multiple_of(chip * 2 * rows, 16)
                weights[which, pl.ds(start, 2 * rows), :] = pair.astype(BF)
            return carry

        lax.fori_loop(0, chips, place_rows, 0)
        pltpu.make_async_copy(weights, w_out, out_sem).start()

    for which in range(3):
        value = jnp.dot(frames[...], weights[which], preferred_element_type=F32)
        if which == 0:
            value = value + vector[0:1, :]
        if which == 2:
            value = value + vector[1:2, :]
        outs[which][...] = value.astype(BF)

    @pl.when(pl.program_id(0) == pl.num_programs(0) - 1)
    def finish():
        pltpu.make_async_copy(weights, w_out, out_sem).wait()


def project_qkv(place, frames, vector, blocks, tile=256):
    count, width = frames.shape
    rows = blocks[0].shape[2]
    low = struct((count, width), BF)
    row_tile = pl.BlockSpec((tile, width), lambda i: (i, 0))
    anywhere = pl.BlockSpec(memory_space=pl.ANY)
    return pl.pallas_call(
        partial(qkv_kernel, place.depth),
        grid=(count // tile,),
        in_specs=[
            pl.BlockSpec(memory_space=pltpu.SMEM),
            row_tile,
            pl.BlockSpec(vector.shape, lambda i: (0, 0)),
        ]
        + [anywhere] * 16,
        out_specs=[row_tile] * 3 + [anywhere],
        out_shape=[low, low, low, struct((3, width, width), BF)],
        scratch_shapes=[
            pltpu.VMEM((place.count, 3, rows, width), BF),
            pltpu.VMEM((3, width, width), BF),
            pltpu.SemaphoreType.DMA((16, place.depth // 2)),
            pltpu.SemaphoreType.DMA,
        ],
        compiler_params=params(),
        cost_estimate=cost(6 * count * width * width, 10 * count * width),
        name="project_qkv",
    )(place.coords, frames, vector, *blocks)


def attention_forward_kernel(q_ref, k_ref, v_ref, q_mark, k_mark, out_ref, log_ref):
    count = q_ref.shape[0]
    values = v_ref[...].T
    lane = lax.broadcasted_iota(jnp.int32, (count, 128), 1)
    outs = []
    for head in (0, 1):
        own = (lane < 64) == (head == 0)
        keys = jnp.where(own, k_ref[...], k_mark[...])
        queries = jnp.where(own, q_ref[...] * BF(SCORE_SCALE), q_mark[...])
        scores = lax.dot_general(keys, queries, NT, preferred_element_type=F32)
        maximum = jnp.max(scores, axis=0, keepdims=True)
        raised = jnp.exp(scores - maximum)
        total = jnp.sum(raised, axis=0, keepdims=True)
        weights = (raised * (1.0 / total)).astype(BF)
        log_ref[0, head : head + 1, :] = maximum + jnp.log(total)
        rows = values[64 * head : 64 * head + 64, :]
        outs.append(jnp.dot(rows, weights, preferred_element_type=F32))
    out_ref[...] = jnp.concatenate(outs, axis=0).T.astype(BF)


def attention_forward(q, k, v, q_mark, k_mark):
    count, width = q.shape
    pairs = width // 128
    column = pl.BlockSpec((count, 128), lambda i: (0, i))
    whole = pl.BlockSpec((count, 128), lambda i: (0, 0))
    return pl.pallas_call(
        attention_forward_kernel,
        grid=(pairs,),
        in_specs=[column] * 3 + [whole] * 2,
        out_specs=(column, pl.BlockSpec((1, 8, count), lambda i: (i, 0, 0))),
        out_shape=(struct((count, width), BF), struct((pairs, 8, count), F32)),
        compiler_params=params(),
        cost_estimate=cost(16 * count * count * width, 8 * count * width, 12 * count * count),
        name="attention_forward",
    )(q, k, v, q_mark, k_mark)


def attention_backward_kernel(
    valid, q_ref, k_ref, v_ref, g_ref, q_mark, k_mark, log_ref,
    dq_ref, dk_ref, dv_ref, sum_ref, p_scr, ds_scr,
):
    count = q_ref.shape[0]
    keys_turned = k_ref[0:valid, :].T
    lane = lax.broadcasted_iota(jnp.int32, (count, 128), 1)
    lane_valid = lax.broadcasted_iota(jnp.int32, (valid, 128), 1)
    turned = []
    dk = jnp.zeros((valid, 128), F32)
    dv = jnp.zeros((valid, 128), F32)
    for head in (0, 1):
        own = (lane < 64) == (head == 0)
        scaled = q_ref[...] * BF(SCORE_SCALE)
        keys = jnp.where((lane_valid < 64) == (head == 0), k_ref[0:valid, :], k_mark[0:valid, :])
        queries = jnp.where(own, scaled, q_mark[...])
        grads = jnp.where(own, g_ref[...], BF(0))
        scores = lax.dot_general(keys, queries, NT, preferred_element_type=F32)
        weights = jnp.exp(scores - log_ref[0, head : head + 1, :])
        slopes = lax.dot_general(v_ref[0:valid, :], grads, NT, preferred_element_type=F32)
        inner = jnp.sum(weights * slopes, axis=0, keepdims=True)
        ds_scr[head] = (weights * (slopes - inner)).astype(BF)
        p_scr[head] = weights.astype(BF)
        turned.append(
            jnp.dot(
                keys_turned[64 * head : 64 * head + 64, :],
                ds_scr[head],
                preferred_element_type=F32,
            )
            * SCORE_SCALE
        )
        dk = dk + jnp.dot(
            ds_scr[head], jnp.where(own, scaled, BF(0)), preferred_element_type=F32
        )
        dv = dv + jnp.dot(p_scr[head], grads, preferred_element_type=F32)
    dq = jnp.concatenate(turned, axis=0).T.astype(BF)
    dq_ref[...] = dq
    dk_ref[0:valid, :] = dk.astype(BF)
    dv = dv.astype(BF)
    dv_ref[0:valid, :] = dv
    if valid < count:
        dk_ref[valid:count, :] = jnp.zeros((count - valid, 128), BF)
        dv_ref[valid:count, :] = jnp.zeros((count - valid, 128), BF)
    sum_ref[0:1, :] = jnp.sum(dq.astype(F32), axis=0, keepdims=True)
    sum_ref[1:2, :] = jnp.sum(dv.astype(F32), axis=0, keepdims=True)
    sum_ref[2:8, :] = jnp.zeros((6, 128), F32)


def attention_backward(q, k, v, grads, q_mark, k_mark, logs, valid):
    count, width = q.shape
    pairs = width // 128
    column = pl.BlockSpec((count, 128), lambda i: (0, i))
    whole = pl.BlockSpec((count, 128), lambda i: (0, 0))
    low = struct((count, width), BF)
    return pl.pallas_call(
        partial(attention_backward_kernel, valid),
        grid=(pairs,),
        in_specs=[column] * 4 + [whole] * 2 + [pl.BlockSpec((1, 8, count), lambda i: (i, 0, 0))],
        out_specs=(column, column, column, pl.BlockSpec((8, 128), lambda i: (0, i))),
        out_shape=(low, low, low, struct((8, width), F32)),
        scratch_shapes=[pltpu.VMEM((2, valid, count), BF)] * 2,
        compiler_params=params(),
        cost_estimate=cost(40 * count * count * width, 14 * count * width, 12 * count * count),
        name="attention_backward",
    )(q, k, v, grads, q_mark, k_mark, logs)


def gelu_parts(value):
    size = jnp.abs(value)
    fall = jnp.exp(value * value * -0.5)
    t = 1.0 / (1.0 + (0.3275911 * INV_SQRT2) * size)
    poly = 0.5 * 1.061405429
    poly = poly * t + 0.5 * -1.453152027
    poly = poly * t + 0.5 * 1.421413741
    poly = poly * t + 0.5 * -0.284496736
    poly = poly * t + 0.5 * 0.254829592
    tail = poly * t * fall
    upper = jnp.where(value >= 0.0, 1.0 - tail, tail)
    return value * upper, upper + value * fall * INV_SQRT_2PI


def normalize(hidden):
    mean = jnp.mean(hidden, axis=-1, keepdims=True)
    centred = hidden - mean
    variance = jnp.mean(centred * centred, axis=-1, keepdims=True)
    inverse = lax.rsqrt(variance + NORM_EPS)
    return centred * inverse, inverse


def norm_backward(grad_output, hat, inverse, gain):
    scaled = grad_output * gain
    return inverse * (
        scaled
        - jnp.mean(scaled, axis=-1, keepdims=True)
        - hat * jnp.mean(scaled * hat, axis=-1, keepdims=True)
    )


def column_sums(value):
    return jnp.sum(value, axis=0, keepdims=True)


def middle_kernel(
    packed, total_ref, frames, context, cotangent, vector, *refs
):
    weight_refs = refs[: 1 if packed else 3]
    (
        result, normed_out, activated_out, down_g_out, up_g_out, first_g_out, attended_g_out,
        context_g_out, sums, up_w, down_w, out_w, raw_up, raw_out, slopes, sems,
    ) = refs[len(weight_refs) :]
    step = pl.program_id(0)
    tile, width = frames.shape
    hidden = up_w.shape[1]
    chunks = hidden // width

    if packed:
        wire = weight_refs[0]
        copies = (
            pltpu.make_async_copy(wire.at[:, 2 * width : 2 * width + 256], raw_out, sems.at[0]),
            pltpu.make_async_copy(wire.at[:, width : 2 * width], raw_up, sems.at[1]),
            pltpu.make_async_copy(wire.at[:, 0:width], down_w, sems.at[2]),
        )
    else:
        copies = (
            pltpu.make_async_copy(weight_refs[0], out_w, sems.at[0]),
            pltpu.make_async_copy(weight_refs[1], up_w, sems.at[1]),
            pltpu.make_async_copy(weight_refs[2], down_w, sems.at[2]),
        )

    def unpack(raw, target, columns, pieces):
        rows = 24

        def pair(chip, carry):
            start = pl.multiple_of(chip * 8 * rows, 16)
            value = raw[pl.ds(start, 8 * rows), :].astype(F32)
            for j in range(pieces):
                both = jnp.concatenate(
                    [
                        value[j * rows : (j + 1) * rows],
                        value[(4 + j) * rows : (5 + j) * rows],
                    ],
                    axis=0,
                )
                to = pl.multiple_of(chip * 2 * rows, 16)
                target[pl.ds(to, 2 * rows), j * columns : (j + 1) * columns] = both.astype(BF)
            return carry

        lax.fori_loop(0, width // (2 * rows), pair, 0)

    @pl.when(step == 0)
    def load():
        for copy in copies:
            copy.start()
        sums[...] = jnp.zeros_like(sums)
        copies[0].wait()
        if packed:
            unpack(raw_out, out_w, 256, 3)
        copies[1].wait()
        if packed:
            unpack(raw_up, up_w, width, 4)
        copies[2].wait()

    def add_sum(row, value):
        sums[row : row + 1, :] += value

    position = step * tile + lax.broadcasted_iota(jnp.int32, (tile, 1), 0)
    valid = (position < total_ref[0]).astype(F32)
    attended = jnp.dot(context[...], out_w[...], preferred_element_type=F32) + vector[2:3, :]
    first_sum = frames[...].astype(F32) + attended
    first_hat, first_inverse = normalize(first_sum)
    normed = (first_hat * vector[4:5, :] + vector[5:6, :]).astype(BF)
    normed_out[...] = normed
    down_out = jnp.broadcast_to(vector[3:4, :], (tile, width))
    for j in range(chunks):
        part = slice(j * width, (j + 1) * width)
        pre = jnp.dot(normed, up_w[:, part], preferred_element_type=F32) + vector[8 + j : 9 + j, :]
        activated, slope = gelu_parts(pre)
        slopes[:, part] = slope
        activated = activated.astype(BF)
        activated_out[:, part] = activated
        down_out = down_out + jnp.dot(activated, down_w[part, :], preferred_element_type=F32)
    second_sum = normed.astype(F32) + down_out
    second_hat, second_inverse = normalize(second_sum)
    result[...] = (second_hat * vector[6:7, :] + vector[7:8, :]).astype(BF)
    add_sum(12, column_sums(valid * attended * attended))
    add_sum(13, column_sums(valid * first_sum * first_sum))
    add_sum(14, column_sums(valid * down_out * down_out))
    add_sum(15, column_sums(valid * second_sum * second_sum))
    add_sum(16, jnp.broadcast_to(column_sums(valid), (1, width)))
    out_g = cotangent[...].astype(F32) * valid
    grad_second = norm_backward(out_g, second_hat, second_inverse, vector[6:7, :])
    add_sum(6, column_sums(out_g * second_hat))
    add_sum(7, column_sums(out_g))
    down_g = grad_second.astype(BF)
    down_g_out[...] = down_g
    add_sum(3, column_sums(down_g.astype(F32)))
    grad_normed = grad_second
    for j in range(chunks):
        part = slice(j * width, (j + 1) * width)
        grad = lax.dot_general(down_g, down_w[part, :], NT, preferred_element_type=F32)
        up_g = (grad * slopes[:, part]).astype(BF)
        up_g_out[:, part] = up_g
        add_sum(8 + j, column_sums(up_g.astype(F32)))
        grad_normed = grad_normed + lax.dot_general(
            up_g, up_w[:, part], NT, preferred_element_type=F32
        )
    grad_first = norm_backward(grad_normed, first_hat, first_inverse, vector[4:5, :])
    add_sum(4, column_sums(grad_normed * first_hat))
    add_sum(5, column_sums(grad_normed))
    first_g_out[...] = grad_first
    attended_g = grad_first.astype(BF)
    attended_g_out[...] = attended_g
    add_sum(2, column_sums(attended_g.astype(F32)))
    context_g_out[...] = lax.dot_general(
        attended_g, out_w[...], NT, preferred_element_type=F32
    ).astype(BF)


def middle(frames, context, cotangent, vector, total, weights, hidden, tile=256):
    count, width = frames.shape
    packed = len(weights) == 1
    row_tile = pl.BlockSpec((tile, width), lambda i: (i, 0))
    wide_tile = pl.BlockSpec((tile, hidden), lambda i: (i, 0))
    anywhere = pl.BlockSpec(memory_space=pl.ANY)
    low = struct((count, width), BF)
    wide = struct((count, hidden), BF)
    raw = hidden if packed else 16
    return pl.pallas_call(
        partial(middle_kernel, packed),
        grid=(count // tile,),
        in_specs=[
            pl.BlockSpec(memory_space=pltpu.SMEM),
            row_tile,
            row_tile,
            row_tile,
            pl.BlockSpec(vector.shape, lambda i: (0, 0)),
        ]
        + [anywhere] * len(weights),
        out_specs=[
            row_tile, row_tile, wide_tile, row_tile, wide_tile, row_tile, row_tile, row_tile,
            pl.BlockSpec((24, width), lambda i: (0, 0)),
        ],
        out_shape=[
            low, low, wide, low, wide, struct((count, width), F32), low, low,
            struct((24, width), F32),
        ],
        scratch_shapes=[
            pltpu.VMEM((width, hidden), BF),
            pltpu.VMEM((hidden, width), BF),
            pltpu.VMEM((width, width), BF),
            pltpu.VMEM((raw, width), BF),
            pltpu.VMEM((raw, 256), BF),
            pltpu.VMEM((tile, hidden), F32),
            pltpu.SemaphoreType.DMA((3,)),
        ],
        compiler_params=params(),
        cost_estimate=cost(
            2 * count * width * (4 * hidden + 2 * width),
            count * (14 * width + 4 * hidden) + 4 * width * hidden,
            2 * count * hidden,
        ),
        name="feed_forward",
    )(total, frames, context, cotangent, vector, *weights)


def down_grad_kernel(valid, rows, coords, left, right, mine, theirs):
    value = lax.dot_general(
        left[0:valid, :], right[0:valid, :], TN, preferred_element_type=F32
    )
    first = coords[3] == 0
    for chip in range(mine.shape[0]):
        start = 2 * chip * rows
        low = value[start : start + rows]
        high = value[start + rows : start + 2 * rows]
        mine[chip] = jnp.where(first, low, high).astype(BF)
        theirs[chip] = jnp.where(first, high, low).astype(BF)


def down_grad(place, left, right, valid, chips=2):
    count, hidden = left.shape
    width = right.shape[1]
    rows = hidden // place.count
    tile = 2 * rows * chips
    out = pl.BlockSpec((chips, rows, width), lambda i, c: (i, 0, 0))
    outs = struct((place.count // 2, rows, width), BF)
    return pl.pallas_call(
        partial(down_grad_kernel, valid, rows),
        grid_spec=pltpu.PrefetchScalarGridSpec(
            num_scalar_prefetch=1,
            grid=(hidden // tile,),
            in_specs=[
                pl.BlockSpec((count, tile), lambda i, c: (0, i)),
                pl.BlockSpec((count, width), lambda i, c: (0, 0)),
            ],
            out_specs=[out, out],
        ),
        out_shape=[outs, outs],
        compiler_params=params(),
        cost_estimate=cost(2 * count * hidden * width, 2 * count * (hidden + width)),
        name="grad_down",
    )(place.coords, left, right)


def row_grad_kernel(valid, rows, sizes, coords, *refs):
    lefts = refs[: len(sizes)]
    rights = refs[len(sizes) : 2 * len(sizes)]
    mine, theirs, total = refs[2 * len(sizes) :]
    first = coords[3] == 0
    start = 0
    for left, right, size in zip(lefts, rights, sizes):

        @pl.when((pl.program_id(0) >= start) & (pl.program_id(0) < start + size))
        def multiply(left=left, right=right):
            total[...] = lax.dot_general(
                left[0:valid, :], right[0:valid, :], TN, preferred_element_type=F32
            )

        start += size
    for chip in range(mine.shape[0]):
        low = total[2 * chip * rows : (2 * chip + 1) * rows, :]
        high = total[(2 * chip + 1) * rows : (2 * chip + 2) * rows, :]
        mine[chip] = jnp.where(first, low, high).astype(BF)
        theirs[chip] = jnp.where(first, high, low).astype(BF)


def row_grad(place, lefts, rights, valid, name):
    count, width = lefts[0].shape
    rows = width // place.count
    sizes = [right.shape[1] // width for right in rights]
    starts = [sum(sizes[:i]) for i in range(len(sizes))]
    whole = pl.BlockSpec((count, width), lambda i, c: (0, 0))

    def column(start, size):
        return pl.BlockSpec(
            (count, width), lambda i, c: (0, jnp.clip(i - start, 0, size - 1))
        )

    steps = sum(sizes)
    out = pl.BlockSpec((place.count // 2, rows, width), lambda i, c: (0, 0, i))
    outs = struct((place.count // 2, rows, steps * width), BF)
    return pl.pallas_call(
        partial(row_grad_kernel, valid, rows, sizes),
        grid_spec=pltpu.PrefetchScalarGridSpec(
            num_scalar_prefetch=1,
            grid=(steps,),
            in_specs=[whole] * len(lefts) + [column(a, s) for a, s in zip(starts, sizes)],
            out_specs=[out, out],
            scratch_shapes=[pltpu.VMEM((width, width), F32)],
        ),
        out_shape=[outs, outs],
        compiler_params=params(),
        cost_estimate=cost(
            2 * count * steps * width * width, 2 * (count + width) * (steps + 1) * width
        ),
        name=name,
    )(place.coords, *lefts, *rights)


def frames_grad_kernel(first_g, q_g, k_g, v_g, weights, out):
    value = first_g[...]
    for which, grad in enumerate((q_g, k_g, v_g)):
        value = value + lax.dot_general(
            grad[...], weights[which], NT, preferred_element_type=F32
        )
    out[...] = value.astype(BF)


def frames_gradient(first_g, q_g, k_g, v_g, weights, tile=256):
    count, width = first_g.shape
    row_tile = pl.BlockSpec((tile, width), lambda i: (i, 0))
    return pl.pallas_call(
        frames_grad_kernel,
        grid=(count // tile,),
        in_specs=[row_tile] * 4 + [pl.BlockSpec(weights.shape, lambda i: (0, 0, 0))],
        out_specs=row_tile,
        out_shape=struct((count, width), BF),
        compiler_params=params(),
        cost_estimate=cost(6 * count * width * width, 12 * count * width + 6 * width * width),
        name="frames_gradient",
    )(first_g, q_g, k_g, v_g, weights)


def adam_update(master, first, second, gradient, step_rate, decay_rate):
    first_new = BETA_FIRST * first + (1.0 - BETA_FIRST) * gradient
    second_new = BETA_SECOND * second + (1.0 - BETA_SECOND) * gradient * gradient
    first_hat = first_new / (1.0 - BETA_FIRST**STEP)
    second_hat = second_new / (1.0 - BETA_SECOND**STEP)
    updated = master - step_rate * (
        first_hat / (jnp.sqrt(second_hat) + ADAM_EPS) + decay_rate * master
    )
    return (first_new, second_new, updated, updated.astype(BF))


def segment_marks(length_row, frame_count):
    clip_ends = jnp.cumsum(length_row)
    position = jnp.arange(frame_count, dtype=jnp.int32)
    segment = jnp.sum((clip_ends[None, :] <= position[:, None]).astype(jnp.int32), axis=1)
    lane = jnp.arange(128, dtype=jnp.int32)[None, :] % 64
    same = lane == segment[:, None]
    q_mark = jnp.where(same, 1.0, 0.0).astype(BF)
    k_mark = jnp.where(same | (lane >= 8), 0.0, -MASKED).astype(BF)
    return q_mark, k_mark, clip_ends[-1:].astype(jnp.int32)


def gather_vector(place, shard):
    blank = jnp.zeros((place.count, shard.shape[0]), BF)
    own = lax.dynamic_update_slice(blank, shard[None, :], (place.index, 0))
    return place.total(own)


def after(values, things):
    return lax.optimization_barrier((values, things))[0]


def shards(n_dp, n_fsdp, *arrays):
    (
        frames, cotangent, lengths, qkv_master, out_master, up_master, down_master, vector_master,
        qkv_first, qkv_second, out_first, out_second, up_first, up_second, down_first,
        down_second, vector_first, vector_second,
    ) = arrays
    place = Place(n_dp, n_fsdp)
    frame_count, width = frames.shape
    hidden = up_master.shape[1]
    rows = out_master.shape[0]
    valid = min(frame_count, -(-MOST_VALID // 16) * 16)
    fast = n_dp == 4 and place.depth % 2 == 0 and rows == 24

    q_mark, k_mark, total = segment_marks(lengths[0], frame_count)
    if fast:
        qkv_low, wire_low, vector_low = pack(
            qkv_master, out_master, up_master, down_master, vector_master[None, :]
        )
        wire = lax.all_gather(wire_low, AXES, axis=0, tiled=True)
        vector = gather_vector(place, vector_low[0]).astype(F32).reshape(-1, width)
        blocks = gather_blocks(place, qkv_low)
        queries, keys, values, qkv_full = project_qkv(place, frames, vector, blocks)
        weights = (wire,)
    else:
        vector = gather_vector(place, vector_master.astype(BF)).astype(F32).reshape(-1, width)
        qkv_full = lax.all_gather(qkv_master.astype(BF), AXES, axis=1, tiled=True)
        projected = jnp.einsum("fd,cde->cfe", frames, qkv_full, preferred_element_type=F32)
        queries = (projected[0] + vector[0]).astype(BF)
        keys = projected[1].astype(BF)
        values = (projected[2] + vector[1]).astype(BF)
        weights = tuple(
            lax.all_gather(w.astype(BF), AXES, axis=0, tiled=True)
            for w in (out_master, up_master, down_master)
        )

    context, logs = attention_forward(queries, keys, values, q_mark, k_mark)
    (
        result, normed, activated, down_g, up_g, first_g, attended_g, context_g, sums,
    ) = middle(frames, context, cotangent, vector, total, weights, hidden)

    if fast:
        mine, theirs = down_grad(place, activated, down_g, valid)
        down_sum = Reduction(place, mine, theirs, width)
        mine, theirs = row_grad(
            place, (normed, context), (up_g, attended_g), valid, "grad_up_and_out"
        )
        up_sum = Reduction(place, mine, theirs, width)
        down_sum.first()
        up_sum.first()

    q_g, k_g, v_g, bias_sums = attention_backward(
        queries, keys, values, context_g, q_mark, k_mark, logs, valid
    )

    if fast:
        mine, theirs = row_grad(
            place, (frames, frames, frames), (q_g, k_g, v_g), valid, "grad_qkv"
        )
        qkv_sum = Reduction(place, mine, theirs, width)
        down_sum.second()
        up_sum.second()
        qkv_sum.first()
        down_sum.third()
        up_sum.third()
        qkv_sum.second()
        qkv_sum.third()
        grad_down = down_sum.result()
        grad_up_out = up_sum.result()
        grad_up = grad_up_out[:, :hidden]
        grad_out = grad_up_out[:, hidden:]
        grad_qkv = qkv_sum.result().reshape(rows, 3, width).transpose(1, 0, 2)
    else:
        def scatter(value, dimension):
            return lax.psum_scatter(value, AXES, scatter_dimension=dimension, tiled=True)

        def product(left, right):
            return lax.dot_general(left, right, TN, preferred_element_type=F32)

        grad_down = scatter(product(activated, down_g), 0)
        grad_up = scatter(product(normed, up_g), 0)
        grad_out = scatter(product(context, attended_g), 0)
        grad_qkv = scatter(jnp.stack([product(frames, g) for g in (q_g, k_g, v_g)]), 1)

    frames_grad = frames_gradient(first_g, q_g, k_g, v_g, qkv_full)
    sums = place.total(sums + jnp.pad(bias_sums, ((0, 16), (0, 0))))
    grad_vector = lax.dynamic_slice(
        sums[0:12].reshape(-1),
        (place.index * vector_master.shape[0],),
        (vector_master.shape[0],),
    )
    layer_rms = jnp.sqrt(jnp.sum(sums[12:16], axis=1) / jnp.sum(sums[16]))

    down_new = adam_update(
        down_master, down_first, down_second, grad_down, MATRIX_RATE, WEIGHT_DECAY
    )
    up_new = adam_update(up_master, up_first, up_second, grad_up, MATRIX_RATE, WEIGHT_DECAY)
    out_new = adam_update(out_master, out_first, out_second, grad_out, MATRIX_RATE, WEIGHT_DECAY)
    qkv_new = adam_update(qkv_master, qkv_first, qkv_second, grad_qkv, MATRIX_RATE, WEIGHT_DECAY)
    vector_new = adam_update(
        vector_master, vector_first, vector_second, grad_vector, VECTOR_RATE, 0.0
    )
    return (
        (result, frames_grad, layer_rms) + qkv_new + out_new + up_new + down_new + vector_new
    )


def solution(mesh):
    rows = P(AXES, None)
    middle_rows = P(None, AXES, None)
    entries = P(AXES)
    return jax.shard_map(
        partial(shards, mesh.shape["dp"], mesh.shape["fsdp"]),
        mesh=mesh,
        in_specs=(
            rows, rows, rows, middle_rows, rows, rows, rows, entries,
            middle_rows, middle_rows, rows, rows, rows, rows, rows, rows, entries, entries,
        ),
        out_specs=(rows, rows, P())
        + (middle_rows,) * 4
        + (rows,) * 12
        + (entries,) * 4,
        check_vma=False,
    )
```

```python
from functools import partial

import jax
import jax.numpy as jnp
from jax import lax
from jax.experimental import pallas as pl
from jax.experimental.pallas import tpu as pltpu
from jax.sharding import PartitionSpec as P

HEADS = 12
STEP = 10
MOST_VALID = 900

MASKED = 1e30
NORM_EPS = 1e-05
SCORE_SCALE = 0.125
BETA_FIRST = 0.9
BETA_SECOND = 0.98
ADAM_EPS = 1e-06
MATRIX_RATE = 0.05
VECTOR_RATE = 0.3
WEIGHT_DECAY = 0.01
AXES = ("dp", "fsdp")
BF = jnp.bfloat16
F32 = jnp.float32
NT = (((1,), (1,)), ((), ()))
TN = (((0,), (0,)), ((), ()))
VMEM_LIMIT = 60 * 2**20
INV_SQRT2 = 0.7071067811865476
INV_SQRT_2PI = 0.3989422804014327
LOG2_E = 1.4426950408889634


def struct(shape, dtype):
    return jax.ShapeDtypeStruct(shape, dtype)


def params(**more):
    return pltpu.CompilerParams(vmem_limit_bytes=VMEM_LIMIT, **more)


def cost(flops, bytes_accessed, transcendentals=0, times=1000):
    return pl.CostEstimate(
        flops=int(flops) * times,
        bytes_accessed=int(bytes_accessed) * times,
        transcendentals=int(transcendentals) * times,
    )


class Place:
    def __init__(self, n_dp, n_fsdp):
        self.n_dp = n_dp
        self.n_fsdp = n_fsdp
        self.depth = n_fsdp // 2
        self.count = n_dp * n_fsdp
        dp = lax.axis_index("dp")
        fsdp = lax.axis_index("fsdp")
        self.index = dp * n_fsdp + fsdp
        self.coords = jnp.stack([dp // 2, dp % 2, fsdp // 2, fsdp % 2, self.index])

    def swap_x(self, value):
        return lax.ppermute(value, "dp", [(i, i ^ 1) for i in range(self.n_dp)])

    def swap_y(self, value):
        return lax.ppermute(value, "dp", [(i, i ^ 2) for i in range(self.n_dp)])

    def swap_core(self, value):
        return lax.ppermute(value, "fsdp", [(i, i ^ 1) for i in range(self.n_fsdp)])

    def shift_z(self, value, step):
        depth = self.depth
        pairs = [(i, ((i // 2 + step) % depth) * 2 + i % 2) for i in range(self.n_fsdp)]
        return lax.ppermute(value, "fsdp", pairs)

    def swap_z(self, value, bit):
        pairs = [(i, i ^ (2 * bit)) for i in range(self.n_fsdp)]
        return lax.ppermute(value, "fsdp", pairs)

    def total(self, value):
        for axis, size in (("fsdp", self.n_fsdp), ("dp", self.n_dp)):
            bit = 1
            while bit < size:
                other = lax.ppermute(value, axis, [(i, i ^ bit) for i in range(size)])
                value = value + other
                bit *= 2
        return value


def gather_blocks(place, block):
    depth = place.depth
    column = [block] + [place.shift_z(block, step) for step in range(1, depth)]
    near = jnp.stack(column[: depth // 2])
    far = jnp.stack(column[depth // 2 :])
    near_x = place.swap_x(near)
    far_y = place.swap_y(far)
    halves = [
        [near, near_x, place.swap_y(near), place.swap_y(near_x)],
        [far, place.swap_x(far), far_y, place.swap_x(far_y)],
    ]
    own = halves[0] + halves[1]
    return own + [place.swap_core(value) for value in own]


def rounded_sum(left, right):
    return (left.astype(F32) + right.astype(F32)).astype(BF)


def first_add_kernel(coords, *refs):
    for number, out in enumerate(refs[8:]):
        out[0] = rounded_sum(refs[2 * number][0, 0], refs[2 * number + 1][0, 0])


def first_add(place, mine, got):
    half = place.depth // 2
    rows, columns = mine.shape[1:]
    shape = (2, 2, place.depth, rows, columns)
    mine = mine.reshape(shape)
    got = got.reshape(shape)
    block = (1, 1, half, rows, columns)
    specs = [
        pl.BlockSpec(block, lambda i, c: (i, c[1], 0, 0, 0)),
        pl.BlockSpec(block, lambda i, c: (i, 1 - c[1], 0, 0, 0)),
        pl.BlockSpec(block, lambda i, c: (c[0], i, 1, 0, 0)),
        pl.BlockSpec(block, lambda i, c: (1 - c[0], i, 1, 0, 0)),
    ]
    out = pl.BlockSpec((1, half, rows, columns), lambda i, c: (i, 0, 0, 0))
    return pl.pallas_call(
        first_add_kernel,
        grid_spec=pltpu.PrefetchScalarGridSpec(
            num_scalar_prefetch=1,
            grid=(2,),
            in_specs=[spec for spec in specs for _ in range(2)],
            out_specs=[out] * 4,
        ),
        out_shape=[struct((2, half, rows, columns), BF)] * 4,
        compiler_params=params(),
        cost_estimate=cost(mine.size, 6 * mine.size),
        name="reduce_over_core",
    )(place.coords, *([mine, got] * 4))


def second_add_kernel(widths, coords, *refs):
    outs = refs[8 * len(widths) :]
    start = 0
    for part, width in enumerate(widths):
        ins = refs[8 * part : 8 * part + 8]
        for number, out in enumerate(outs):
            out[:, :, start : start + width] = rounded_sum(
                ins[2 * number][0], ins[2 * number + 1][0]
            )
        start += width


def second_add(place, parts):
    half, rows = parts[0][0].shape[1:3]
    widths = [part[0].shape[3] for part in parts]
    specs = []
    ins = []
    for (keep_a, got_a, keep_b, got_b), width in zip(parts, widths):
        block = (1, half, rows, width)
        stay_a = pl.BlockSpec(block, lambda i, c: (c[0], 0, 0, 0))
        leave_a = pl.BlockSpec(block, lambda i, c: (1 - c[0], 0, 0, 0))
        stay_b = pl.BlockSpec(block, lambda i, c: (c[1], 0, 0, 0))
        leave_b = pl.BlockSpec(block, lambda i, c: (1 - c[1], 0, 0, 0))
        specs += [stay_a] * 2 + [leave_a] * 2 + [stay_b] * 2 + [leave_b] * 2
        ins += [keep_a, got_a] * 2 + [keep_b, got_b] * 2
    shape = (half, rows, sum(widths))
    return pl.pallas_call(
        partial(second_add_kernel, widths),
        grid_spec=pltpu.PrefetchScalarGridSpec(
            num_scalar_prefetch=1,
            grid=(1,),
            in_specs=specs,
            out_specs=[pl.BlockSpec(shape, lambda i, c: (0, 0, 0))] * 4,
        ),
        out_shape=[struct(shape, BF)] * 4,
        compiler_params=params(),
        cost_estimate=cost(4 * half * rows * shape[2], 24 * half * rows * shape[2]),
        name="reduce_over_first_link",
    )(place.coords, *ins)


def third_add_kernel(coords, keep_a, got_a, keep_b, got_b, keep, send):
    own = lax.rem(coords[2], 2)
    for out, which in ((keep, own), (send, 1 - own)):
        out[0] = rounded_sum(keep_a[which], got_a[which])
        out[1] = rounded_sum(keep_b[which], got_b[which])


def fourth_add_kernel(coords, keep, got, keep_out, send):
    own = lax.div(coords[2], 2)
    keep_out[...] = rounded_sum(keep[own], got[own])
    send[...] = rounded_sum(keep[1 - own], got[1 - own])


def small_add(place, kernel, ins, shape, name):
    inside = pl.BlockSpec(memory_space=pltpu.VMEM)
    return pl.pallas_call(
        kernel,
        in_specs=[pl.BlockSpec(memory_space=pltpu.SMEM)] + [inside] * len(ins),
        out_specs=[inside] * 2,
        out_shape=[struct(shape, BF)] * 2,
        compiler_params=params(),
        cost_estimate=cost(2 * ins[0].size, 6 * ins[0].size),
        name=name,
    )(place.coords, *ins)


class Reduction:
    def __init__(self, place):
        self.place = place
        self.parts = []

    def first(self, mine, got):
        place = self.place
        keep_a, send_a, keep_b, send_b = first_add(place, mine, got)
        self.parts.append((keep_a, place.swap_x(send_a), keep_b, place.swap_y(send_b)))
        return keep_a

    def second(self):
        place = self.place
        keep_a, send_a, keep_b, send_b = second_add(place, self.parts)
        self.sums = (keep_a, place.swap_y(send_a), keep_b, place.swap_x(send_b))
        return keep_a

    def third(self):
        place = self.place
        keep, send = small_add(
            place, third_add_kernel, self.sums, self.sums[0].shape, "reduce_over_second_link"
        )
        self.sums = (keep, place.swap_z(send, 1))
        return keep

    def fourth(self):
        place = self.place
        keep, send = small_add(
            place, fourth_add_kernel, self.sums, self.sums[0].shape[1:], "reduce_over_z"
        )
        self.sums = (keep, place.swap_z(send, 2))
        return keep

    def result(self):
        return self.sums[0].astype(F32) + self.sums[1].astype(F32)


def pack_kernel(coords, qkv, out, up, down, vector, qkv_wire, wire, line):
    rows, width = out.shape
    for which in range(3):
        qkv_wire[:, which * width : (which + 1) * width] = qkv[which].astype(BF)
    line[...] = jnp.zeros_like(line)
    line[0:1, 0 : vector.shape[1]] = vector[...]
    moved = pltpu.roll(line[...], 32 * (coords[4] % 4), 1)
    pieces = [moved[0:1, j * 128 : (j + 1) * 128] for j in range(4)]
    pieces.append(jnp.zeros((rows - 4, 128), F32))
    qkv_wire[:, 3 * width : 3 * width + 128] = jnp.concatenate(pieces, axis=0).astype(BF)
    wire[:, 0:width] = down[...].astype(BF)
    pieces = [up[:, j * width : (j + 1) * width] for j in range(4)]
    wire[:, width : 2 * width] = jnp.concatenate(pieces, axis=0).astype(BF)
    pieces = [out[:, j * 256 : (j + 1) * 256] for j in range(3)]
    pieces.append(jnp.zeros((rows, 256), F32))
    wire[:, 2 * width : 2 * width + 256] = jnp.concatenate(pieces, axis=0).astype(BF)


def pack(place, qkv, out, up, down, vector):
    rows, width = out.shape
    inside = pl.BlockSpec(memory_space=pltpu.VMEM)
    return pl.pallas_call(
        pack_kernel,
        in_specs=[pl.BlockSpec(memory_space=pltpu.SMEM)] + [inside] * 5,
        out_shape=(
            struct((rows, 3 * width + 128), BF),
            struct((4 * rows, 2 * width + 256), BF),
        ),
        scratch_shapes=[pltpu.VMEM((8, 512), F32)],
        compiler_params=params(),
        name="round_masters",
    )(place.coords, qkv, out, up, down, vector)


def qkv_kernel(depth, coords, frames, *refs):
    blocks = refs[:16]
    q_ref, k_ref, v_ref, vector_out, w_out, raw, weights, entries, sems, out_sem = refs[16:]
    half = depth // 2
    chips = 4 * depth
    rows = raw.shape[1]
    width = weights.shape[2]
    outs = (q_ref, k_ref, v_ref)

    @pl.when(pl.program_id(0) == 0)
    def load():
        copies = []
        for number, block in enumerate(blocks):
            core = number // 8
            far = (number // 4) % 2
            dy = (number // 2) % 2
            dx = number % 2
            y = (coords[0] + dy) % 2
            x = (coords[1] + dx) % 2
            other = (coords[3] + core) % 2
            for j in range(half):
                z = (coords[2] + depth - (far * half + j)) % depth
                device = ((y * 2 + x) * depth + z) * 2 + other
                copies.append(
                    pltpu.make_async_copy(block.at[j], raw.at[device], sems.at[number, j])
                )
        for copy in copies:
            copy.start()
        entries[...] = jnp.zeros_like(entries)
        for copy in copies:
            copy.wait()

        def place_rows(chip, carry):
            start = pl.multiple_of(chip * 2 * rows, 16)
            for which in range(3):
                part = slice(which * width, (which + 1) * width)
                pair = jnp.concatenate(
                    [raw[2 * chip, :, part].astype(F32), raw[2 * chip + 1, :, part].astype(F32)],
                    axis=0,
                )
                weights[which, pl.ds(start, 2 * rows), :] = pair.astype(BF)
            return carry

        lax.fori_loop(0, chips, place_rows, 0)
        pltpu.make_async_copy(weights, w_out, out_sem).start()
        for device in range(2 * chips):
            first = 9 * (device // 4) + 2 * (device % 4)
            window = raw[device, :, 3 * width : 3 * width + 128].astype(F32)
            entries[first : first + 4, :] += window[0:4, :]
        vector_out[...] = jnp.zeros_like(vector_out)
        pieces = width // 128
        for row in range(12):
            for j in range(pieces):
                vector_out[row : row + 1, j * 128 : (j + 1) * 128] = entries[
                    row * pieces + j : row * pieces + j + 1, :
                ]

    for which in range(3):
        value = jnp.dot(frames[...], weights[which], preferred_element_type=F32)
        if which == 0:
            value = value + vector_out[0:1, :]
        if which == 2:
            value = value + vector_out[1:2, :]
        outs[which][...] = value.astype(BF)

    @pl.when(pl.program_id(0) == pl.num_programs(0) - 1)
    def finish():
        pltpu.make_async_copy(weights, w_out, out_sem).wait()


def project_qkv(place, frames, blocks, tile=256):
    count, width = frames.shape
    rows, wire_width = blocks[0].shape[1:]
    low = struct((count, width), BF)
    row_tile = pl.BlockSpec((tile, width), lambda i: (i, 0))
    anywhere = pl.BlockSpec(memory_space=pl.ANY)
    return pl.pallas_call(
        partial(qkv_kernel, place.depth),
        grid=(count // tile,),
        in_specs=[pl.BlockSpec(memory_space=pltpu.SMEM), row_tile] + [anywhere] * 16,
        out_specs=[row_tile] * 3 + [pl.BlockSpec((16, width), lambda i: (0, 0)), anywhere],
        out_shape=[low, low, low, struct((16, width), F32), struct((3, width, width), BF)],
        scratch_shapes=[
            pltpu.VMEM((place.count, rows, wire_width), BF),
            pltpu.VMEM((3, width, width), BF),
            pltpu.VMEM((80, 128), F32),
            pltpu.SemaphoreType.DMA((16, place.depth // 2)),
            pltpu.SemaphoreType.DMA,
        ],
        compiler_params=params(),
        cost_estimate=cost(6 * count * width * width, 10 * count * width, times=1),
        name="project_qkv",
    )(place.coords, frames, *blocks)


def attention_forward_kernel(q_ref, k_ref, v_ref, q_mark, k_mark, out_ref, log_ref):
    count = q_ref.shape[0]
    values = v_ref[...].T
    lane = lax.broadcasted_iota(jnp.int32, (count, 128), 1)
    outs = []
    for head in (0, 1):
        own = (lane < 64) == (head == 0)
        keys = jnp.where(own, k_ref[...], k_mark[...])
        queries = jnp.where(own, q_ref[...] * BF(SCORE_SCALE), q_mark[...])
        scores = lax.dot_general(keys, queries, NT, preferred_element_type=F32)
        maximum = jnp.max(scores, axis=0, keepdims=True)
        raised = jnp.exp(scores - maximum)
        total = jnp.sum(raised, axis=0, keepdims=True)
        weights = (raised * (1.0 / total)).astype(BF)
        log_ref[0, head : head + 1, :] = maximum + jnp.log(total)
        rows = values[64 * head : 64 * head + 64, :]
        outs.append(jnp.dot(rows, weights, preferred_element_type=F32))
    out_ref[...] = jnp.concatenate(outs, axis=0).T.astype(BF)


def attention_forward(q, k, v, q_mark, k_mark):
    count, width = q.shape
    pairs = width // 128
    column = pl.BlockSpec((count, 128), lambda i: (0, i))
    whole = pl.BlockSpec((count, 128), lambda i: (0, 0))
    return pl.pallas_call(
        attention_forward_kernel,
        grid=(pairs,),
        in_specs=[column] * 3 + [whole] * 2,
        out_specs=(column, pl.BlockSpec((1, 8, count), lambda i: (i, 0, 0))),
        out_shape=(struct((count, width), BF), struct((pairs, 8, count), F32)),
        compiler_params=params(),
        cost_estimate=cost(
            16 * count * count * width, 8 * count * width, 12 * count * count, times=1
        ),
        name="attention_forward",
    )(q, k, v, q_mark, k_mark)


def attention_backward_kernel(
    valid, q_ref, k_ref, v_ref, g_ref, q_mark, k_mark, log_ref, grads_ref, sum_ref, p_scr, ds_scr
):
    count = q_ref.shape[0]
    keys_turned = k_ref[0:valid, :].T
    lane = lax.broadcasted_iota(jnp.int32, (count, 128), 1)
    lane_valid = lax.broadcasted_iota(jnp.int32, (valid, 128), 1)
    turned = []
    dk = jnp.zeros((valid, 128), F32)
    dv = jnp.zeros((valid, 128), F32)
    for head in (0, 1):
        own = (lane < 64) == (head == 0)
        scaled = q_ref[...] * BF(SCORE_SCALE)
        keys = jnp.where((lane_valid < 64) == (head == 0), k_ref[0:valid, :], k_mark[0:valid, :])
        queries = jnp.where(own, scaled, q_mark[...])
        grads = jnp.where(own, g_ref[...], BF(0))
        scores = lax.dot_general(keys, queries, NT, preferred_element_type=F32)
        weights = jnp.exp(scores - log_ref[0, head : head + 1, :])
        slopes = lax.dot_general(v_ref[0:valid, :], grads, NT, preferred_element_type=F32)
        inner = jnp.sum(weights * slopes, axis=0, keepdims=True)
        ds_scr[head] = (weights * (slopes - inner)).astype(BF)
        p_scr[head] = weights.astype(BF)
        turned.append(
            jnp.dot(
                keys_turned[64 * head : 64 * head + 64, :],
                ds_scr[head],
                preferred_element_type=F32,
            )
            * SCORE_SCALE
        )
        dk = dk + jnp.dot(
            ds_scr[head], jnp.where(own, scaled, BF(0)), preferred_element_type=F32
        )
        dv = dv + jnp.dot(p_scr[head], grads, preferred_element_type=F32)
    dq = jnp.concatenate(turned, axis=0).T.astype(BF)
    grads_ref[0] = dq
    grads_ref[1, 0:valid, :] = dk.astype(BF)
    dv = dv.astype(BF)
    grads_ref[2, 0:valid, :] = dv
    if valid < count:
        grads_ref[1, valid:count, :] = jnp.zeros((count - valid, 128), BF)
        grads_ref[2, valid:count, :] = jnp.zeros((count - valid, 128), BF)
    sum_ref[0:1, :] = jnp.sum(dq.astype(F32), axis=0, keepdims=True)
    sum_ref[1:2, :] = jnp.sum(dv.astype(F32), axis=0, keepdims=True)
    sum_ref[2:8, :] = jnp.zeros((6, 128), F32)


def attention_backward(q, k, v, grads, q_mark, k_mark, logs, valid, first, pairs, earlier=()):
    count, width = q.shape
    column = pl.BlockSpec((count, 128), lambda i: (0, first + i))
    whole = pl.BlockSpec((count, 128), lambda i: (0, 0))

    def kernel(*refs):
        attention_backward_kernel(valid, *refs[:7], *refs[7 + len(earlier) :])

    return pl.pallas_call(
        kernel,
        grid=(pairs,),
        in_specs=[column] * 4
        + [whole] * 2
        + [pl.BlockSpec((1, 8, count), lambda i: (first + i, 0, 0))]
        + [pl.BlockSpec(memory_space=pl.ANY)] * len(earlier),
        out_specs=(
            pl.BlockSpec((3, count, 128), lambda i: (0, 0, first + i)),
            pl.BlockSpec((8, 128), lambda i: (0, first + i)),
        ),
        out_shape=(struct((3, count, width), BF), struct((8, width), F32)),
        scratch_shapes=[pltpu.VMEM((2, valid, count), BF)] * 2,
        input_output_aliases={7 + i: i for i in range(len(earlier))},
        compiler_params=params(),
        cost_estimate=cost(
            40 * count * count * 128 * pairs, 14 * count * 128 * pairs, 2 * count * count * pairs
        ),
        name="attention_backward",
    )(q, k, v, grads, q_mark, k_mark, logs, *earlier)


def gelu_parts(value):
    upper = 0.5 + 0.5 * lax.erf(value * INV_SQRT2)
    fall = jnp.exp2(value * value * (-0.5 * LOG2_E))
    return value * upper, upper + value * fall * INV_SQRT_2PI


def normalize(hidden):
    mean = jnp.mean(hidden, axis=-1, keepdims=True)
    centred = hidden - mean
    variance = jnp.mean(centred * centred, axis=-1, keepdims=True)
    inverse = lax.rsqrt(variance + NORM_EPS)
    return centred * inverse, inverse


def norm_backward(grad_output, hat, inverse, gain):
    scaled = grad_output * gain
    return inverse * (
        scaled
        - jnp.mean(scaled, axis=-1, keepdims=True)
        - hat * jnp.mean(scaled * hat, axis=-1, keepdims=True)
    )


def column_sums(value):
    return jnp.sum(value, axis=0, keepdims=True)


def interleave(*works):
    works = list(works)
    while works:
        for work in list(works):
            try:
                next(work)
            except StopIteration:
                works.remove(work)


def middle_kernel(packed, last_rows, chunk, total_ref, frames, context, cotangent, vector, *refs):
    weight_refs = refs[: 1 if packed else 3]
    (
        result, normed_out, activated_out, down_g_out, up_g_out, first_g_out, attended_g_out,
        context_g_out, sums, up_w, down_w, out_w, raw_up, raw_out, slopes, first_hats,
        second_hats, inverses, sems,
    ) = refs[len(weight_refs) :]
    step = pl.program_id(0)
    tiles = pl.num_programs(0) - 1
    tile, width = frames.shape
    hidden = up_w.shape[1]
    parts = [slice(j * chunk, (j + 1) * chunk) for j in range(hidden // chunk)]

    if packed:
        wire = weight_refs[0]
        copies = (
            pltpu.make_async_copy(wire.at[:, 2 * width : 2 * width + 256], raw_out, sems.at[0]),
            pltpu.make_async_copy(wire.at[:, width : 2 * width], raw_up, sems.at[1]),
            pltpu.make_async_copy(wire.at[:, 0:width], down_w, sems.at[2]),
        )
    else:
        copies = (
            pltpu.make_async_copy(weight_refs[0], out_w, sems.at[0]),
            pltpu.make_async_copy(weight_refs[1], up_w, sems.at[1]),
            pltpu.make_async_copy(weight_refs[2], down_w, sems.at[2]),
        )

    def unpack(raw, target, columns, pieces):
        rows = 24

        def pair(chip, carry):
            start = pl.multiple_of(chip * 8 * rows, 16)
            value = raw[pl.ds(start, 8 * rows), :].astype(F32)
            for j in range(pieces):
                both = jnp.concatenate(
                    [
                        value[j * rows : (j + 1) * rows],
                        value[(4 + j) * rows : (5 + j) * rows],
                    ],
                    axis=0,
                )
                to = pl.multiple_of(chip * 2 * rows, 16)
                target[pl.ds(to, 2 * rows), j * columns : (j + 1) * columns] = both.astype(BF)
            return carry

        lax.fori_loop(0, width // (2 * rows), pair, 0)

    def add_sum(row, value):
        sums[row : row + 1, :] += value

    def valid_rows(number, rows):
        position = number * tile + lax.broadcasted_iota(jnp.int32, (rows, 1), 0)
        return (position < total_ref[0]).astype(F32)

    def forward():
        slot = step % 2
        valid = valid_rows(step, tile)
        attended = jnp.dot(context[...], out_w[...], preferred_element_type=F32)
        yield
        attended = attended + vector[2:3, :]
        first_sum = frames[...].astype(F32) + attended
        first_hat, first_inverse = normalize(first_sum)
        normed = (first_hat * vector[4:5, :] + vector[5:6, :]).astype(BF)
        normed_out[...] = normed
        first_hats[slot] = first_hat
        inverses[slot, 0] = jnp.broadcast_to(first_inverse, (tile, 128))
        add_sum(12, column_sums(valid * attended * attended))
        add_sum(13, column_sums(valid * first_sum * first_sum))
        add_sum(16, jnp.broadcast_to(column_sums(valid), (1, width)))
        yield
        down_out = jnp.broadcast_to(vector[3:4, :], (tile, width))
        pre = jnp.dot(normed, up_w[:, parts[0]], preferred_element_type=F32)
        yield
        for j, part in enumerate(parts):
            if j + 1 < len(parts):
                later = jnp.dot(normed, up_w[:, parts[j + 1]], preferred_element_type=F32)
            row = 8 + part.start // width
            bias = vector[row : row + 1, part.start % width : part.start % width + chunk]
            activated, slope = gelu_parts(pre + bias)
            slopes[slot, :, part] = slope
            activated = activated.astype(BF)
            activated_out[:, part] = activated
            yield
            down_out = down_out + jnp.dot(activated, down_w[part, :], preferred_element_type=F32)
            pre = later
            yield
        second_sum = normed.astype(F32) + down_out
        second_hat, second_inverse = normalize(second_sum)
        result[...] = (second_hat * vector[6:7, :] + vector[7:8, :]).astype(BF)
        second_hats[slot] = second_hat
        inverses[slot, 1] = jnp.broadcast_to(second_inverse, (tile, 128))
        add_sum(14, column_sums(valid * down_out * down_out))
        add_sum(15, column_sums(valid * second_sum * second_sum))

    def backward(rows):
        slot = (step + 1) % 2
        valid = valid_rows(step - 1, rows)
        out_g = cotangent[0:rows, :].astype(F32) * valid
        second_hat = second_hats[slot, 0:rows, :]
        grad_second = norm_backward(
            out_g, second_hat, inverses[slot, 1, 0:rows, 0:1], vector[6:7, :]
        )
        add_sum(6, column_sums(out_g * second_hat))
        add_sum(7, column_sums(out_g))
        down_g = grad_second.astype(BF)
        down_g_out[0:rows, :] = down_g
        add_sum(3, column_sums(down_g.astype(F32)))
        yield
        grad_normed = grad_second
        grad = lax.dot_general(down_g, down_w[parts[0], :], NT, preferred_element_type=F32)
        yield
        for j, part in enumerate(parts):
            if j + 1 < len(parts):
                later = lax.dot_general(
                    down_g, down_w[parts[j + 1], :], NT, preferred_element_type=F32
                )
            up_g = (grad * slopes[slot, 0:rows, part]).astype(BF)
            up_g_out[0:rows, part] = up_g
            row = 8 + part.start // width
            lanes = slice(part.start % width, part.start % width + chunk)
            sums[row : row + 1, lanes] += column_sums(up_g.astype(F32))
            yield
            grad_normed = grad_normed + lax.dot_general(
                up_g, up_w[:, part], NT, preferred_element_type=F32
            )
            grad = later
            yield
        first_hat = first_hats[slot, 0:rows, :]
        grad_first = norm_backward(
            grad_normed, first_hat, inverses[slot, 0, 0:rows, 0:1], vector[4:5, :]
        )
        add_sum(4, column_sums(grad_normed * first_hat))
        add_sum(5, column_sums(grad_normed))
        first_g_out[0:rows, :] = grad_first
        attended_g = grad_first.astype(BF)
        attended_g_out[0:rows, :] = attended_g
        add_sum(2, column_sums(attended_g.astype(F32)))
        yield
        context_g_out[0:rows, :] = lax.dot_general(
            attended_g, out_w[...], NT, preferred_element_type=F32
        ).astype(BF)

    @pl.when(step == 0)
    def first_step():
        for copy in copies:
            copy.start()
        sums[...] = jnp.zeros_like(sums)
        copies[0].wait()
        if packed:
            unpack(raw_out, out_w, 256, 3)
        copies[1].wait()
        if packed:
            unpack(raw_up, up_w, width, 4)
        copies[2].wait()
        interleave(forward())

    @pl.when((step > 0) & (step < tiles))
    def middle_step():
        interleave(forward(), backward(tile))

    @pl.when(step == tiles)
    def last_step():
        interleave(backward(last_rows))
        if last_rows < tile:
            for ref in (down_g_out, up_g_out, first_g_out, attended_g_out, context_g_out):
                ref[last_rows:tile, :] = jnp.zeros((tile - last_rows, ref.shape[1]), ref.dtype)


def middle(frames, context, cotangent, vector, total, weights, hidden, valid, tile=256, chunk=768):
    count, width = frames.shape
    packed = len(weights) == 1
    tiles = count // tile
    last_rows = min(tile, valid - (tiles - 1) * tile)

    def early(columns):
        return pl.BlockSpec((tile, columns), lambda i: (jnp.minimum(i, tiles - 1), 0))

    def late(columns):
        return pl.BlockSpec((tile, columns), lambda i: (jnp.maximum(i - 1, 0), 0))

    anywhere = pl.BlockSpec(memory_space=pl.ANY)
    low = struct((count, width), BF)
    wide = struct((count, hidden), BF)
    raw = hidden if packed else 16
    return pl.pallas_call(
        partial(middle_kernel, packed, last_rows, chunk),
        grid=(tiles + 1,),
        in_specs=[
            pl.BlockSpec(memory_space=pltpu.SMEM),
            early(width),
            early(width),
            late(width),
            pl.BlockSpec(vector.shape, lambda i: (0, 0)),
        ]
        + [anywhere] * len(weights),
        out_specs=[
            early(width), early(width), early(hidden), late(width), late(hidden), late(width),
            late(width), late(width), pl.BlockSpec((24, width), lambda i: (0, 0)),
        ],
        out_shape=[
            low, low, wide, low, wide, struct((count, width), F32), low, low,
            struct((24, width), F32),
        ],
        scratch_shapes=[
            pltpu.VMEM((width, hidden), BF),
            pltpu.VMEM((hidden, width), BF),
            pltpu.VMEM((width, width), BF),
            pltpu.VMEM((raw, width), BF),
            pltpu.VMEM((raw, 256), BF),
            pltpu.VMEM((2, tile, hidden), F32),
            pltpu.VMEM((2, tile, width), F32),
            pltpu.VMEM((2, tile, width), F32),
            pltpu.VMEM((2, 2, tile, 128), F32),
            pltpu.SemaphoreType.DMA((3,)),
        ],
        compiler_params=params(),
        cost_estimate=cost(
            2 * count * width * (4 * hidden + 2 * width),
            count * (14 * width + 4 * hidden) + 4 * width * hidden,
            2 * count * hidden,
        ),
        name="feed_forward",
    )(total, frames, context, cotangent, vector, *weights)


def split_by_core(value, rows, first, mine, theirs):
    for chip in range(value.shape[0] // (2 * rows)):
        low = value[2 * chip * rows : (2 * chip + 1) * rows, :]
        high = value[(2 * chip + 1) * rows : (2 * chip + 2) * rows, :]
        mine[chip] = jnp.where(first, low, high).astype(BF)
        theirs[chip] = jnp.where(first, high, low).astype(BF)


def down_grad_kernel(valid, rows, coords, left, right, mine, theirs):
    value = lax.dot_general(
        left[0:valid, :], right[0:valid, :], TN, preferred_element_type=F32
    )
    first = coords[3] == 0
    width = right.shape[1]
    for chip in range(mine.shape[0]):
        for j in range(4):
            lanes = slice(j * width, (j + 1) * width)
            start = 8 * chip * rows + j * rows
            low = value[start : start + rows, :]
            high = value[start + 4 * rows : start + 5 * rows, :]
            mine[chip, :, lanes] = jnp.where(first, low, high).astype(BF)
            theirs[chip, :, lanes] = jnp.where(first, high, low).astype(BF)


def down_grad(place, left, right, valid, chips=4):
    count, hidden = left.shape
    width = right.shape[1]
    rows = width // place.count
    tile = 8 * rows * chips
    out = pl.BlockSpec((chips, rows, 4 * width), lambda i, c: (i, 0, 0))
    outs = struct((place.count // 2, rows, 4 * width), BF)
    return pl.pallas_call(
        partial(down_grad_kernel, valid, rows),
        grid_spec=pltpu.PrefetchScalarGridSpec(
            num_scalar_prefetch=1,
            grid=(hidden // tile,),
            in_specs=[
                pl.BlockSpec((count, tile), lambda i, c: (0, i)),
                pl.BlockSpec((count, width), lambda i, c: (0, 0)),
            ],
            out_specs=[out, out],
        ),
        out_shape=[outs, outs],
        compiler_params=params(),
        cost_estimate=cost(2 * count * hidden * width, 2 * count * (hidden + width)),
        name="grad_down",
    )(place.coords, left, right)


def up_grad_kernel(
    valid, rows, coords, left, right, out_left, out_right, mine, theirs, lefts, rights, sems
):
    step = pl.program_id(0)
    last = pl.num_programs(0) - 1
    copies = (
        pltpu.make_async_copy(out_left, lefts, sems.at[0]),
        pltpu.make_async_copy(out_right, rights, sems.at[1]),
    )

    @pl.when(step == 0)
    def fetch():
        for copy in copies:
            copy.start()

    @pl.when(step < last)
    def up_part():
        value = lax.dot_general(
            left[0:valid, :], right[0:valid, :], TN, preferred_element_type=F32
        )
        split_by_core(value, rows, coords[3] == 0, mine, theirs)

    @pl.when(step == last)
    def out_part():
        for copy in copies:
            copy.wait()
        value = lax.dot_general(
            lefts[0:valid, :], rights[0:valid, :], TN, preferred_element_type=F32
        )
        split_by_core(value, rows, coords[3] == 0, mine, theirs)


def up_grad(place, left, right, out_left, out_right, valid):
    count, width = left.shape
    rows = width // place.count
    steps = right.shape[1] // width + 1
    anywhere = pl.BlockSpec(memory_space=pl.ANY)
    out = pl.BlockSpec((place.count // 2, rows, width), lambda i, c: (0, 0, i))
    outs = struct((place.count // 2, rows, steps * width), BF)
    return pl.pallas_call(
        partial(up_grad_kernel, valid, rows),
        grid_spec=pltpu.PrefetchScalarGridSpec(
            num_scalar_prefetch=1,
            grid=(steps,),
            in_specs=[
                pl.BlockSpec((count, width), lambda i, c: (0, 0)),
                pl.BlockSpec((count, width), lambda i, c: (0, jnp.minimum(i, steps - 2))),
                anywhere,
                anywhere,
            ],
            out_specs=[out, out],
            scratch_shapes=[
                pltpu.VMEM((count, width), BF),
                pltpu.VMEM((count, width), BF),
                pltpu.SemaphoreType.DMA((2,)),
            ],
        ),
        out_shape=[outs, outs],
        compiler_params=params(),
        cost_estimate=cost(
            2 * count * steps * width * width, 2 * (count + width) * (steps + 1) * width
        ),
        name="grad_up_and_out",
    )(place.coords, left, right, out_left, out_right)


def qkv_grad_kernel(
    valid, rows, coords, left, right, sums, more, mine, theirs, kept, sent, entries, sems
):
    step = pl.program_id(0)
    width = left.shape[1]
    first = coords[3] == 0

    def copies(start, size, number):
        lanes = pl.ds(start, size)
        return (
            pltpu.make_async_copy(kept.at[:, :, lanes], mine.at[:, :, lanes], sems.at[0, number]),
            pltpu.make_async_copy(sent.at[:, :, lanes], theirs.at[:, :, lanes], sems.at[1, number]),
        )

    for which in range(3):

        @pl.when(step == which)
        def part(which=which):
            lanes = slice(which * width, (which + 1) * width)
            value = lax.dot_general(
                left[0:valid, :], right[0, 0:valid, :], TN, preferred_element_type=F32
            )
            split_by_core(value, rows, first, kept.at[:, :, lanes], sent.at[:, :, lanes])
            for copy in copies(which * width, width, which):
                copy.start()

    @pl.when(step == 2)
    def vector_part():
        pieces = width // 128
        entries[...] = jnp.zeros_like(entries)
        for row in range(12):
            value = sums[row : row + 1, :]
            if row < 2:
                value = value + more[row : row + 1, :]
            for j in range(pieces):
                entries[row * pieces + j : row * pieces + j + 1, :] = value[
                    :, j * 128 : (j + 1) * 128
                ]
        blank = jnp.zeros((rows - 4, 128), F32)
        lanes = slice(3 * width, 3 * width + 128)
        for chip in range(kept.shape[0]):
            windows = []
            for device in (2 * chip, 2 * chip + 1):
                start = 9 * (device // 4) + 2 * (device % 4)
                windows.append(jnp.concatenate([entries[start : start + 4, :], blank], axis=0))
            kept[chip, :, lanes] = jnp.where(first, windows[0], windows[1]).astype(BF)
            sent[chip, :, lanes] = jnp.where(first, windows[1], windows[0]).astype(BF)
        for copy in copies(3 * width, 128, 3):
            copy.start()
        for which in range(3):
            for copy in copies(which * width, width, which):
                copy.wait()
        for copy in copies(3 * width, 128, 3):
            copy.wait()


def qkv_grad(place, left, right, sums, more, valid):
    count, width = left.shape
    rows = width // place.count
    wire = (place.count // 2, rows, 3 * width + 128)
    anywhere = pl.BlockSpec(memory_space=pl.ANY)
    return pl.pallas_call(
        partial(qkv_grad_kernel, valid, rows),
        grid_spec=pltpu.PrefetchScalarGridSpec(
            num_scalar_prefetch=1,
            grid=(3,),
            in_specs=[
                pl.BlockSpec((count, width), lambda i, c: (0, 0)),
                pl.BlockSpec((1, count, width), lambda i, c: (i, 0, 0)),
                pl.BlockSpec(sums.shape, lambda i, c: (0, 0)),
                pl.BlockSpec(more.shape, lambda i, c: (0, 0)),
            ],
            out_specs=[anywhere, anywhere],
            scratch_shapes=[
                pltpu.VMEM(wire, BF),
                pltpu.VMEM(wire, BF),
                pltpu.VMEM((80, 128), F32),
                pltpu.SemaphoreType.DMA((2, 4)),
            ],
        ),
        out_shape=[struct(wire, BF)] * 2,
        compiler_params=params(),
        cost_estimate=cost(6 * count * width * width, 8 * (count + width) * width),
        name="grad_qkv",
    )(place.coords, left, right, sums, more)


def frames_grad_kernel(first_g, grads, weights, out):
    value = first_g[...]
    for which in range(3):
        value = value + lax.dot_general(
            grads[which], weights[which], NT, preferred_element_type=F32
        )
    out[...] = value.astype(BF)


def frames_gradient(first_g, grads, weights, tile=256):
    count, width = first_g.shape
    row_tile = pl.BlockSpec((tile, width), lambda i: (i, 0))
    return pl.pallas_call(
        frames_grad_kernel,
        grid=(count // tile,),
        in_specs=[
            row_tile,
            pl.BlockSpec((3, tile, width), lambda i: (0, i, 0)),
            pl.BlockSpec(weights.shape, lambda i: (0, 0, 0)),
        ],
        out_specs=row_tile,
        out_shape=struct((count, width), BF),
        compiler_params=params(),
        cost_estimate=cost(6 * count * width * width, 12 * count * width + 6 * width * width),
        name="frames_gradient",
    )(first_g, grads, weights)


def adam_update(master, first, second, gradient, step_rate, decay_rate):
    first_new = BETA_FIRST * first + (1.0 - BETA_FIRST) * gradient
    second_new = BETA_SECOND * second + (1.0 - BETA_SECOND) * gradient * gradient
    first_hat = first_new / (1.0 - BETA_FIRST**STEP)
    second_hat = second_new / (1.0 - BETA_SECOND**STEP)
    updated = master - step_rate * (
        first_hat / (jnp.sqrt(second_hat) + ADAM_EPS) + decay_rate * master
    )
    return (first_new, second_new, updated, updated.astype(BF))


def segment_marks(length_row, frame_count):
    clip_ends = jnp.cumsum(length_row)
    position = jnp.arange(frame_count, dtype=jnp.int32)
    segment = jnp.sum((clip_ends[None, :] <= position[:, None]).astype(jnp.int32), axis=1)
    lane = jnp.arange(128, dtype=jnp.int32)[None, :] % 64
    same = lane == segment[:, None]
    q_mark = jnp.where(same, 1.0, 0.0).astype(BF)
    k_mark = jnp.where(same | (lane >= 8), 0.0, -MASKED).astype(BF)
    return q_mark, k_mark, clip_ends[-1:].astype(jnp.int32)


def gather_vector(place, shard):
    blank = jnp.zeros((place.count, shard.shape[0]), BF)
    own = lax.dynamic_update_slice(blank, shard[None, :], (place.index, 0))
    return place.total(own)


def after(values, things):
    return lax.optimization_barrier((values, things))[0]


def shards(n_dp, n_fsdp, *arrays):
    (
        frames, cotangent, lengths, qkv_master, out_master, up_master, down_master, vector_master,
        qkv_first, qkv_second, out_first, out_second, up_first, up_second, down_first,
        down_second, vector_first, vector_second,
    ) = arrays
    place = Place(n_dp, n_fsdp)
    frame_count, width = frames.shape
    hidden = up_master.shape[1]
    rows = out_master.shape[0]
    valid = min(frame_count, -(-MOST_VALID // 16) * 16)
    fast = n_dp == 4 and place.depth == 4 and rows == 24

    q_mark, k_mark, total = segment_marks(lengths[0], frame_count)
    if fast:
        qkv_wire, wire_low = pack(
            place, qkv_master, out_master, up_master, down_master, vector_master[None, :]
        )
        wire = lax.all_gather(wire_low, AXES, axis=0, tiled=True)
        blocks = gather_blocks(place, qkv_wire)
        queries, keys, values, vector, qkv_full = project_qkv(place, frames, blocks)
        weights = (wire,)
    else:
        vector = gather_vector(place, vector_master.astype(BF)).astype(F32).reshape(-1, width)
        qkv_full = lax.all_gather(qkv_master.astype(BF), AXES, axis=1, tiled=True)
        projected = jnp.einsum("fd,cde->cfe", frames, qkv_full, preferred_element_type=F32)
        queries = (projected[0] + vector[0]).astype(BF)
        keys = projected[1].astype(BF)
        values = (projected[2] + vector[1]).astype(BF)
        weights = tuple(
            lax.all_gather(w.astype(BF), AXES, axis=0, tiled=True)
            for w in (out_master, up_master, down_master)
        )

    context, logs = attention_forward(queries, keys, values, q_mark, k_mark)
    (
        result, normed, activated, down_g, up_g, first_g, attended_g, context_g, sums,
    ) = middle(frames, context, cotangent, vector, total, weights, hidden, valid)

    def attention_part(first, pairs, start, earlier=()):
        return attention_backward(
            start, keys, values, context_g, q_mark, k_mark, logs, valid, first, pairs, earlier
        )

    if fast:
        down_mine, theirs = down_grad(place, activated, down_g, valid)
        down_got = place.swap_core(theirs)
        up_mine, theirs = up_grad(
            place, after(normed, down_mine), up_g, context, attended_g, valid
        )
        up_got = place.swap_core(theirs)
        all_sums = lax.all_gather(sums, AXES, axis=0)
        most = Reduction(place)
        done = most.first(after(down_mine, up_mine), down_got)
        grads = attention_part(0, 2, after(queries, done))
        done = most.first(after(up_mine, grads[1]), up_got)
        grads = attention_part(2, 2, after(queries, done), grads)
        most.parts[0] = after(most.parts[0], grads[1])
        done = most.second()
        qkv_g, bias_sums = attention_part(4, 2, after(queries, done), grads)
        most.sums = after(most.sums, bias_sums)
        done = most.third()
        mine, theirs = qkv_grad(place, after(frames, done), qkv_g, sums, bias_sums, valid)
        got = place.swap_core(theirs)
        frames_grad = frames_gradient(after(first_g, mine), qkv_g, qkv_full)
        most.sums = after(most.sums, frames_grad)
        done = most.fourth()
        last = Reduction(place)
        last.first(after(mine, done), got)
        done = last.second()
        most.sums = after(most.sums, done)
        last.third()
        last.fourth()
        grad_most = most.result()
        grad_qkv = last.result()
        grad_down = grad_most[:, : 4 * width].reshape(rows, 4, width)
        grad_down = grad_down.transpose(1, 0, 2).reshape(4 * rows, width)
        grad_up = grad_most[:, 4 * width : 8 * width]
        grad_out = grad_most[:, 8 * width :]
        window = grad_qkv[0:4, 3 * width :].reshape(-1)
        grad_vector = lax.dynamic_slice(
            window, (32 * (place.index % 4),), (vector_master.shape[0],)
        )
        grad_qkv = grad_qkv[:, : 3 * width].reshape(rows, 3, width).transpose(1, 0, 2)
        squares = jnp.sum(all_sums[:, 12:17], axis=(0, 2))
        layer_rms = jnp.sqrt(squares[0:4] / squares[4])
    else:
        def scatter(value, dimension):
            return lax.psum_scatter(value, AXES, scatter_dimension=dimension, tiled=True)

        def product(left, right):
            return lax.dot_general(left, right, TN, preferred_element_type=F32)

        qkv_g, bias_sums = attention_part(0, HEADS // 2, queries)
        grad_down = scatter(product(activated, down_g), 0)
        grad_up = scatter(product(normed, up_g), 0)
        grad_out = scatter(product(context, attended_g), 0)
        grad_qkv = scatter(jnp.stack([product(frames, qkv_g[i]) for i in range(3)]), 1)
        frames_grad = frames_gradient(first_g, qkv_g, qkv_full)
        sums = place.total(sums + jnp.pad(bias_sums, ((0, 16), (0, 0))))
        grad_vector = lax.dynamic_slice(
            sums[0:12].reshape(-1),
            (place.index * vector_master.shape[0],),
            (vector_master.shape[0],),
        )
        layer_rms = jnp.sqrt(jnp.sum(sums[12:16], axis=1) / jnp.sum(sums[16]))

    down_new = adam_update(
        down_master, down_first, down_second, grad_down, MATRIX_RATE, WEIGHT_DECAY
    )
    up_new = adam_update(up_master, up_first, up_second, grad_up, MATRIX_RATE, WEIGHT_DECAY)
    out_new = adam_update(out_master, out_first, out_second, grad_out, MATRIX_RATE, WEIGHT_DECAY)
    qkv_new = adam_update(qkv_master, qkv_first, qkv_second, grad_qkv, MATRIX_RATE, WEIGHT_DECAY)
    vector_new = adam_update(
        vector_master, vector_first, vector_second, grad_vector, VECTOR_RATE, 0.0
    )
    return (
        (result, frames_grad, layer_rms) + qkv_new + out_new + up_new + down_new + vector_new
    )


def solution(mesh):
    rows = P(AXES, None)
    middle_rows = P(None, AXES, None)
    entries = P(AXES)
    return jax.shard_map(
        partial(shards, mesh.shape["dp"], mesh.shape["fsdp"]),
        mesh=mesh,
        in_specs=(
            rows, rows, rows, middle_rows, rows, rows, rows, entries,
            middle_rows, middle_rows, rows, rows, rows, rows, rows, rows, entries, entries,
        ),
        out_specs=(rows, rows, P())
        + (middle_rows,) * 4
        + (rows,) * 12
        + (entries,) * 4,
        check_vma=False,
    )
```

```python
from functools import partial

import jax
import jax.numpy as jnp
from jax import lax
from jax.experimental import pallas as pl
from jax.experimental.pallas import tpu as pltpu
from jax.sharding import PartitionSpec as P

HEADS = 12
STEP = 10
LONG = 780
SHORT = 150
MOST_VALID = 900

MASKED = 1e30
NORM_EPS = 1e-05
SCORE_SCALE = 0.125
BETA_FIRST = 0.9
BETA_SECOND = 0.98
ADAM_EPS = 1e-06
MATRIX_RATE = 0.05
VECTOR_RATE = 0.3
WEIGHT_DECAY = 0.01
AXES = ("dp", "fsdp")
BF = jnp.bfloat16
F32 = jnp.float32
NT = (((1,), (1,)), ((), ()))
TN = (((0,), (0,)), ((), ()))
VMEM_LIMIT = 60 * 2**20
INV_SQRT2 = 0.7071067811865476
INV_SQRT_2PI = 0.3989422804014327
LOG2_E = 1.4426950408889634


def struct(shape, dtype):
    return jax.ShapeDtypeStruct(shape, dtype)


def params(**more):
    return pltpu.CompilerParams(vmem_limit_bytes=VMEM_LIMIT, **more)


def cost(flops, bytes_accessed, transcendentals=0, times=1000):
    return pl.CostEstimate(
        flops=int(flops) * times,
        bytes_accessed=int(bytes_accessed) * times,
        transcendentals=int(transcendentals) * times,
    )


class Place:
    def __init__(self, n_dp, n_fsdp):
        self.n_dp = n_dp
        self.n_fsdp = n_fsdp
        self.depth = n_fsdp // 2
        self.count = n_dp * n_fsdp
        dp = lax.axis_index("dp")
        fsdp = lax.axis_index("fsdp")
        self.index = dp * n_fsdp + fsdp
        self.coords = jnp.stack([dp // 2, dp % 2, fsdp // 2, fsdp % 2, self.index])

    def swap_x(self, value):
        return lax.ppermute(value, "dp", [(i, i ^ 1) for i in range(self.n_dp)])

    def swap_y(self, value):
        return lax.ppermute(value, "dp", [(i, i ^ 2) for i in range(self.n_dp)])

    def swap_core(self, value):
        return lax.ppermute(value, "fsdp", [(i, i ^ 1) for i in range(self.n_fsdp)])

    def shift_z(self, value, step):
        depth = self.depth
        pairs = [(i, ((i // 2 + step) % depth) * 2 + i % 2) for i in range(self.n_fsdp)]
        return lax.ppermute(value, "fsdp", pairs)

    def swap_z(self, value, bit):
        pairs = [(i, i ^ (2 * bit)) for i in range(self.n_fsdp)]
        return lax.ppermute(value, "fsdp", pairs)

    def total(self, value):
        for axis, size in (("fsdp", self.n_fsdp), ("dp", self.n_dp)):
            bit = 1
            while bit < size:
                other = lax.ppermute(value, axis, [(i, i ^ bit) for i in range(size)])
                value = value + other
                bit *= 2
        return value


def gather_blocks(place, block):
    depth = place.depth
    column = [block] + [place.shift_z(block, step) for step in range(1, depth)]
    near = jnp.stack(column[: depth // 2])
    far = jnp.stack(column[depth // 2 :])
    near_x = place.swap_x(near)
    far_y = place.swap_y(far)
    halves = [
        [near, near_x, place.swap_y(near), place.swap_y(near_x)],
        [far, place.swap_x(far), far_y, place.swap_x(far_y)],
    ]
    own = halves[0] + halves[1]
    return own + [place.swap_core(value) for value in own]


def rounded_sum(left, right):
    return (left.astype(F32) + right.astype(F32)).astype(BF)


def first_add_kernel(coords, *refs):
    for number, out in enumerate(refs[8:]):
        out[0] = rounded_sum(refs[2 * number][0, 0], refs[2 * number + 1][0, 0])


def first_add(place, mine, got):
    half = place.depth // 2
    rows, columns = mine.shape[1:]
    shape = (2, 2, place.depth, rows, columns)
    mine = mine.reshape(shape)
    got = got.reshape(shape)
    block = (1, 1, half, rows, columns)
    specs = [
        pl.BlockSpec(block, lambda i, c: (i, c[1], 0, 0, 0)),
        pl.BlockSpec(block, lambda i, c: (i, 1 - c[1], 0, 0, 0)),
        pl.BlockSpec(block, lambda i, c: (c[0], i, 1, 0, 0)),
        pl.BlockSpec(block, lambda i, c: (1 - c[0], i, 1, 0, 0)),
    ]
    out = pl.BlockSpec((1, half, rows, columns), lambda i, c: (i, 0, 0, 0))
    return pl.pallas_call(
        first_add_kernel,
        grid_spec=pltpu.PrefetchScalarGridSpec(
            num_scalar_prefetch=1,
            grid=(2,),
            in_specs=[spec for spec in specs for _ in range(2)],
            out_specs=[out] * 4,
        ),
        out_shape=[struct((2, half, rows, columns), BF)] * 4,
        compiler_params=params(),
        cost_estimate=cost(mine.size, 6 * mine.size, times=10**6),
        name="reduce_over_core",
    )(place.coords, *([mine, got] * 4))


def second_add_kernel(widths, coords, *refs):
    outs = refs[8 * len(widths) :]
    start = 0
    for part, width in enumerate(widths):
        ins = refs[8 * part : 8 * part + 8]
        for number, out in enumerate(outs):
            out[:, :, start : start + width] = rounded_sum(
                ins[2 * number][0], ins[2 * number + 1][0]
            )
        start += width


def second_add(place, parts):
    half, rows = parts[0][0].shape[1:3]
    widths = [part[0].shape[3] for part in parts]
    specs = []
    ins = []
    for (keep_a, got_a, keep_b, got_b), width in zip(parts, widths):
        block = (1, half, rows, width)
        stay_a = pl.BlockSpec(block, lambda i, c: (c[0], 0, 0, 0))
        leave_a = pl.BlockSpec(block, lambda i, c: (1 - c[0], 0, 0, 0))
        stay_b = pl.BlockSpec(block, lambda i, c: (c[1], 0, 0, 0))
        leave_b = pl.BlockSpec(block, lambda i, c: (1 - c[1], 0, 0, 0))
        specs += [stay_a] * 2 + [leave_a] * 2 + [stay_b] * 2 + [leave_b] * 2
        ins += [keep_a, got_a] * 2 + [keep_b, got_b] * 2
    shape = (half, rows, sum(widths))
    return pl.pallas_call(
        partial(second_add_kernel, widths),
        grid_spec=pltpu.PrefetchScalarGridSpec(
            num_scalar_prefetch=1,
            grid=(1,),
            in_specs=specs,
            out_specs=[pl.BlockSpec(shape, lambda i, c: (0, 0, 0))] * 4,
        ),
        out_shape=[struct(shape, BF)] * 4,
        compiler_params=params(),
        cost_estimate=cost(
            4 * half * rows * shape[2], 24 * half * rows * shape[2], times=10**6
        ),
        name="reduce_over_first_link",
    )(place.coords, *ins)


def third_add_kernel(coords, keep_a, got_a, keep_b, got_b, keep, send):
    own = lax.rem(coords[2], 2)
    for out, which in ((keep, own), (send, 1 - own)):
        out[0] = rounded_sum(keep_a[which], got_a[which])
        out[1] = rounded_sum(keep_b[which], got_b[which])


def spread_add_kernel(coords, keep_a, got_a, keep_b, got_b, *outs):
    half = keep_a.shape[0]
    for step, out in enumerate(outs):
        target = lax.rem(coords[2] + step, 2 * half)
        inner = lax.rem(target, half)
        near = keep_a[inner].astype(F32) + got_a[inner].astype(F32)
        far = keep_b[inner].astype(F32) + got_b[inner].astype(F32)
        out[...] = jnp.where(target < half, near, far).astype(BF)


def fourth_add_kernel(coords, keep, got, keep_out, send):
    own = lax.div(coords[2], 2)
    keep_out[...] = rounded_sum(keep[own], got[own])
    send[...] = rounded_sum(keep[1 - own], got[1 - own])


def small_add(place, kernel, ins, shape, name, times=10**6, outs=2):
    inside = pl.BlockSpec(memory_space=pltpu.VMEM)
    return pl.pallas_call(
        kernel,
        in_specs=[pl.BlockSpec(memory_space=pltpu.SMEM)] + [inside] * len(ins),
        out_specs=[inside] * outs,
        out_shape=[struct(shape, BF)] * outs,
        compiler_params=params(),
        cost_estimate=cost(2 * ins[0].size, 6 * ins[0].size, times=times),
        name=name,
    )(place.coords, *ins)


class Reduction:
    def __init__(self, place):
        self.place = place
        self.parts = []

    def first(self, mine, got):
        place = self.place
        keep_a, send_a, keep_b, send_b = first_add(place, mine, got)
        self.parts.append((keep_a, place.swap_x(send_a), keep_b, place.swap_y(send_b)))
        return keep_a

    def second(self):
        place = self.place
        keep_a, send_a, keep_b, send_b = second_add(place, self.parts)
        self.sums = (keep_a, place.swap_y(send_a), keep_b, place.swap_x(send_b))
        return keep_a

    def third(self, times=10**6):
        place = self.place
        keep, send = small_add(
            place, third_add_kernel, self.sums, self.sums[0].shape, "reduce_over_second_link", times
        )
        self.sums = (keep, place.swap_z(send, 1))
        return keep

    def fourth(self, times=10**6):
        place = self.place
        keep, send = small_add(
            place, fourth_add_kernel, self.sums, self.sums[0].shape[1:], "reduce_over_z", times
        )
        self.sums = (keep, place.swap_z(send, 2))
        return keep

    def spread(self):
        place = self.place
        blocks = small_add(
            place, spread_add_kernel, self.sums, self.sums[0].shape[1:],
            "reduce_over_second_link", outs=place.depth,
        )
        self.sums = (blocks[0],) + tuple(
            place.shift_z(blocks[step], step) for step in range(1, place.depth)
        )
        return blocks[0]

    def result(self):
        total = self.sums[0].astype(F32)
        for part in self.sums[1:]:
            total = total + part.astype(F32)
        return total


def pack_kernel(coords, qkv, out, up, down, vector, qkv_wire, wire, line):
    rows, width = out.shape
    for which in range(3):
        qkv_wire[:, which * width : (which + 1) * width] = qkv[which].astype(BF)
    line[...] = jnp.zeros_like(line)
    line[0:1, 0 : vector.shape[1]] = vector[...]
    moved = pltpu.roll(line[...], 32 * (coords[4] % 4), 1)
    pieces = [moved[0:1, j * 128 : (j + 1) * 128] for j in range(4)]
    pieces.append(jnp.zeros((rows - 4, 128), F32))
    qkv_wire[:, 3 * width : 3 * width + 128] = jnp.concatenate(pieces, axis=0).astype(BF)
    wire[:, 0:width] = down[...].astype(BF)
    pieces = [up[:, j * width : (j + 1) * width] for j in range(4)]
    wire[:, width : 2 * width] = jnp.concatenate(pieces, axis=0).astype(BF)
    pieces = [out[:, j * 256 : (j + 1) * 256] for j in range(3)]
    pieces.append(jnp.zeros((rows, 256), F32))
    wire[:, 2 * width : 2 * width + 256] = jnp.concatenate(pieces, axis=0).astype(BF)


def pack(place, qkv, out, up, down, vector):
    rows, width = out.shape
    inside = pl.BlockSpec(memory_space=pltpu.VMEM)
    return pl.pallas_call(
        pack_kernel,
        in_specs=[pl.BlockSpec(memory_space=pltpu.SMEM)] + [inside] * 5,
        out_shape=(
            struct((rows, 3 * width + 128), BF),
            struct((4 * rows, 2 * width + 256), BF),
        ),
        scratch_shapes=[pltpu.VMEM((8, 512), F32)],
        compiler_params=params(),
        name="round_masters",
    )(place.coords, qkv, out, up, down, vector)


def qkv_kernel(depth, coords, frames, *refs):
    blocks = refs[:16]
    q_ref, k_ref, v_ref, vector_out, w_out, weights, windows, entries, sem = refs[16:]
    half = depth // 2
    rows = blocks[0].shape[1]
    width = weights.shape[2]
    outs = (q_ref, k_ref, v_ref)
    copy = pltpu.make_async_copy(weights, w_out, sem)

    @pl.when(pl.program_id(0) == 0)
    def assemble():
        first_core = coords[3] == 0
        for number in range(8):
            far = number // 4
            y = (coords[0] + (number // 2) % 2) % 2
            x = (coords[1] + number % 2) % 2
            for j in range(half):
                z = (coords[2] + depth - (far * half + j)) % depth
                chip = (y * 2 + x) * depth + z
                start = pl.multiple_of(chip * 2 * rows, 16)
                for which in range(3):
                    part = slice(which * width, (which + 1) * width)
                    own = blocks[number][j, :, part].astype(F32)
                    other = blocks[number + 8][j, :, part].astype(F32)
                    low = jnp.where(first_core, own, other)
                    high = jnp.where(first_core, other, own)
                    weights[which, pl.ds(start, 2 * rows), :] = jnp.concatenate(
                        [low, high], axis=0
                    ).astype(BF)
                part = slice(3 * width, 3 * width + 128)
                windows[chip * 2 + coords[3]] = blocks[number][j, :, part].astype(F32)[0:8]
                windows[chip * 2 + 1 - coords[3]] = blocks[number + 8][j, :, part].astype(F32)[0:8]
        copy.start()
        entries[...] = jnp.zeros_like(entries)
        for device in range(windows.shape[0]):
            first = 9 * (device // 4) + 2 * (device % 4)
            entries[first : first + 4, :] += windows[device, 0:4, :]
        vector_out[...] = jnp.zeros_like(vector_out)
        pieces = width // 128
        for row in range(12):
            for j in range(pieces):
                vector_out[row : row + 1, j * 128 : (j + 1) * 128] = entries[
                    row * pieces + j : row * pieces + j + 1, :
                ]

    for which in range(3):
        value = jnp.dot(frames[...], weights[which], preferred_element_type=F32)
        if which == 0:
            value = value + vector_out[0:1, :]
        if which == 2:
            value = value + vector_out[1:2, :]
        outs[which][...] = value.astype(BF)

    @pl.when(pl.program_id(0) == pl.num_programs(0) - 1)
    def finish():
        copy.wait()


def project_qkv(place, frames, blocks, tile=256):
    count, width = frames.shape
    low = struct((count, width), BF)
    row_tile = pl.BlockSpec((tile, width), lambda i: (i, 0))
    anywhere = pl.BlockSpec(memory_space=pl.ANY)
    return pl.pallas_call(
        partial(qkv_kernel, place.depth),
        grid=(count // tile,),
        in_specs=[pl.BlockSpec(memory_space=pltpu.SMEM), row_tile]
        + [pl.BlockSpec(block.shape, lambda i: (0, 0, 0)) for block in blocks],
        out_specs=[row_tile] * 3
        + [pl.BlockSpec((16, width), lambda i: (0, 0)), anywhere],
        out_shape=[low, low, low, struct((16, width), F32), struct((3, width, width), BF)],
        scratch_shapes=[
            pltpu.VMEM((3, width, width), BF),
            pltpu.VMEM((place.count, 8, 128), F32),
            pltpu.VMEM((80, 128), F32),
            pltpu.SemaphoreType.DMA,
        ],
        compiler_params=params(),
        cost_estimate=cost(6 * count * width * width, 10 * count * width, times=1),
        name="project_qkv",
    )(place.coords, frames, *blocks)


def attention_forward_kernel(q_ref, k_ref, v_ref, q_mark, k_mark, out_ref, weights_ref):
    count = q_ref.shape[0]
    valid = weights_ref.shape[2]
    values = v_ref[...].T
    lane = lax.broadcasted_iota(jnp.int32, (count, 128), 1)
    outs = []
    for head in (0, 1):
        own = (lane < 64) == (head == 0)
        keys = jnp.where(own, k_ref[...], k_mark[...])
        queries = jnp.where(own, q_ref[...] * BF(SCORE_SCALE), q_mark[...])
        scores = lax.dot_general(keys, queries, NT, preferred_element_type=F32)
        maximum = jnp.max(scores, axis=0, keepdims=True)
        raised = jnp.exp(scores - maximum)
        total = jnp.sum(raised, axis=0, keepdims=True)
        weights = (raised * (1.0 / total)).astype(BF)
        weights_ref[0, head] = weights[0:valid, :]
        rows = values[64 * head : 64 * head + 64, :]
        outs.append(jnp.dot(rows, weights, preferred_element_type=F32))
    out_ref[...] = jnp.concatenate(outs, axis=0).T.astype(BF)


def attention_forward(q, k, v, q_mark, k_mark, valid):
    count, width = q.shape
    pairs = width // 128
    column = pl.BlockSpec((count, 128), lambda i: (0, i))
    whole = pl.BlockSpec((count, 128), lambda i: (0, 0))
    return pl.pallas_call(
        attention_forward_kernel,
        grid=(pairs,),
        in_specs=[column] * 3 + [whole] * 2,
        out_specs=(column, pl.BlockSpec((1, 2, valid, count), lambda i: (i, 0, 0, 0))),
        out_shape=(struct((count, width), BF), struct((pairs, 2, valid, count), BF)),
        compiler_params=params(),
        cost_estimate=cost(
            16 * count * count * width, 8 * count * width, 12 * count * count, times=1
        ),
        name="attention_forward",
    )(q, k, v, q_mark, k_mark)


def attention_backward_kernel(
    valid, long_clip, lead_ref, q_ref, k_ref, v_ref, g_ref, weights_ref, grads_ref, sum_ref,
    dk_scr, dv_scr,
):
    count = q_ref.shape[0]

    def gradients(tiles, key_rows, query_rows):
        lane = lax.broadcasted_iota(jnp.int32, (count, 128), 1)
        keys_turned = k_ref[0:key_rows, :].T
        single = len(tiles) == 1
        if not single:
            dk_scr[...] = jnp.zeros_like(dk_scr)
            dv_scr[...] = jnp.zeros_like(dv_scr)
        masked = []
        for head in (0, 1):
            own = (lane < 64) == (head == 0)
            masked.append(
                (
                    jnp.where(own, q_ref[...] * BF(SCORE_SCALE), BF(0)),
                    jnp.where(own, g_ref[...], BF(0)),
                )
            )
        for queries, keys in tiles:
            turned = []
            dk = None
            for head in (0, 1):
                grads = masked[head][1][queries]
                weights_low = weights_ref[0, head, keys, queries]
                slopes = lax.dot_general(v_ref[keys, :], grads, NT, preferred_element_type=F32)
                weights = weights_low.astype(F32)
                inner = jnp.sum(weights * slopes, axis=0, keepdims=True)
                ds = (weights * (slopes - inner)).astype(BF)
                turned.append(
                    jnp.dot(
                        keys_turned[64 * head : 64 * head + 64, keys],
                        ds,
                        preferred_element_type=F32,
                    )
                    * SCORE_SCALE
                )
                dk_part = jnp.dot(ds, masked[head][0][queries], preferred_element_type=F32)
                dv_part = jnp.dot(weights_low, grads, preferred_element_type=F32)
                dk = dk_part if dk is None else dk + dk_part
                dv = dv_part if head == 0 else dv + dv_part
            dq = jnp.concatenate(turned, axis=0).T.astype(BF)
            grads_ref[0, queries, :] = dq
            sum_ref[0:1, :] += jnp.sum(dq.astype(F32), axis=0, keepdims=True)
            if not single:
                dk_scr[keys, :] += dk
                dv_scr[keys, :] += dv
        if not single:
            dk = dk_scr[0:key_rows, :]
            dv = dv_scr[0:key_rows, :]
        grads_ref[1, 0:key_rows, :] = dk.astype(BF)
        dv = dv.astype(BF)
        grads_ref[2, 0:key_rows, :] = dv
        sum_ref[1:2, :] += jnp.sum(dv.astype(F32), axis=0, keepdims=True)
        rest = jnp.zeros((count - key_rows, 128), BF)
        if key_rows < count:
            grads_ref[1, key_rows:count, :] = rest
            grads_ref[2, key_rows:count, :] = rest
        if query_rows < count:
            grads_ref[0, query_rows:count, :] = jnp.zeros((count - query_rows, 128), BF)

    sum_ref[...] = jnp.zeros_like(sum_ref)

    @pl.when(lead_ref[0] > 0)
    def one_long_clip():
        keys = -(-long_clip // 16) * 16
        queries = -(-long_clip // 128) * 128
        gradients([(slice(0, queries), slice(0, keys))], keys, queries)

    @pl.when(lead_ref[0] == 0)
    def short_clips():
        tiles = []
        for start in range(0, valid, 512):
            first = start // SHORT * SHORT // 128 * 128
            last = min(-(-(start + 512) // SHORT) * SHORT, valid)
            keys = slice(first, min(-(-last // 16) * 16, valid))
            tiles.append((slice(start, start + 512), keys))
        gradients(tiles, valid, count)


def attention_backward(lead, q, k, v, grads, weights, valid, first, pairs, earlier=()):
    count, width = q.shape
    column = pl.BlockSpec((count, 128), lambda i: (0, first + i))

    def kernel(*refs):
        attention_backward_kernel(valid, LONG, *refs[:6], *refs[6 + len(earlier) :])

    return pl.pallas_call(
        kernel,
        grid=(pairs,),
        in_specs=[pl.BlockSpec(memory_space=pltpu.SMEM)]
        + [column] * 4
        + [pl.BlockSpec((1, 2, valid, count), lambda i: (first + i, 0, 0, 0))]
        + [pl.BlockSpec(memory_space=pl.ANY)] * len(earlier),
        out_specs=(
            pl.BlockSpec((3, count, 128), lambda i: (0, 0, first + i)),
            pl.BlockSpec((8, 128), lambda i: (0, first + i)),
        ),
        out_shape=(struct((3, count, width), BF), struct((8, width), F32)),
        scratch_shapes=[pltpu.VMEM((valid, 128), F32)] * 2,
        input_output_aliases={6 + i: i for i in range(len(earlier))},
        compiler_params=params(),
        cost_estimate=cost(
            32 * count * count * 128 * pairs, 14 * count * 128 * pairs, 2 * count * count * pairs
        ),
        name="attention_backward",
    )(lead, q, k, v, grads, weights, *earlier)


def gelu_parts(value):
    upper = 0.5 + 0.5 * lax.erf(value * INV_SQRT2)
    fall = jnp.exp2(value * value * (-0.5 * LOG2_E))
    return value * upper, upper + value * fall * INV_SQRT_2PI


def normalize(hidden):
    mean = jnp.mean(hidden, axis=-1, keepdims=True)
    centred = hidden - mean
    variance = jnp.mean(centred * centred, axis=-1, keepdims=True)
    inverse = lax.rsqrt(variance + NORM_EPS)
    return centred * inverse, inverse


def norm_backward(grad_output, hat, inverse, gain):
    scaled = grad_output * gain
    return inverse * (
        scaled
        - jnp.mean(scaled, axis=-1, keepdims=True)
        - hat * jnp.mean(scaled * hat, axis=-1, keepdims=True)
    )


def column_sums(value):
    return jnp.sum(value, axis=0, keepdims=True)


def interleave(*works):
    works = list(works)
    while works:
        for work in list(works):
            try:
                next(work)
            except StopIteration:
                works.remove(work)


def middle_kernel(packed, last_rows, total_ref, frames, context, cotangent, vector, *refs):
    weight_refs = refs[: 1 if packed else 3]
    (
        result, normed_out, activated_out, down_g_out, up_g_out, first_g_out, attended_g_out,
        context_g_out, sums, up_w, down_w, out_w, raw_up, raw_out, slopes, first_hats,
        second_hats, inverses, down_total, grad_total, sems,
    ) = refs[len(weight_refs) :]
    step = pl.program_id(0)
    tiles = pl.num_programs(0) - 1
    tile, width = frames.shape
    hidden = up_w.shape[1]

    if packed:
        wire = weight_refs[0]
        copies = (
            pltpu.make_async_copy(wire.at[:, 2 * width : 2 * width + 256], raw_out, sems.at[0]),
            pltpu.make_async_copy(wire.at[:, width : 2 * width], raw_up, sems.at[1]),
            pltpu.make_async_copy(wire.at[:, 0:width], down_w, sems.at[2]),
        )
    else:
        copies = (
            pltpu.make_async_copy(weight_refs[0], out_w, sems.at[0]),
            pltpu.make_async_copy(weight_refs[1], up_w, sems.at[1]),
            pltpu.make_async_copy(weight_refs[2], down_w, sems.at[2]),
        )

    def unpack(raw, target, columns, pieces):
        rows = 24

        def pair(chip, carry):
            start = pl.multiple_of(chip * 8 * rows, 16)
            value = raw[pl.ds(start, 8 * rows), :].astype(F32)
            for j in range(pieces):
                both = jnp.concatenate(
                    [
                        value[j * rows : (j + 1) * rows],
                        value[(4 + j) * rows : (5 + j) * rows],
                    ],
                    axis=0,
                )
                to = pl.multiple_of(chip * 2 * rows, 16)
                target[pl.ds(to, 2 * rows), j * columns : (j + 1) * columns] = both.astype(BF)
            return carry

        lax.fori_loop(0, width // (2 * rows), pair, 0)

    def add_sum(row, value):
        sums[row : row + 1, :] += value

    def valid_rows(number, rows):
        position = number * tile + lax.broadcasted_iota(jnp.int32, (rows, 1), 0)
        return (position < total_ref[0]).astype(F32)

    def forward_start():
        attended = jnp.dot(context[...], out_w[...], preferred_element_type=F32) + vector[2:3, :]
        first_sum = frames[...].astype(F32) + attended
        first_hat, first_inverse = normalize(first_sum)
        normed_out[...] = (first_hat * vector[4:5, :] + vector[5:6, :]).astype(BF)
        first_hats[slot] = first_hat
        inverses[slot, 0] = jnp.broadcast_to(first_inverse, (tile, 128))
        valid = valid_rows(step, tile)
        add_sum(12, column_sums(valid * attended * attended))
        add_sum(13, column_sums(valid * first_sum * first_sum))
        add_sum(16, jnp.broadcast_to(column_sums(valid), (1, width)))
        down_total[...] = jnp.broadcast_to(vector[3:4, :], (tile, width))

    def forward_chunk(part, row):
        pre = jnp.dot(normed_out[...], up_w[:, part], preferred_element_type=F32)
        yield
        activated, slope = gelu_parts(pre + vector[pl.ds(row, 1), :])
        slopes[slot, :, part] = slope
        activated = activated.astype(BF)
        activated_out[:, part] = activated
        yield
        down_total[...] += jnp.dot(activated, down_w[part, :], preferred_element_type=F32)

    def forward_end():
        down_out = down_total[...]
        second_sum = normed_out[...].astype(F32) + down_out
        second_hat, second_inverse = normalize(second_sum)
        result[...] = (second_hat * vector[6:7, :] + vector[7:8, :]).astype(BF)
        second_hats[slot] = second_hat
        inverses[slot, 1] = jnp.broadcast_to(second_inverse, (tile, 128))
        valid = valid_rows(step, tile)
        add_sum(14, column_sums(valid * down_out * down_out))
        add_sum(15, column_sums(valid * second_sum * second_sum))

    def backward_start(rows):
        out_g = cotangent[0:rows, :].astype(F32) * valid_rows(step - 1, rows)
        second_hat = second_hats[other, 0:rows, :]
        grad_second = norm_backward(
            out_g, second_hat, inverses[other, 1, 0:rows, 0:1], vector[6:7, :]
        )
        add_sum(6, column_sums(out_g * second_hat))
        add_sum(7, column_sums(out_g))
        down_g = grad_second.astype(BF)
        down_g_out[0:rows, :] = down_g
        add_sum(3, column_sums(down_g.astype(F32)))
        grad_total[0:rows, :] = grad_second

    def backward_chunk(rows, part, row):
        grad = lax.dot_general(
            down_g_out[0:rows, :], down_w[part, :], NT, preferred_element_type=F32
        )
        yield
        up_g = (grad * slopes[other, 0:rows, part]).astype(BF)
        up_g_out[0:rows, part] = up_g
        sums[pl.ds(row, 1), :] += column_sums(up_g.astype(F32))
        yield
        grad_total[0:rows, :] += lax.dot_general(
            up_g, up_w[:, part], NT, preferred_element_type=F32
        )

    def backward_end(rows):
        grad_normed = grad_total[0:rows, :]
        first_hat = first_hats[other, 0:rows, :]
        grad_first = norm_backward(
            grad_normed, first_hat, inverses[other, 0, 0:rows, 0:1], vector[4:5, :]
        )
        add_sum(4, column_sums(grad_normed * first_hat))
        add_sum(5, column_sums(grad_normed))
        first_g_out[0:rows, :] = grad_first
        attended_g = grad_first.astype(BF)
        attended_g_out[0:rows, :] = attended_g
        add_sum(2, column_sums(attended_g.astype(F32)))
        context_g_out[0:rows, :] = lax.dot_general(
            attended_g, out_w[...], NT, preferred_element_type=F32
        ).astype(BF)

    def chunks(work, unroll):
        def body(j, carry):
            work(pl.ds(pl.multiple_of(j * width, width), width), 8 + j)
            return carry

        lax.fori_loop(0, hidden // width, body, 0, unroll=unroll)

    slot = lax.rem(step, 2)
    other = 1 - slot

    @pl.when(step == 0)
    def first_step():
        for copy in copies:
            copy.start()
        sums[...] = jnp.zeros_like(sums)
        copies[0].wait()
        if packed:
            unpack(raw_out, out_w, 256, 3)
        forward_start()
        copies[1].wait()
        if packed:
            unpack(raw_up, up_w, width, 4)
        copies[2].wait()
        chunks(lambda part, row: interleave(forward_chunk(part, row)), 2)
        forward_end()

    @pl.when((step > 0) & (step < tiles))
    def middle_step():
        forward_start()
        backward_start(tile)
        chunks(
            lambda part, row: interleave(
                backward_chunk(tile, part, row), forward_chunk(part, row)
            ),
            4,
        )
        forward_end()
        backward_end(tile)

    @pl.when(step == tiles)
    def last_step():
        backward_start(last_rows)
        chunks(lambda part, row: interleave(backward_chunk(last_rows, part, row)), 2)
        backward_end(last_rows)
        if last_rows < tile:
            for ref in (down_g_out, up_g_out, first_g_out, attended_g_out, context_g_out):
                ref[last_rows:tile, :] = jnp.zeros((tile - last_rows, ref.shape[1]), ref.dtype)


def middle(frames, context, cotangent, vector, total, weights, hidden, valid, tile=256):
    count, width = frames.shape
    packed = len(weights) == 1
    tiles = count // tile
    last_rows = min(tile, valid - (tiles - 1) * tile)

    def early(columns):
        return pl.BlockSpec((tile, columns), lambda i: (jnp.minimum(i, tiles - 1), 0))

    def late(columns):
        return pl.BlockSpec((tile, columns), lambda i: (jnp.maximum(i - 1, 0), 0))

    anywhere = pl.BlockSpec(memory_space=pl.ANY)
    low = struct((count, width), BF)
    wide = struct((count, hidden), BF)
    raw = hidden if packed else 16
    return pl.pallas_call(
        partial(middle_kernel, packed, last_rows),
        grid=(tiles + 1,),
        in_specs=[
            pl.BlockSpec(memory_space=pltpu.SMEM),
            early(width),
            early(width),
            late(width),
            pl.BlockSpec(vector.shape, lambda i: (0, 0)),
        ]
        + [anywhere] * len(weights),
        out_specs=[
            early(width), early(width), early(hidden), late(width), late(hidden), late(width),
            late(width), late(width), pl.BlockSpec((24, width), lambda i: (0, 0)),
        ],
        out_shape=[
            low, low, wide, low, wide, struct((count, width), F32), low, low,
            struct((24, width), F32),
        ],
        scratch_shapes=[
            pltpu.VMEM((width, hidden), BF),
            pltpu.VMEM((hidden, width), BF),
            pltpu.VMEM((width, width), BF),
            pltpu.VMEM((raw, width), BF),
            pltpu.VMEM((raw, 256), BF),
            pltpu.VMEM((2, tile, hidden), F32),
            pltpu.VMEM((2, tile, width), F32),
            pltpu.VMEM((2, tile, width), F32),
            pltpu.VMEM((2, 2, tile, 128), F32),
            pltpu.VMEM((tile, width), F32),
            pltpu.VMEM((tile, width), F32),
            pltpu.SemaphoreType.DMA((3,)),
        ],
        compiler_params=params(),
        cost_estimate=cost(
            2 * count * width * (4 * hidden + 2 * width),
            count * (14 * width + 4 * hidden) + 4 * width * hidden,
            2 * count * hidden,
        ),
        name="feed_forward",
    )(total, frames, context, cotangent, vector, *weights)


def split_by_core(value, rows, first, mine, theirs):
    for chip in range(value.shape[0] // (2 * rows)):
        low = value[2 * chip * rows : (2 * chip + 1) * rows, :]
        high = value[(2 * chip + 1) * rows : (2 * chip + 2) * rows, :]
        mine[chip] = jnp.where(first, low, high).astype(BF)
        theirs[chip] = jnp.where(first, high, low).astype(BF)


def down_grad_kernel(valid, rows, coords, left, right, mine, theirs):
    value = lax.dot_general(
        left[0:valid, :], right[0:valid, :], TN, preferred_element_type=F32
    )
    first = coords[3] == 0
    width = right.shape[1]
    for chip in range(mine.shape[0]):
        for j in range(4):
            lanes = slice(j * width, (j + 1) * width)
            start = 8 * chip * rows + j * rows
            low = value[start : start + rows, :]
            high = value[start + 4 * rows : start + 5 * rows, :]
            mine[chip, :, lanes] = jnp.where(first, low, high).astype(BF)
            theirs[chip, :, lanes] = jnp.where(first, high, low).astype(BF)


def down_grad(place, left, right, valid, chips=4):
    count, hidden = left.shape
    width = right.shape[1]
    rows = width // place.count
    tile = 8 * rows * chips
    out = pl.BlockSpec((chips, rows, 4 * width), lambda i, c: (i, 0, 0))
    outs = struct((place.count // 2, rows, 4 * width), BF)
    return pl.pallas_call(
        partial(down_grad_kernel, valid, rows),
        grid_spec=pltpu.PrefetchScalarGridSpec(
            num_scalar_prefetch=1,
            grid=(hidden // tile,),
            in_specs=[
                pl.BlockSpec((count, tile), lambda i, c: (0, i)),
                pl.BlockSpec((count, width), lambda i, c: (0, 0)),
            ],
            out_specs=[out, out],
        ),
        out_shape=[outs, outs],
        compiler_params=params(),
        cost_estimate=cost(2 * count * hidden * width, 2 * count * (hidden + width)),
        name="grad_down",
    )(place.coords, left, right)


def up_grad_kernel(
    valid, rows, coords, left, right, out_left, out_right, mine, theirs, lefts, rights, sems
):
    step = pl.program_id(0)
    last = pl.num_programs(0) - 1
    copies = (
        pltpu.make_async_copy(out_left, lefts, sems.at[0]),
        pltpu.make_async_copy(out_right, rights, sems.at[1]),
    )

    @pl.when(step == 0)
    def fetch():
        for copy in copies:
            copy.start()

    @pl.when(step < last)
    def up_part():
        value = lax.dot_general(
            left[0:valid, :], right[0:valid, :], TN, preferred_element_type=F32
        )
        split_by_core(value, rows, coords[3] == 0, mine, theirs)

    @pl.when(step == last)
    def out_part():
        for copy in copies:
            copy.wait()
        value = lax.dot_general(
            lefts[0:valid, :], rights[0:valid, :], TN, preferred_element_type=F32
        )
        split_by_core(value, rows, coords[3] == 0, mine, theirs)


def up_grad(place, left, right, out_left, out_right, valid):
    count, width = left.shape
    rows = width // place.count
    steps = right.shape[1] // width + 1
    anywhere = pl.BlockSpec(memory_space=pl.ANY)
    out = pl.BlockSpec((place.count // 2, rows, width), lambda i, c: (0, 0, i))
    outs = struct((place.count // 2, rows, steps * width), BF)
    return pl.pallas_call(
        partial(up_grad_kernel, valid, rows),
        grid_spec=pltpu.PrefetchScalarGridSpec(
            num_scalar_prefetch=1,
            grid=(steps,),
            in_specs=[
                pl.BlockSpec((count, width), lambda i, c: (0, 0)),
                pl.BlockSpec((count, width), lambda i, c: (0, jnp.minimum(i, steps - 2))),
                anywhere,
                anywhere,
            ],
            out_specs=[out, out],
            scratch_shapes=[
                pltpu.VMEM((count, width), BF),
                pltpu.VMEM((count, width), BF),
                pltpu.SemaphoreType.DMA((2,)),
            ],
        ),
        out_shape=[outs, outs],
        compiler_params=params(),
        cost_estimate=cost(
            2 * count * steps * width * width, 2 * (count + width) * (steps + 1) * width
        ),
        name="grad_up_and_out",
    )(place.coords, left, right, out_left, out_right)


def qkv_grad_kernel(
    valid, rows, coords, left, right, sums, more, mine, theirs, kept, sent, entries, sems
):
    step = pl.program_id(0)
    width = left.shape[1]
    first = coords[3] == 0

    def copies(start, size, number):
        lanes = pl.ds(start, size)
        return (
            pltpu.make_async_copy(kept.at[:, :, lanes], mine.at[:, :, lanes], sems.at[0, number]),
            pltpu.make_async_copy(sent.at[:, :, lanes], theirs.at[:, :, lanes], sems.at[1, number]),
        )

    for which in range(3):

        @pl.when(step == which)
        def part(which=which):
            lanes = slice(which * width, (which + 1) * width)
            value = lax.dot_general(
                left[0:valid, :], right[0, 0:valid, :], TN, preferred_element_type=F32
            )
            split_by_core(value, rows, first, kept.at[:, :, lanes], sent.at[:, :, lanes])
            for copy in copies(which * width, width, which):
                copy.start()

    @pl.when(step == 2)
    def vector_part():
        pieces = width // 128
        entries[...] = jnp.zeros_like(entries)
        for row in range(12):
            value = sums[row : row + 1, :]
            if row < 2:
                value = value + more[row : row + 1, :]
            for j in range(pieces):
                entries[row * pieces + j : row * pieces + j + 1, :] = value[
                    :, j * 128 : (j + 1) * 128
                ]
        blank = jnp.zeros((rows - 4, 128), F32)
        lanes = slice(3 * width, 3 * width + 128)
        for chip in range(kept.shape[0]):
            windows = []
            for device in (2 * chip, 2 * chip + 1):
                start = 9 * (device // 4) + 2 * (device % 4)
                windows.append(jnp.concatenate([entries[start : start + 4, :], blank], axis=0))
            kept[chip, :, lanes] = jnp.where(first, windows[0], windows[1]).astype(BF)
            sent[chip, :, lanes] = jnp.where(first, windows[1], windows[0]).astype(BF)
        for copy in copies(3 * width, 128, 3):
            copy.start()
        for which in range(3):
            for copy in copies(which * width, width, which):
                copy.wait()
        for copy in copies(3 * width, 128, 3):
            copy.wait()


def qkv_grad(place, left, right, sums, more, valid):
    count, width = left.shape
    rows = width // place.count
    wire = (place.count // 2, rows, 3 * width + 128)
    anywhere = pl.BlockSpec(memory_space=pl.ANY)
    return pl.pallas_call(
        partial(qkv_grad_kernel, valid, rows),
        grid_spec=pltpu.PrefetchScalarGridSpec(
            num_scalar_prefetch=1,
            grid=(3,),
            in_specs=[
                pl.BlockSpec((count, width), lambda i, c: (0, 0)),
                pl.BlockSpec((1, count, width), lambda i, c: (i, 0, 0)),
                pl.BlockSpec(sums.shape, lambda i, c: (0, 0)),
                pl.BlockSpec(more.shape, lambda i, c: (0, 0)),
            ],
            out_specs=[anywhere, anywhere],
            scratch_shapes=[
                pltpu.VMEM(wire, BF),
                pltpu.VMEM(wire, BF),
                pltpu.VMEM((80, 128), F32),
                pltpu.SemaphoreType.DMA((2, 4)),
            ],
        ),
        out_shape=[struct(wire, BF)] * 2,
        compiler_params=params(),
        cost_estimate=cost(6 * count * width * width, 8 * (count + width) * width),
        name="grad_qkv",
    )(place.coords, left, right, sums, more)


def frames_grad_kernel(first_g, grads, weights, out):
    value = first_g[...]
    for which in range(3):
        value = value + lax.dot_general(
            grads[which], weights[which], NT, preferred_element_type=F32
        )
    out[...] = value.astype(BF)


def frames_gradient(first_g, grads, weights, tile=256):
    count, width = first_g.shape
    row_tile = pl.BlockSpec((tile, width), lambda i: (i, 0))
    return pl.pallas_call(
        frames_grad_kernel,
        grid=(count // tile,),
        in_specs=[
            row_tile,
            pl.BlockSpec((3, tile, width), lambda i: (0, i, 0)),
            pl.BlockSpec(weights.shape, lambda i: (0, 0, 0)),
        ],
        out_specs=row_tile,
        out_shape=struct((count, width), BF),
        compiler_params=params(),
        cost_estimate=cost(6 * count * width * width, 12 * count * width + 6 * width * width),
        name="frames_gradient",
    )(first_g, grads, weights)


def adam_update(master, first, second, gradient, step_rate, decay_rate):
    first_new = BETA_FIRST * first + (1.0 - BETA_FIRST) * gradient
    second_new = BETA_SECOND * second + (1.0 - BETA_SECOND) * gradient * gradient
    first_hat = first_new / (1.0 - BETA_FIRST**STEP)
    second_hat = second_new / (1.0 - BETA_SECOND**STEP)
    updated = master - step_rate * (
        first_hat / (jnp.sqrt(second_hat) + ADAM_EPS) + decay_rate * master
    )
    return (first_new, second_new, updated, updated.astype(BF))


def segment_marks(length_row, frame_count):
    clip_ends = jnp.cumsum(length_row)
    position = jnp.arange(frame_count, dtype=jnp.int32)
    segment = jnp.sum((clip_ends[None, :] <= position[:, None]).astype(jnp.int32), axis=1)
    lane = jnp.arange(128, dtype=jnp.int32)[None, :] % 64
    same = lane == segment[:, None]
    q_mark = jnp.where(same, 1.0, 0.0).astype(BF)
    k_mark = jnp.where(same | (lane >= 8), 0.0, -MASKED).astype(BF)
    return q_mark, k_mark, clip_ends[-1:].astype(jnp.int32)


def gather_vector(place, shard):
    blank = jnp.zeros((place.count, shard.shape[0]), BF)
    own = lax.dynamic_update_slice(blank, shard[None, :], (place.index, 0))
    return place.total(own)


def after(values, things):
    return lax.optimization_barrier((values, things))[0]


def shards(n_dp, n_fsdp, *arrays):
    (
        frames, cotangent, lengths, qkv_master, out_master, up_master, down_master, vector_master,
        qkv_first, qkv_second, out_first, out_second, up_first, up_second, down_first,
        down_second, vector_first, vector_second,
    ) = arrays
    place = Place(n_dp, n_fsdp)
    frame_count, width = frames.shape
    hidden = up_master.shape[1]
    rows = out_master.shape[0]
    valid = min(frame_count, -(-MOST_VALID // 16) * 16)
    fast = n_dp == 4 and place.depth == 4 and rows == 24

    q_mark, k_mark, total = segment_marks(lengths[0], frame_count)
    if fast:
        qkv_wire, wire_low = pack(
            place, qkv_master, out_master, up_master, down_master, vector_master[None, :]
        )
        wire = lax.all_gather(wire_low, AXES, axis=0, tiled=True)
        blocks = gather_blocks(place, qkv_wire)
        queries, keys, values, vector, qkv_full = project_qkv(place, frames, blocks)
        weights = (wire,)
    else:
        vector = gather_vector(place, vector_master.astype(BF)).astype(F32).reshape(-1, width)
        qkv_full = lax.all_gather(qkv_master.astype(BF), AXES, axis=1, tiled=True)
        projected = jnp.einsum("fd,cde->cfe", frames, qkv_full, preferred_element_type=F32)
        queries = (projected[0] + vector[0]).astype(BF)
        keys = projected[1].astype(BF)
        values = (projected[2] + vector[1]).astype(BF)
        weights = tuple(
            lax.all_gather(w.astype(BF), AXES, axis=0, tiled=True)
            for w in (out_master, up_master, down_master)
        )

    context, attention = attention_forward(queries, keys, values, q_mark, k_mark, valid)
    (
        result, normed, activated, down_g, up_g, first_g, attended_g, context_g, sums,
    ) = middle(frames, context, cotangent, vector, total, weights, hidden, valid)

    def attention_part(first, pairs, start, earlier=()):
        return attention_backward(
            lengths[0, 0:1], start, keys, values, context_g, attention, valid, first, pairs, earlier
        )

    if fast:
        down_mine, theirs = down_grad(place, activated, down_g, valid)
        down_got = place.swap_core(theirs)
        up_mine, theirs = up_grad(
            place, after(normed, down_mine), up_g, context, attended_g, valid
        )
        up_got = place.swap_core(theirs)
        all_sums = lax.all_gather(sums, AXES, axis=0)
        most = Reduction(place)
        done = most.first(after(down_mine, up_mine), down_got)
        grads = attention_part(0, 3, after(queries, done))
        done = most.first(after(up_mine, grads[1]), up_got)
        qkv_g, bias_sums = attention_part(3, 3, after(queries, done), grads)
        most.parts[0], all_sums = after((most.parts[0], all_sums), bias_sums)
        done = most.second()
        mine, theirs = qkv_grad(
            place, after(frames, (done, all_sums)), qkv_g, sums, bias_sums, valid
        )
        got = place.swap_core(theirs)
        most.sums = after(most.sums, mine)
        done = most.third()
        last = Reduction(place)
        done = last.first(after(mine, done), got)
        frames_grad = frames_gradient(after(first_g, done), qkv_g, qkv_full)
        most.sums = after(most.sums, frames_grad)
        done = most.fourth(0)
        last.parts[0] = after(last.parts[0], done)
        last.second()
        done = last.spread()
        most.sums, all_sums = after((most.sums, all_sums), done)
        grad_most = most.result()
        grad_qkv = last.result()
        grad_down = grad_most[:, : 4 * width].reshape(rows, 4, width)
        grad_down = grad_down.transpose(1, 0, 2).reshape(4 * rows, width)
        grad_up = grad_most[:, 4 * width : 8 * width]
        grad_out = grad_most[:, 8 * width :]
        window = grad_qkv[0:4, 3 * width :].reshape(-1)
        grad_vector = lax.dynamic_slice(
            window, (32 * (place.index % 4),), (vector_master.shape[0],)
        )
        grad_qkv = grad_qkv[:, : 3 * width].reshape(rows, 3, width).transpose(1, 0, 2)
        squares = jnp.sum(all_sums[:, 12:17], axis=(0, 2))
        layer_rms = jnp.sqrt(squares[0:4] / squares[4])
    else:
        def scatter(value, dimension):
            return lax.psum_scatter(value, AXES, scatter_dimension=dimension, tiled=True)

        def product(left, right):
            return lax.dot_general(left, right, TN, preferred_element_type=F32)

        qkv_g, bias_sums = attention_part(0, HEADS // 2, queries)
        grad_down = scatter(product(activated, down_g), 0)
        grad_up = scatter(product(normed, up_g), 0)
        grad_out = scatter(product(context, attended_g), 0)
        grad_qkv = scatter(jnp.stack([product(frames, qkv_g[i]) for i in range(3)]), 1)
        frames_grad = frames_gradient(first_g, qkv_g, qkv_full)
        sums = place.total(sums + jnp.pad(bias_sums, ((0, 16), (0, 0))))
        grad_vector = lax.dynamic_slice(
            sums[0:12].reshape(-1),
            (place.index * vector_master.shape[0],),
            (vector_master.shape[0],),
        )
        layer_rms = jnp.sqrt(jnp.sum(sums[12:16], axis=1) / jnp.sum(sums[16]))

    down_new = adam_update(
        down_master, down_first, down_second, grad_down, MATRIX_RATE, WEIGHT_DECAY
    )
    up_new = adam_update(up_master, up_first, up_second, grad_up, MATRIX_RATE, WEIGHT_DECAY)
    out_new = adam_update(out_master, out_first, out_second, grad_out, MATRIX_RATE, WEIGHT_DECAY)
    qkv_new = adam_update(qkv_master, qkv_first, qkv_second, grad_qkv, MATRIX_RATE, WEIGHT_DECAY)
    vector_new = adam_update(
        vector_master, vector_first, vector_second, grad_vector, VECTOR_RATE, 0.0
    )
    return (
        (result, frames_grad, layer_rms) + qkv_new + out_new + up_new + down_new + vector_new
    )


def solution(mesh):
    rows = P(AXES, None)
    middle_rows = P(None, AXES, None)
    entries = P(AXES)
    return jax.shard_map(
        partial(shards, mesh.shape["dp"], mesh.shape["fsdp"]),
        mesh=mesh,
        in_specs=(
            rows, rows, rows, middle_rows, rows, rows, rows, entries,
            middle_rows, middle_rows, rows, rows, rows, rows, rows, rows, entries, entries,
        ),
        out_specs=(rows, rows, P())
        + (middle_rows,) * 4
        + (rows,) * 12
        + (entries,) * 4,
        check_vma=False,
    )
```

```python
from functools import partial

import jax
import jax.numpy as jnp
from jax import lax
from jax.experimental import pallas as pl
from jax.experimental.pallas import tpu as pltpu
from jax.sharding import PartitionSpec as P

HEADS = 12
STEP = 10
LONG = 780
SHORT = 150
MOST_VALID = 900

MASKED = 1e30
NORM_EPS = 1e-05
SCORE_SCALE = 0.125
BETA_FIRST = 0.9
BETA_SECOND = 0.98
ADAM_EPS = 1e-06
MATRIX_RATE = 0.05
VECTOR_RATE = 0.3
WEIGHT_DECAY = 0.01
AXES = ("dp", "fsdp")
BF = jnp.bfloat16
F32 = jnp.float32
NT = (((1,), (1,)), ((), ()))
TN = (((0,), (0,)), ((), ()))
VMEM_LIMIT = 60 * 2**20
INV_SQRT2 = 0.7071067811865476
INV_SQRT_2PI = 0.3989422804014327
LOG2_E = 1.4426950408889634


def struct(shape, dtype):
    return jax.ShapeDtypeStruct(shape, dtype)


def params(**more):
    return pltpu.CompilerParams(vmem_limit_bytes=VMEM_LIMIT, **more)


def cost(flops, bytes_accessed, transcendentals=0, times=1000):
    return pl.CostEstimate(
        flops=int(flops) * times,
        bytes_accessed=int(bytes_accessed) * times,
        transcendentals=int(transcendentals) * times,
    )


class Place:
    def __init__(self, n_dp, n_fsdp):
        self.n_dp = n_dp
        self.n_fsdp = n_fsdp
        self.depth = n_fsdp // 2
        self.count = n_dp * n_fsdp
        dp = lax.axis_index("dp")
        fsdp = lax.axis_index("fsdp")
        self.index = dp * n_fsdp + fsdp
        self.coords = jnp.stack([dp // 2, dp % 2, fsdp // 2, fsdp % 2, self.index])

    def swap_x(self, value):
        return lax.ppermute(value, "dp", [(i, i ^ 1) for i in range(self.n_dp)])

    def swap_y(self, value):
        return lax.ppermute(value, "dp", [(i, i ^ 2) for i in range(self.n_dp)])

    def swap_core(self, value):
        return lax.ppermute(value, "fsdp", [(i, i ^ 1) for i in range(self.n_fsdp)])

    def shift_z(self, value, step):
        depth = self.depth
        pairs = [(i, ((i // 2 + step) % depth) * 2 + i % 2) for i in range(self.n_fsdp)]
        return lax.ppermute(value, "fsdp", pairs)

    def swap_z(self, value, bit):
        pairs = [(i, i ^ (2 * bit)) for i in range(self.n_fsdp)]
        return lax.ppermute(value, "fsdp", pairs)

    def total(self, value):
        for axis, size in (("fsdp", self.n_fsdp), ("dp", self.n_dp)):
            bit = 1
            while bit < size:
                other = lax.ppermute(value, axis, [(i, i ^ bit) for i in range(size)])
                value = value + other
                bit *= 2
        return value


def gather_blocks(place, block):
    depth = place.depth
    column = [block] + [place.shift_z(block, step) for step in range(1, depth)]
    near = jnp.stack(column[: depth // 2])
    far = jnp.stack(column[depth // 2 :])
    near_x = place.swap_x(near)
    far_y = place.swap_y(far)
    halves = [
        [near, near_x, place.swap_y(near), place.swap_y(near_x)],
        [far, place.swap_x(far), far_y, place.swap_x(far_y)],
    ]
    own = halves[0] + halves[1]
    return own + [place.swap_core(value) for value in own]


def rounded_sum(left, right):
    return (left.astype(F32) + right.astype(F32)).astype(BF)


def first_add_kernel(coords, *refs):
    for number, out in enumerate(refs[8:]):
        out[0] = rounded_sum(refs[2 * number][0, 0], refs[2 * number + 1][0, 0])


def first_add(place, mine, got):
    half = place.depth // 2
    rows, columns = mine.shape[1:]
    shape = (2, 2, place.depth, rows, columns)
    mine = mine.reshape(shape)
    got = got.reshape(shape)
    block = (1, 1, half, rows, columns)
    specs = [
        pl.BlockSpec(block, lambda i, c: (i, c[1], 0, 0, 0)),
        pl.BlockSpec(block, lambda i, c: (i, 1 - c[1], 0, 0, 0)),
        pl.BlockSpec(block, lambda i, c: (c[0], i, 1, 0, 0)),
        pl.BlockSpec(block, lambda i, c: (1 - c[0], i, 1, 0, 0)),
    ]
    out = pl.BlockSpec((1, half, rows, columns), lambda i, c: (i, 0, 0, 0))
    return pl.pallas_call(
        first_add_kernel,
        grid_spec=pltpu.PrefetchScalarGridSpec(
            num_scalar_prefetch=1,
            grid=(2,),
            in_specs=[spec for spec in specs for _ in range(2)],
            out_specs=[out] * 4,
        ),
        out_shape=[struct((2, half, rows, columns), BF)] * 4,
        compiler_params=params(),
        cost_estimate=cost(mine.size, 6 * mine.size, times=10**6),
        name="reduce_over_core",
    )(place.coords, *([mine, got] * 4))


def second_add_kernel(widths, coords, *refs):
    outs = refs[8 * len(widths) :]
    start = 0
    for part, width in enumerate(widths):
        ins = refs[8 * part : 8 * part + 8]
        for number, out in enumerate(outs):
            out[:, :, start : start + width] = rounded_sum(
                ins[2 * number][0], ins[2 * number + 1][0]
            )
        start += width


def second_add(place, parts, times):
    half, rows = parts[0][0].shape[1:3]
    widths = [part[0].shape[3] for part in parts]
    specs = []
    ins = []
    for (keep_a, got_a, keep_b, got_b), width in zip(parts, widths):
        block = (1, half, rows, width)
        stay_a = pl.BlockSpec(block, lambda i, c: (c[0], 0, 0, 0))
        leave_a = pl.BlockSpec(block, lambda i, c: (1 - c[0], 0, 0, 0))
        stay_b = pl.BlockSpec(block, lambda i, c: (c[1], 0, 0, 0))
        leave_b = pl.BlockSpec(block, lambda i, c: (1 - c[1], 0, 0, 0))
        specs += [stay_a] * 2 + [leave_a] * 2 + [stay_b] * 2 + [leave_b] * 2
        ins += [keep_a, got_a] * 2 + [keep_b, got_b] * 2
    shape = (half, rows, sum(widths))
    return pl.pallas_call(
        partial(second_add_kernel, widths),
        grid_spec=pltpu.PrefetchScalarGridSpec(
            num_scalar_prefetch=1,
            grid=(1,),
            in_specs=specs,
            out_specs=[pl.BlockSpec(shape, lambda i, c: (0, 0, 0))] * 4,
        ),
        out_shape=[struct(shape, BF)] * 4,
        compiler_params=params(),
        cost_estimate=cost(
            4 * half * rows * shape[2], 24 * half * rows * shape[2], times=times
        ),
        name="reduce_over_first_link",
    )(place.coords, *ins)


def third_add_kernel(coords, keep_a, got_a, keep_b, got_b, keep, send):
    own = lax.rem(coords[2], 2)
    for out, which in ((keep, own), (send, 1 - own)):
        out[0] = rounded_sum(keep_a[which], got_a[which])
        out[1] = rounded_sum(keep_b[which], got_b[which])


def spread_add_kernel(coords, keep_a, got_a, keep_b, got_b, *outs):
    half = keep_a.shape[0]
    for step, out in enumerate(outs):
        target = lax.rem(coords[2] + step, 2 * half)
        inner = lax.rem(target, half)
        near = keep_a[inner].astype(F32) + got_a[inner].astype(F32)
        far = keep_b[inner].astype(F32) + got_b[inner].astype(F32)
        out[...] = jnp.where(target < half, near, far).astype(BF)


def fourth_add_kernel(coords, keep, got, keep_out, send):
    own = lax.div(coords[2], 2)
    keep_out[...] = rounded_sum(keep[own], got[own])
    send[...] = rounded_sum(keep[1 - own], got[1 - own])


def small_add(place, kernel, ins, shape, name, times=10**6, outs=2):
    inside = pl.BlockSpec(memory_space=pltpu.VMEM)
    return pl.pallas_call(
        kernel,
        in_specs=[pl.BlockSpec(memory_space=pltpu.SMEM)] + [inside] * len(ins),
        out_specs=[inside] * outs,
        out_shape=[struct(shape, BF)] * outs,
        compiler_params=params(),
        cost_estimate=cost(2 * ins[0].size, 6 * ins[0].size, times=times),
        name=name,
    )(place.coords, *ins)


class Reduction:
    def __init__(self, place):
        self.place = place
        self.parts = []

    def first(self, mine, got):
        place = self.place
        keep_a, send_a, keep_b, send_b = first_add(place, mine, got)
        self.parts.append((keep_a, place.swap_x(send_a), keep_b, place.swap_y(send_b)))
        return keep_a

    def second(self, times=10**6):
        place = self.place
        keep_a, send_a, keep_b, send_b = second_add(place, self.parts, times)
        self.sums = (keep_a, place.swap_y(send_a), keep_b, place.swap_x(send_b))
        return keep_a

    def third(self, times=10**6):
        place = self.place
        keep, send = small_add(
            place, third_add_kernel, self.sums, self.sums[0].shape, "reduce_over_second_link", times
        )
        self.sums = (keep, place.swap_z(send, 1))
        return keep

    def fourth(self, times=10**6):
        place = self.place
        keep, send = small_add(
            place, fourth_add_kernel, self.sums, self.sums[0].shape[1:], "reduce_over_z", times
        )
        self.sums = (keep, place.swap_z(send, 2))
        return keep

    def spread(self, times=10**6):
        place = self.place
        blocks = small_add(
            place, spread_add_kernel, self.sums, self.sums[0].shape[1:],
            "reduce_over_second_link", times, outs=place.depth,
        )
        self.sums = (blocks[0],) + tuple(
            place.shift_z(blocks[step], step) for step in range(1, place.depth)
        )
        return blocks[0]

    def result(self):
        total = self.sums[0].astype(F32)
        for part in self.sums[1:]:
            total = total + part.astype(F32)
        return total


def pack_kernel(coords, qkv, out, up, down, vector, qkv_wire, wire, line):
    rows, width = out.shape
    for which in range(3):
        qkv_wire[:, which * width : (which + 1) * width] = qkv[which].astype(BF)
    line[...] = jnp.zeros_like(line)
    line[0:1, 0 : vector.shape[1]] = vector[...]
    moved = pltpu.roll(line[...], 32 * (coords[4] % 4), 1)
    pieces = [moved[0:1, j * 128 : (j + 1) * 128] for j in range(4)]
    pieces.append(jnp.zeros((rows - 4, 128), F32))
    qkv_wire[:, 3 * width : 3 * width + 128] = jnp.concatenate(pieces, axis=0).astype(BF)
    wire[:, 0:width] = down[...].astype(BF)
    pieces = [up[:, j * width : (j + 1) * width] for j in range(4)]
    wire[:, width : 2 * width] = jnp.concatenate(pieces, axis=0).astype(BF)
    pieces = [out[:, j * 256 : (j + 1) * 256] for j in range(3)]
    pieces.append(jnp.zeros((rows, 256), F32))
    wire[:, 2 * width : 2 * width + 256] = jnp.concatenate(pieces, axis=0).astype(BF)


def pack(place, qkv, out, up, down, vector):
    rows, width = out.shape
    inside = pl.BlockSpec(memory_space=pltpu.VMEM)
    return pl.pallas_call(
        pack_kernel,
        in_specs=[pl.BlockSpec(memory_space=pltpu.SMEM)] + [inside] * 5,
        out_shape=(
            struct((rows, 3 * width + 128), BF),
            struct((4 * rows, 2 * width + 256), BF),
        ),
        scratch_shapes=[pltpu.VMEM((8, 512), F32)],
        compiler_params=params(),
        name="round_masters",
    )(place.coords, qkv, out, up, down, vector)


def qkv_kernel(depth, coords, frames, *refs):
    blocks = refs[:16]
    q_ref, k_ref, v_ref, vector_out, w_out, weights, windows, entries, sem = refs[16:]
    half = depth // 2
    rows = blocks[0].shape[1]
    width = weights.shape[2]
    outs = (q_ref, k_ref, v_ref)
    copy = pltpu.make_async_copy(weights, w_out, sem)

    @pl.when(pl.program_id(0) == 0)
    def assemble():
        first_core = coords[3] == 0
        for number in range(8):
            far = number // 4
            y = (coords[0] + (number // 2) % 2) % 2
            x = (coords[1] + number % 2) % 2
            for j in range(half):
                z = (coords[2] + depth - (far * half + j)) % depth
                chip = (y * 2 + x) * depth + z
                start = pl.multiple_of(chip * 2 * rows, 16)
                for which in range(3):
                    part = slice(which * width, (which + 1) * width)
                    own = blocks[number][j, :, part].astype(F32)
                    other = blocks[number + 8][j, :, part].astype(F32)
                    low = jnp.where(first_core, own, other)
                    high = jnp.where(first_core, other, own)
                    weights[which, pl.ds(start, 2 * rows), :] = jnp.concatenate(
                        [low, high], axis=0
                    ).astype(BF)
                part = slice(3 * width, 3 * width + 128)
                windows[chip * 2 + coords[3]] = blocks[number][j, :, part].astype(F32)[0:8]
                windows[chip * 2 + 1 - coords[3]] = blocks[number + 8][j, :, part].astype(F32)[0:8]
        copy.start()
        entries[...] = jnp.zeros_like(entries)
        for device in range(windows.shape[0]):
            first = 9 * (device // 4) + 2 * (device % 4)
            entries[first : first + 4, :] += windows[device, 0:4, :]
        vector_out[...] = jnp.zeros_like(vector_out)
        pieces = width // 128
        for row in range(12):
            for j in range(pieces):
                vector_out[row : row + 1, j * 128 : (j + 1) * 128] = entries[
                    row * pieces + j : row * pieces + j + 1, :
                ]

    for which in range(3):
        value = jnp.dot(frames[...], weights[which], preferred_element_type=F32)
        if which == 0:
            value = value + vector_out[0:1, :]
        if which == 2:
            value = value + vector_out[1:2, :]
        outs[which][...] = value.astype(BF)

    @pl.when(pl.program_id(0) == pl.num_programs(0) - 1)
    def finish():
        copy.wait()


def project_qkv(place, frames, blocks, tile=256):
    count, width = frames.shape
    low = struct((count, width), BF)
    row_tile = pl.BlockSpec((tile, width), lambda i: (i, 0))
    anywhere = pl.BlockSpec(memory_space=pl.ANY)
    return pl.pallas_call(
        partial(qkv_kernel, place.depth),
        grid=(count // tile,),
        in_specs=[pl.BlockSpec(memory_space=pltpu.SMEM), row_tile]
        + [pl.BlockSpec(block.shape, lambda i: (0, 0, 0)) for block in blocks],
        out_specs=[row_tile] * 3
        + [pl.BlockSpec((16, width), lambda i: (0, 0)), anywhere],
        out_shape=[low, low, low, struct((16, width), F32), struct((3, width, width), BF)],
        scratch_shapes=[
            pltpu.VMEM((3, width, width), BF),
            pltpu.VMEM((place.count, 8, 128), F32),
            pltpu.VMEM((80, 128), F32),
            pltpu.SemaphoreType.DMA,
        ],
        compiler_params=params(),
        cost_estimate=cost(6 * count * width * width, 10 * count * width, times=1),
        name="project_qkv",
    )(place.coords, frames, *blocks)


def attention_forward_kernel(q_ref, k_ref, v_ref, q_mark, k_mark, out_ref, weights_ref):
    count = q_ref.shape[0]
    valid = weights_ref.shape[2]
    values = v_ref[...].T
    lane = lax.broadcasted_iota(jnp.int32, (count, 128), 1)
    outs = []
    for head in (0, 1):
        own = (lane < 64) == (head == 0)
        keys = jnp.where(own, k_ref[...], k_mark[...])
        queries = jnp.where(own, q_ref[...] * BF(SCORE_SCALE), q_mark[...])
        scores = lax.dot_general(keys, queries, NT, preferred_element_type=F32)
        maximum = jnp.max(scores, axis=0, keepdims=True)
        raised = jnp.exp(scores - maximum)
        total = jnp.sum(raised, axis=0, keepdims=True)
        weights = (raised * (1.0 / total)).astype(BF)
        weights_ref[0, head] = weights[0:valid, :]
        rows = values[64 * head : 64 * head + 64, :]
        outs.append(jnp.dot(rows, weights, preferred_element_type=F32))
    out_ref[...] = jnp.concatenate(outs, axis=0).T.astype(BF)


def attention_forward(q, k, v, q_mark, k_mark, valid):
    count, width = q.shape
    pairs = width // 128
    column = pl.BlockSpec((count, 128), lambda i: (0, i))
    whole = pl.BlockSpec((count, 128), lambda i: (0, 0))
    return pl.pallas_call(
        attention_forward_kernel,
        grid=(pairs,),
        in_specs=[column] * 3 + [whole] * 2,
        out_specs=(column, pl.BlockSpec((1, 2, valid, count), lambda i: (i, 0, 0, 0))),
        out_shape=(struct((count, width), BF), struct((pairs, 2, valid, count), BF)),
        compiler_params=params(),
        cost_estimate=cost(
            16 * count * count * width, 8 * count * width, 12 * count * count, times=1
        ),
        name="attention_forward",
    )(q, k, v, q_mark, k_mark)


def attention_backward_kernel(
    valid, long_clip, lead_ref, q_ref, k_ref, v_ref, g_ref, weights_ref, grads_ref, sum_ref,
    dk_scr, dv_scr,
):
    count = q_ref.shape[0]

    def gradients(tiles, key_rows, query_rows):
        lane = lax.broadcasted_iota(jnp.int32, (count, 128), 1)
        keys_turned = k_ref[0:key_rows, :].T
        single = len(tiles) == 1
        if not single:
            dk_scr[...] = jnp.zeros_like(dk_scr)
            dv_scr[...] = jnp.zeros_like(dv_scr)
        masked = []
        for head in (0, 1):
            own = (lane < 64) == (head == 0)
            masked.append(
                (
                    jnp.where(own, q_ref[...] * BF(SCORE_SCALE), BF(0)),
                    jnp.where(own, g_ref[...], BF(0)),
                )
            )
        for queries, keys in tiles:
            turned = []
            dk = None
            for head in (0, 1):
                grads = masked[head][1][queries]
                weights_low = weights_ref[0, head, keys, queries]
                slopes = lax.dot_general(v_ref[keys, :], grads, NT, preferred_element_type=F32)
                weights = weights_low.astype(F32)
                inner = jnp.sum(weights * slopes, axis=0, keepdims=True)
                ds = (weights * (slopes - inner)).astype(BF)
                turned.append(
                    jnp.dot(
                        keys_turned[64 * head : 64 * head + 64, keys],
                        ds,
                        preferred_element_type=F32,
                    )
                    * SCORE_SCALE
                )
                dk_part = jnp.dot(ds, masked[head][0][queries], preferred_element_type=F32)
                dv_part = jnp.dot(weights_low, grads, preferred_element_type=F32)
                dk = dk_part if dk is None else dk + dk_part
                dv = dv_part if head == 0 else dv + dv_part
            dq = jnp.concatenate(turned, axis=0).T.astype(BF)
            grads_ref[0, queries, :] = dq
            sum_ref[0:1, :] += jnp.sum(dq.astype(F32), axis=0, keepdims=True)
            if not single:
                dk_scr[keys, :] += dk
                dv_scr[keys, :] += dv
        if not single:
            dk = dk_scr[0:key_rows, :]
            dv = dv_scr[0:key_rows, :]
        grads_ref[1, 0:key_rows, :] = dk.astype(BF)
        dv = dv.astype(BF)
        grads_ref[2, 0:key_rows, :] = dv
        sum_ref[1:2, :] += jnp.sum(dv.astype(F32), axis=0, keepdims=True)
        rest = jnp.zeros((count - key_rows, 128), BF)
        if key_rows < count:
            grads_ref[1, key_rows:count, :] = rest
            grads_ref[2, key_rows:count, :] = rest
        if query_rows < count:
            grads_ref[0, query_rows:count, :] = jnp.zeros((count - query_rows, 128), BF)

    sum_ref[...] = jnp.zeros_like(sum_ref)

    @pl.when(lead_ref[0] > 0)
    def one_long_clip():
        keys = -(-long_clip // 16) * 16
        queries = -(-long_clip // 128) * 128
        gradients([(slice(0, queries), slice(0, keys))], keys, queries)

    @pl.when(lead_ref[0] == 0)
    def short_clips():
        tiles = []
        for start in range(0, valid, 512):
            first = start // SHORT * SHORT // 128 * 128
            last = min(-(-(start + 512) // SHORT) * SHORT, valid)
            keys = slice(first, min(-(-last // 16) * 16, valid))
            tiles.append((slice(start, start + 512), keys))
        gradients(tiles, valid, count)


def attention_backward(lead, q, k, v, grads, weights, valid, first, pairs, earlier=()):
    count, width = q.shape
    column = pl.BlockSpec((count, 128), lambda i: (0, first + i))

    def kernel(*refs):
        attention_backward_kernel(valid, LONG, *refs[:6], *refs[6 + len(earlier) :])

    return pl.pallas_call(
        kernel,
        grid=(pairs,),
        in_specs=[pl.BlockSpec(memory_space=pltpu.SMEM)]
        + [column] * 4
        + [pl.BlockSpec((1, 2, valid, count), lambda i: (first + i, 0, 0, 0))]
        + [pl.BlockSpec(memory_space=pl.ANY)] * len(earlier),
        out_specs=(
            pl.BlockSpec((3, count, 128), lambda i: (0, 0, first + i)),
            pl.BlockSpec((8, 128), lambda i: (0, first + i)),
        ),
        out_shape=(struct((3, count, width), BF), struct((8, width), F32)),
        scratch_shapes=[pltpu.VMEM((valid, 128), F32)] * 2,
        input_output_aliases={6 + i: i for i in range(len(earlier))},
        compiler_params=params(),
        cost_estimate=cost(
            32 * count * count * 128 * pairs, 14 * count * 128 * pairs, 2 * count * count * pairs
        ),
        name="attention_backward",
    )(lead, q, k, v, grads, weights, *earlier)


def gelu_parts(value):
    upper = 0.5 + 0.5 * lax.erf(value * INV_SQRT2)
    fall = jnp.exp2(value * value * (-0.5 * LOG2_E))
    return value * upper, upper + value * fall * INV_SQRT_2PI


def normalize(hidden):
    mean = jnp.mean(hidden, axis=-1, keepdims=True)
    centred = hidden - mean
    variance = jnp.mean(centred * centred, axis=-1, keepdims=True)
    inverse = lax.rsqrt(variance + NORM_EPS)
    return centred * inverse, inverse


def norm_backward(grad_output, hat, inverse, gain):
    scaled = grad_output * gain
    return inverse * (
        scaled
        - jnp.mean(scaled, axis=-1, keepdims=True)
        - hat * jnp.mean(scaled * hat, axis=-1, keepdims=True)
    )


def column_sums(value):
    return jnp.sum(value, axis=0, keepdims=True)


def interleave(*works):
    works = list(works)
    while works:
        for work in list(works):
            try:
                next(work)
            except StopIteration:
                works.remove(work)


def middle_kernel(packed, last_rows, total_ref, frames, context, cotangent, vector, *refs):
    weight_refs = refs[: 1 if packed else 3]
    (
        result, normed_out, activated_out, down_g_out, up_g_out, first_g_out, attended_g_out,
        context_g_out, sums, up_w, down_w, out_w, raw_up, raw_out, slopes, first_hats,
        second_hats, inverses, down_total, grad_total, sems,
    ) = refs[len(weight_refs) :]
    step = pl.program_id(0)
    tiles = pl.num_programs(0) - 1
    tile, width = frames.shape
    hidden = up_w.shape[1]

    if packed:
        wire = weight_refs[0]
        copies = (
            pltpu.make_async_copy(wire.at[:, 2 * width : 2 * width + 256], raw_out, sems.at[0]),
            pltpu.make_async_copy(wire.at[:, width : 2 * width], raw_up, sems.at[1]),
            pltpu.make_async_copy(wire.at[:, 0:width], down_w, sems.at[2]),
        )
    else:
        copies = (
            pltpu.make_async_copy(weight_refs[0], out_w, sems.at[0]),
            pltpu.make_async_copy(weight_refs[1], up_w, sems.at[1]),
            pltpu.make_async_copy(weight_refs[2], down_w, sems.at[2]),
        )

    def unpack(raw, target, columns, pieces):
        rows = 24

        def pair(chip, carry):
            start = pl.multiple_of(chip * 8 * rows, 16)
            value = raw[pl.ds(start, 8 * rows), :].astype(F32)
            for j in range(pieces):
                both = jnp.concatenate(
                    [
                        value[j * rows : (j + 1) * rows],
                        value[(4 + j) * rows : (5 + j) * rows],
                    ],
                    axis=0,
                )
                to = pl.multiple_of(chip * 2 * rows, 16)
                target[pl.ds(to, 2 * rows), j * columns : (j + 1) * columns] = both.astype(BF)
            return carry

        lax.fori_loop(0, width // (2 * rows), pair, 0)

    def add_sum(row, value):
        sums[row : row + 1, :] += value

    def valid_rows(number, rows):
        position = number * tile + lax.broadcasted_iota(jnp.int32, (rows, 1), 0)
        return (position < total_ref[0]).astype(F32)

    def forward_start():
        attended = jnp.dot(context[...], out_w[...], preferred_element_type=F32) + vector[2:3, :]
        first_sum = frames[...].astype(F32) + attended
        first_hat, first_inverse = normalize(first_sum)
        normed_out[...] = (first_hat * vector[4:5, :] + vector[5:6, :]).astype(BF)
        first_hats[slot] = first_hat
        inverses[slot, 0] = jnp.broadcast_to(first_inverse, (tile, 128))
        valid = valid_rows(step, tile)
        add_sum(12, column_sums(valid * attended * attended))
        add_sum(13, column_sums(valid * first_sum * first_sum))
        add_sum(16, jnp.broadcast_to(column_sums(valid), (1, width)))
        down_total[...] = jnp.broadcast_to(vector[3:4, :], (tile, width))

    def forward_chunk(part, row):
        pre = jnp.dot(normed_out[...], up_w[:, part], preferred_element_type=F32)
        yield
        activated, slope = gelu_parts(pre + vector[pl.ds(row, 1), :])
        slopes[slot, :, part] = slope
        activated = activated.astype(BF)
        activated_out[:, part] = activated
        yield
        down_total[...] += jnp.dot(activated, down_w[part, :], preferred_element_type=F32)

    def forward_end():
        down_out = down_total[...]
        second_sum = normed_out[...].astype(F32) + down_out
        second_hat, second_inverse = normalize(second_sum)
        result[...] = (second_hat * vector[6:7, :] + vector[7:8, :]).astype(BF)
        second_hats[slot] = second_hat
        inverses[slot, 1] = jnp.broadcast_to(second_inverse, (tile, 128))
        valid = valid_rows(step, tile)
        add_sum(14, column_sums(valid * down_out * down_out))
        add_sum(15, column_sums(valid * second_sum * second_sum))

    def backward_start(rows):
        out_g = cotangent[0:rows, :].astype(F32) * valid_rows(step - 1, rows)
        second_hat = second_hats[other, 0:rows, :]
        grad_second = norm_backward(
            out_g, second_hat, inverses[other, 1, 0:rows, 0:1], vector[6:7, :]
        )
        add_sum(6, column_sums(out_g * second_hat))
        add_sum(7, column_sums(out_g))
        down_g = grad_second.astype(BF)
        down_g_out[0:rows, :] = down_g
        add_sum(3, column_sums(down_g.astype(F32)))
        grad_total[0:rows, :] = grad_second

    def backward_chunk(rows, part, row):
        grad = lax.dot_general(
            down_g_out[0:rows, :], down_w[part, :], NT, preferred_element_type=F32
        )
        yield
        up_g = (grad * slopes[other, 0:rows, part]).astype(BF)
        up_g_out[0:rows, part] = up_g
        sums[pl.ds(row, 1), :] += column_sums(up_g.astype(F32))
        yield
        grad_total[0:rows, :] += lax.dot_general(
            up_g, up_w[:, part], NT, preferred_element_type=F32
        )

    def backward_end(rows):
        grad_normed = grad_total[0:rows, :]
        first_hat = first_hats[other, 0:rows, :]
        grad_first = norm_backward(
            grad_normed, first_hat, inverses[other, 0, 0:rows, 0:1], vector[4:5, :]
        )
        add_sum(4, column_sums(grad_normed * first_hat))
        add_sum(5, column_sums(grad_normed))
        first_g_out[0:rows, :] = grad_first
        attended_g = grad_first.astype(BF)
        attended_g_out[0:rows, :] = attended_g
        add_sum(2, column_sums(attended_g.astype(F32)))
        context_g_out[0:rows, :] = lax.dot_general(
            attended_g, out_w[...], NT, preferred_element_type=F32
        ).astype(BF)

    def chunks(work, unroll):
        def body(j, carry):
            work(pl.ds(pl.multiple_of(j * width, width), width), 8 + j)
            return carry

        lax.fori_loop(0, hidden // width, body, 0, unroll=unroll)

    slot = lax.rem(step, 2)
    other = 1 - slot

    @pl.when(step == 0)
    def first_step():
        for copy in copies:
            copy.start()
        sums[...] = jnp.zeros_like(sums)
        copies[0].wait()
        if packed:
            unpack(raw_out, out_w, 256, 3)
        forward_start()
        copies[1].wait()
        if packed:
            unpack(raw_up, up_w, width, 4)
        copies[2].wait()
        chunks(lambda part, row: interleave(forward_chunk(part, row)), 2)
        forward_end()

    @pl.when((step > 0) & (step < tiles))
    def middle_step():
        forward_start()
        backward_start(tile)
        chunks(
            lambda part, row: interleave(
                backward_chunk(tile, part, row), forward_chunk(part, row)
            ),
            4,
        )
        forward_end()
        backward_end(tile)

    @pl.when(step == tiles)
    def last_step():
        backward_start(last_rows)
        chunks(lambda part, row: interleave(backward_chunk(last_rows, part, row)), 2)
        backward_end(last_rows)
        if last_rows < tile:
            for ref in (down_g_out, up_g_out, first_g_out, attended_g_out, context_g_out):
                ref[last_rows:tile, :] = jnp.zeros((tile - last_rows, ref.shape[1]), ref.dtype)


def middle(frames, context, cotangent, vector, total, weights, hidden, valid, tile=256):
    count, width = frames.shape
    packed = len(weights) == 1
    tiles = count // tile
    last_rows = min(tile, valid - (tiles - 1) * tile)

    def early(columns):
        return pl.BlockSpec((tile, columns), lambda i: (jnp.minimum(i, tiles - 1), 0))

    def late(columns):
        return pl.BlockSpec((tile, columns), lambda i: (jnp.maximum(i - 1, 0), 0))

    anywhere = pl.BlockSpec(memory_space=pl.ANY)
    low = struct((count, width), BF)
    wide = struct((count, hidden), BF)
    raw = hidden if packed else 16
    return pl.pallas_call(
        partial(middle_kernel, packed, last_rows),
        grid=(tiles + 1,),
        in_specs=[
            pl.BlockSpec(memory_space=pltpu.SMEM),
            early(width),
            early(width),
            late(width),
            pl.BlockSpec(vector.shape, lambda i: (0, 0)),
        ]
        + [anywhere] * len(weights),
        out_specs=[
            early(width), early(width), early(hidden), late(width), late(hidden), late(width),
            late(width), late(width), pl.BlockSpec((24, width), lambda i: (0, 0)),
        ],
        out_shape=[
            low, low, wide, low, wide, struct((count, width), F32), low, low,
            struct((24, width), F32),
        ],
        scratch_shapes=[
            pltpu.VMEM((width, hidden), BF),
            pltpu.VMEM((hidden, width), BF),
            pltpu.VMEM((width, width), BF),
            pltpu.VMEM((raw, width), BF),
            pltpu.VMEM((raw, 256), BF),
            pltpu.VMEM((2, tile, hidden), F32),
            pltpu.VMEM((2, tile, width), F32),
            pltpu.VMEM((2, tile, width), F32),
            pltpu.VMEM((2, 2, tile, 128), F32),
            pltpu.VMEM((tile, width), F32),
            pltpu.VMEM((tile, width), F32),
            pltpu.SemaphoreType.DMA((3,)),
        ],
        compiler_params=params(),
        cost_estimate=cost(
            2 * count * width * (4 * hidden + 2 * width),
            count * (14 * width + 4 * hidden) + 4 * width * hidden,
            2 * count * hidden,
        ),
        name="feed_forward",
    )(total, frames, context, cotangent, vector, *weights)


def split_by_core(value, rows, first, mine, theirs):
    for chip in range(value.shape[0] // (2 * rows)):
        low = value[2 * chip * rows : (2 * chip + 1) * rows, :]
        high = value[(2 * chip + 1) * rows : (2 * chip + 2) * rows, :]
        mine[chip] = jnp.where(first, low, high).astype(BF)
        theirs[chip] = jnp.where(first, high, low).astype(BF)


def down_grad_kernel(valid, rows, coords, left, right, mine, theirs):
    value = lax.dot_general(
        left[0:valid, :], right[0:valid, :], TN, preferred_element_type=F32
    )
    first = coords[3] == 0
    width = right.shape[1]
    for chip in range(mine.shape[0]):
        for j in range(4):
            lanes = slice(j * width, (j + 1) * width)
            start = 8 * chip * rows + j * rows
            low = value[start : start + rows, :]
            high = value[start + 4 * rows : start + 5 * rows, :]
            mine[chip, :, lanes] = jnp.where(first, low, high).astype(BF)
            theirs[chip, :, lanes] = jnp.where(first, high, low).astype(BF)


def down_grad(place, left, right, valid, chips=4):
    count, hidden = left.shape
    width = right.shape[1]
    rows = width // place.count
    tile = 8 * rows * chips
    out = pl.BlockSpec((chips, rows, 4 * width), lambda i, c: (i, 0, 0))
    outs = struct((place.count // 2, rows, 4 * width), BF)
    return pl.pallas_call(
        partial(down_grad_kernel, valid, rows),
        grid_spec=pltpu.PrefetchScalarGridSpec(
            num_scalar_prefetch=1,
            grid=(hidden // tile,),
            in_specs=[
                pl.BlockSpec((count, tile), lambda i, c: (0, i)),
                pl.BlockSpec((count, width), lambda i, c: (0, 0)),
            ],
            out_specs=[out, out],
        ),
        out_shape=[outs, outs],
        compiler_params=params(),
        cost_estimate=cost(2 * count * hidden * width, 2 * count * (hidden + width)),
        name="grad_down",
    )(place.coords, left, right)


def up_grad_kernel(
    valid, rows, coords, left, right, out_left, out_right, mine, theirs, lefts, rights, sems
):
    step = pl.program_id(0)
    last = pl.num_programs(0) - 1
    copies = (
        pltpu.make_async_copy(out_left, lefts, sems.at[0]),
        pltpu.make_async_copy(out_right, rights, sems.at[1]),
    )

    @pl.when(step == 0)
    def fetch():
        for copy in copies:
            copy.start()

    @pl.when(step < last)
    def up_part():
        value = lax.dot_general(
            left[0:valid, :], right[0:valid, :], TN, preferred_element_type=F32
        )
        split_by_core(value, rows, coords[3] == 0, mine, theirs)

    @pl.when(step == last)
    def out_part():
        for copy in copies:
            copy.wait()
        value = lax.dot_general(
            lefts[0:valid, :], rights[0:valid, :], TN, preferred_element_type=F32
        )
        split_by_core(value, rows, coords[3] == 0, mine, theirs)


def up_grad(place, left, right, out_left, out_right, valid):
    count, width = left.shape
    rows = width // place.count
    steps = right.shape[1] // width + 1
    anywhere = pl.BlockSpec(memory_space=pl.ANY)
    out = pl.BlockSpec((place.count // 2, rows, width), lambda i, c: (0, 0, i))
    outs = struct((place.count // 2, rows, steps * width), BF)
    return pl.pallas_call(
        partial(up_grad_kernel, valid, rows),
        grid_spec=pltpu.PrefetchScalarGridSpec(
            num_scalar_prefetch=1,
            grid=(steps,),
            in_specs=[
                pl.BlockSpec((count, width), lambda i, c: (0, 0)),
                pl.BlockSpec((count, width), lambda i, c: (0, jnp.minimum(i, steps - 2))),
                anywhere,
                anywhere,
            ],
            out_specs=[out, out],
            scratch_shapes=[
                pltpu.VMEM((count, width), BF),
                pltpu.VMEM((count, width), BF),
                pltpu.SemaphoreType.DMA((2,)),
            ],
        ),
        out_shape=[outs, outs],
        compiler_params=params(),
        cost_estimate=cost(
            2 * count * steps * width * width, 2 * (count + width) * (steps + 1) * width
        ),
        name="grad_up_and_out",
    )(place.coords, left, right, out_left, out_right)


def qkv_grad_kernel(
    valid, rows, coords, left, right, sums, more, mine, theirs, kept, sent, entries, sems
):
    step = pl.program_id(0)
    width = left.shape[1]
    first = coords[3] == 0

    def copies(start, size, number):
        lanes = pl.ds(start, size)
        return (
            pltpu.make_async_copy(kept.at[:, :, lanes], mine.at[:, :, lanes], sems.at[0, number]),
            pltpu.make_async_copy(sent.at[:, :, lanes], theirs.at[:, :, lanes], sems.at[1, number]),
        )

    for which in range(3):

        @pl.when(step == which)
        def part(which=which):
            lanes = slice(which * width, (which + 1) * width)
            value = lax.dot_general(
                left[0:valid, :], right[0, 0:valid, :], TN, preferred_element_type=F32
            )
            split_by_core(value, rows, first, kept.at[:, :, lanes], sent.at[:, :, lanes])
            for copy in copies(which * width, width, which):
                copy.start()

    @pl.when(step == 2)
    def vector_part():
        pieces = width // 128
        entries[...] = jnp.zeros_like(entries)
        for row in range(12):
            value = sums[row : row + 1, :]
            if row < 2:
                value = value + more[row : row + 1, :]
            for j in range(pieces):
                entries[row * pieces + j : row * pieces + j + 1, :] = value[
                    :, j * 128 : (j + 1) * 128
                ]
        blank = jnp.zeros((rows - 4, 128), F32)
        lanes = slice(3 * width, 3 * width + 128)
        for chip in range(kept.shape[0]):
            windows = []
            for device in (2 * chip, 2 * chip + 1):
                start = 9 * (device // 4) + 2 * (device % 4)
                windows.append(jnp.concatenate([entries[start : start + 4, :], blank], axis=0))
            kept[chip, :, lanes] = jnp.where(first, windows[0], windows[1]).astype(BF)
            sent[chip, :, lanes] = jnp.where(first, windows[1], windows[0]).astype(BF)
        for copy in copies(3 * width, 128, 3):
            copy.start()
        for which in range(3):
            for copy in copies(which * width, width, which):
                copy.wait()
        for copy in copies(3 * width, 128, 3):
            copy.wait()


def qkv_grad(place, left, right, sums, more, valid):
    count, width = left.shape
    rows = width // place.count
    wire = (place.count // 2, rows, 3 * width + 128)
    anywhere = pl.BlockSpec(memory_space=pl.ANY)
    return pl.pallas_call(
        partial(qkv_grad_kernel, valid, rows),
        grid_spec=pltpu.PrefetchScalarGridSpec(
            num_scalar_prefetch=1,
            grid=(3,),
            in_specs=[
                pl.BlockSpec((count, width), lambda i, c: (0, 0)),
                pl.BlockSpec((1, count, width), lambda i, c: (i, 0, 0)),
                pl.BlockSpec(sums.shape, lambda i, c: (0, 0)),
                pl.BlockSpec(more.shape, lambda i, c: (0, 0)),
            ],
            out_specs=[anywhere, anywhere],
            scratch_shapes=[
                pltpu.VMEM(wire, BF),
                pltpu.VMEM(wire, BF),
                pltpu.VMEM((80, 128), F32),
                pltpu.SemaphoreType.DMA((2, 4)),
            ],
        ),
        out_shape=[struct(wire, BF)] * 2,
        compiler_params=params(),
        cost_estimate=cost(6 * count * width * width, 8 * (count + width) * width),
        name="grad_qkv",
    )(place.coords, left, right, sums, more)


def frames_grad_kernel(first_g, grads, weights, out):
    value = first_g[...]
    for which in range(3):
        value = value + lax.dot_general(
            grads[which], weights[which], NT, preferred_element_type=F32
        )
    out[...] = value.astype(BF)


def frames_gradient(first_g, grads, weights, tile=256):
    count, width = first_g.shape
    row_tile = pl.BlockSpec((tile, width), lambda i: (i, 0))
    return pl.pallas_call(
        frames_grad_kernel,
        grid=(count // tile,),
        in_specs=[
            row_tile,
            pl.BlockSpec((3, tile, width), lambda i: (0, i, 0)),
            pl.BlockSpec(weights.shape, lambda i: (0, 0, 0)),
        ],
        out_specs=row_tile,
        out_shape=struct((count, width), BF),
        compiler_params=params(),
        cost_estimate=cost(6 * count * width * width, 12 * count * width + 6 * width * width),
        name="frames_gradient",
    )(first_g, grads, weights)


def adam_update(master, first, second, gradient, step_rate, decay_rate):
    first_new = BETA_FIRST * first + (1.0 - BETA_FIRST) * gradient
    second_new = BETA_SECOND * second + (1.0 - BETA_SECOND) * gradient * gradient
    first_hat = first_new / (1.0 - BETA_FIRST**STEP)
    second_hat = second_new / (1.0 - BETA_SECOND**STEP)
    updated = master - step_rate * (
        first_hat / (jnp.sqrt(second_hat) + ADAM_EPS) + decay_rate * master
    )
    return (first_new, second_new, updated, updated.astype(BF))


def segment_marks(length_row, frame_count):
    clip_ends = jnp.cumsum(length_row)
    position = jnp.arange(frame_count, dtype=jnp.int32)
    segment = jnp.sum((clip_ends[None, :] <= position[:, None]).astype(jnp.int32), axis=1)
    lane = jnp.arange(128, dtype=jnp.int32)[None, :] % 64
    same = lane == segment[:, None]
    q_mark = jnp.where(same, 1.0, 0.0).astype(BF)
    k_mark = jnp.where(same | (lane >= 8), 0.0, -MASKED).astype(BF)
    return q_mark, k_mark, clip_ends[-1:].astype(jnp.int32)


def gather_vector(place, shard):
    blank = jnp.zeros((place.count, shard.shape[0]), BF)
    own = lax.dynamic_update_slice(blank, shard[None, :], (place.index, 0))
    return place.total(own)


def after(values, things):
    return lax.optimization_barrier((values, things))[0]


def shards(n_dp, n_fsdp, *arrays):
    (
        frames, cotangent, lengths, qkv_master, out_master, up_master, down_master, vector_master,
        qkv_first, qkv_second, out_first, out_second, up_first, up_second, down_first,
        down_second, vector_first, vector_second,
    ) = arrays
    place = Place(n_dp, n_fsdp)
    frame_count, width = frames.shape
    hidden = up_master.shape[1]
    rows = out_master.shape[0]
    valid = min(frame_count, -(-MOST_VALID // 16) * 16)
    fast = n_dp == 4 and place.depth == 4 and rows == 24

    q_mark, k_mark, total = segment_marks(lengths[0], frame_count)
    if fast:
        qkv_wire, wire_low = pack(
            place, qkv_master, out_master, up_master, down_master, vector_master[None, :]
        )
        wire = lax.all_gather(wire_low, AXES, axis=0, tiled=True)
        blocks = gather_blocks(place, qkv_wire)
        queries, keys, values, vector, qkv_full = project_qkv(place, frames, blocks)
        weights = (wire,)
    else:
        vector = gather_vector(place, vector_master.astype(BF)).astype(F32).reshape(-1, width)
        qkv_full = lax.all_gather(qkv_master.astype(BF), AXES, axis=1, tiled=True)
        projected = jnp.einsum("fd,cde->cfe", frames, qkv_full, preferred_element_type=F32)
        queries = (projected[0] + vector[0]).astype(BF)
        keys = projected[1].astype(BF)
        values = (projected[2] + vector[1]).astype(BF)
        weights = tuple(
            lax.all_gather(w.astype(BF), AXES, axis=0, tiled=True)
            for w in (out_master, up_master, down_master)
        )

    context, attention = attention_forward(queries, keys, values, q_mark, k_mark, valid)
    (
        result, normed, activated, down_g, up_g, first_g, attended_g, context_g, sums,
    ) = middle(frames, context, cotangent, vector, total, weights, hidden, valid)

    def attention_part(first, pairs, start, earlier=()):
        return attention_backward(
            lengths[0, 0:1], start, keys, values, context_g, attention, valid, first, pairs, earlier
        )

    if fast:
        down_mine, theirs = down_grad(place, activated, down_g, valid)
        down_got = place.swap_core(theirs)
        up_mine, theirs = up_grad(
            place, after(normed, down_mine), up_g, context, attended_g, valid
        )
        up_got = place.swap_core(theirs)
        all_sums = lax.all_gather(sums, AXES, axis=0)
        most = Reduction(place)
        done = most.first(after(down_mine, up_mine), down_got)
        grads = attention_part(0, 2, after(queries, done))
        done = most.first(after(up_mine, grads[1]), up_got)
        qkv_g, bias_sums = attention_part(2, 4, after(queries, done), grads)
        most.parts[0], all_sums = after((most.parts[0], all_sums), bias_sums)
        done = most.second()
        mine, theirs = qkv_grad(
            place, after(frames, (done, all_sums)), qkv_g, sums, bias_sums, valid
        )
        got = place.swap_core(theirs)
        most.sums = after(most.sums, mine)
        done = most.third()
        last = Reduction(place)
        done = last.first(after(mine, done), got)
        frames_grad = frames_gradient(after(first_g, done), qkv_g, qkv_full)
        most.sums = after(most.sums, frames_grad)
        done = most.fourth(0)
        last.parts[0] = after(last.parts[0], done)
        last.second(1000)
        done = last.spread(1000)
        most.sums, all_sums = after((most.sums, all_sums), done)
        grad_most = most.result()
        grad_qkv = last.result()
        grad_down = grad_most[:, : 4 * width].reshape(rows, 4, width)
        grad_down = grad_down.transpose(1, 0, 2).reshape(4 * rows, width)
        grad_up = grad_most[:, 4 * width : 8 * width]
        grad_out = grad_most[:, 8 * width :]
        window = grad_qkv[0:4, 3 * width :].reshape(-1)
        grad_vector = lax.dynamic_slice(
            window, (32 * (place.index % 4),), (vector_master.shape[0],)
        )
        grad_qkv = grad_qkv[:, : 3 * width].reshape(rows, 3, width).transpose(1, 0, 2)
        squares = jnp.sum(all_sums[:, 12:17], axis=(0, 2))
        layer_rms = jnp.sqrt(squares[0:4] / squares[4])
    else:
        def scatter(value, dimension):
            return lax.psum_scatter(value, AXES, scatter_dimension=dimension, tiled=True)

        def product(left, right):
            return lax.dot_general(left, right, TN, preferred_element_type=F32)

        qkv_g, bias_sums = attention_part(0, HEADS // 2, queries)
        grad_down = scatter(product(activated, down_g), 0)
        grad_up = scatter(product(normed, up_g), 0)
        grad_out = scatter(product(context, attended_g), 0)
        grad_qkv = scatter(jnp.stack([product(frames, qkv_g[i]) for i in range(3)]), 1)
        frames_grad = frames_gradient(first_g, qkv_g, qkv_full)
        sums = place.total(sums + jnp.pad(bias_sums, ((0, 16), (0, 0))))
        grad_vector = lax.dynamic_slice(
            sums[0:12].reshape(-1),
            (place.index * vector_master.shape[0],),
            (vector_master.shape[0],),
        )
        layer_rms = jnp.sqrt(jnp.sum(sums[12:16], axis=1) / jnp.sum(sums[16]))

    down_new = adam_update(
        down_master, down_first, down_second, grad_down, MATRIX_RATE, WEIGHT_DECAY
    )
    up_new = adam_update(up_master, up_first, up_second, grad_up, MATRIX_RATE, WEIGHT_DECAY)
    out_new = adam_update(out_master, out_first, out_second, grad_out, MATRIX_RATE, WEIGHT_DECAY)
    qkv_new = adam_update(qkv_master, qkv_first, qkv_second, grad_qkv, MATRIX_RATE, WEIGHT_DECAY)
    vector_new = adam_update(
        vector_master, vector_first, vector_second, grad_vector, VECTOR_RATE, 0.0
    )
    return (
        (result, frames_grad, layer_rms) + qkv_new + out_new + up_new + down_new + vector_new
    )


def solution(mesh):
    rows = P(AXES, None)
    middle_rows = P(None, AXES, None)
    entries = P(AXES)
    return jax.shard_map(
        partial(shards, mesh.shape["dp"], mesh.shape["fsdp"]),
        mesh=mesh,
        in_specs=(
            rows, rows, rows, middle_rows, rows, rows, rows, entries,
            middle_rows, middle_rows, rows, rows, rows, rows, rows, rows, entries, entries,
        ),
        out_specs=(rows, rows, P())
        + (middle_rows,) * 4
        + (rows,) * 12
        + (entries,) * 4,
        check_vma=False,
    )
```

```python
from functools import partial

import jax
import jax.numpy as jnp
from jax import lax
from jax.experimental import pallas as pl
from jax.experimental.pallas import tpu as pltpu
from jax.sharding import PartitionSpec as P

HEADS = 12
STEP = 10
LONG = 780
SHORT = 150
MOST_VALID = 900

MASKED = 1e30
NORM_EPS = 1e-05
SCORE_SCALE = 0.125
BETA_FIRST = 0.9
BETA_SECOND = 0.98
ADAM_EPS = 1e-06
MATRIX_RATE = 0.05
VECTOR_RATE = 0.3
WEIGHT_DECAY = 0.01
AXES = ("dp", "fsdp")
BF = jnp.bfloat16
F32 = jnp.float32
NT = (((1,), (1,)), ((), ()))
TN = (((0,), (0,)), ((), ()))
VMEM_LIMIT = 60 * 2**20
INV_SQRT2 = 0.7071067811865476
INV_SQRT_2PI = 0.3989422804014327
LOG2_E = 1.4426950408889634


def struct(shape, dtype):
    return jax.ShapeDtypeStruct(shape, dtype)


def params(**more):
    return pltpu.CompilerParams(vmem_limit_bytes=VMEM_LIMIT, **more)


def cost(flops, bytes_accessed, transcendentals=0, times=1000):
    return pl.CostEstimate(
        flops=int(flops) * times,
        bytes_accessed=int(bytes_accessed) * times,
        transcendentals=int(transcendentals) * times,
    )


class Place:
    def __init__(self, n_dp, n_fsdp):
        self.n_dp = n_dp
        self.n_fsdp = n_fsdp
        self.depth = n_fsdp // 2
        self.count = n_dp * n_fsdp
        dp = lax.axis_index("dp")
        fsdp = lax.axis_index("fsdp")
        self.index = dp * n_fsdp + fsdp
        self.coords = jnp.stack([dp // 2, dp % 2, fsdp // 2, fsdp % 2, self.index])

    def swap_x(self, value):
        return lax.ppermute(value, "dp", [(i, i ^ 1) for i in range(self.n_dp)])

    def swap_y(self, value):
        return lax.ppermute(value, "dp", [(i, i ^ 2) for i in range(self.n_dp)])

    def swap_core(self, value):
        return lax.ppermute(value, "fsdp", [(i, i ^ 1) for i in range(self.n_fsdp)])

    def shift_z(self, value, step):
        depth = self.depth
        pairs = [(i, ((i // 2 + step) % depth) * 2 + i % 2) for i in range(self.n_fsdp)]
        return lax.ppermute(value, "fsdp", pairs)

    def swap_z(self, value, bit):
        pairs = [(i, i ^ (2 * bit)) for i in range(self.n_fsdp)]
        return lax.ppermute(value, "fsdp", pairs)

    def total(self, value):
        for axis, size in (("fsdp", self.n_fsdp), ("dp", self.n_dp)):
            bit = 1
            while bit < size:
                other = lax.ppermute(value, axis, [(i, i ^ bit) for i in range(size)])
                value = value + other
                bit *= 2
        return value


def gather_blocks(place, block):
    depth = place.depth
    column = [block] + [place.shift_z(block, step) for step in range(1, depth)]
    near = jnp.stack(column[: depth // 2])
    far = jnp.stack(column[depth // 2 :])
    near_x = place.swap_x(near)
    far_y = place.swap_y(far)
    halves = [
        [near, near_x, place.swap_y(near), place.swap_y(near_x)],
        [far, place.swap_x(far), far_y, place.swap_x(far_y)],
    ]
    own = halves[0] + halves[1]
    return own + [place.swap_core(value) for value in own]


def rounded_sum(left, right):
    return (left.astype(F32) + right.astype(F32)).astype(BF)


def first_add_kernel(coords, *refs):
    for number, out in enumerate(refs[8:]):
        out[0] = rounded_sum(refs[2 * number][0, 0], refs[2 * number + 1][0, 0])


def first_add(place, mine, got):
    half = place.depth // 2
    rows, columns = mine.shape[1:]
    shape = (2, 2, place.depth, rows, columns)
    mine = mine.reshape(shape)
    got = got.reshape(shape)
    block = (1, 1, half, rows, columns)
    specs = [
        pl.BlockSpec(block, lambda i, c: (i, c[1], 0, 0, 0)),
        pl.BlockSpec(block, lambda i, c: (i, 1 - c[1], 0, 0, 0)),
        pl.BlockSpec(block, lambda i, c: (c[0], i, 1, 0, 0)),
        pl.BlockSpec(block, lambda i, c: (1 - c[0], i, 1, 0, 0)),
    ]
    out = pl.BlockSpec((1, half, rows, columns), lambda i, c: (i, 0, 0, 0))
    return pl.pallas_call(
        first_add_kernel,
        grid_spec=pltpu.PrefetchScalarGridSpec(
            num_scalar_prefetch=1,
            grid=(2,),
            in_specs=[spec for spec in specs for _ in range(2)],
            out_specs=[out] * 4,
        ),
        out_shape=[struct((2, half, rows, columns), BF)] * 4,
        compiler_params=params(),
        cost_estimate=cost(mine.size, 6 * mine.size, times=10**6),
        name="reduce_over_core",
    )(place.coords, *([mine, got] * 4))


def second_add_kernel(widths, coords, *refs):
    outs = refs[8 * len(widths) :]
    start = 0
    for part, width in enumerate(widths):
        ins = refs[8 * part : 8 * part + 8]
        for number, out in enumerate(outs):
            out[:, :, start : start + width] = rounded_sum(
                ins[2 * number][0], ins[2 * number + 1][0]
            )
        start += width


def second_add(place, parts, times):
    half, rows = parts[0][0].shape[1:3]
    widths = [part[0].shape[3] for part in parts]
    specs = []
    ins = []
    for (keep_a, got_a, keep_b, got_b), width in zip(parts, widths):
        block = (1, half, rows, width)
        stay_a = pl.BlockSpec(block, lambda i, c: (c[0], 0, 0, 0))
        leave_a = pl.BlockSpec(block, lambda i, c: (1 - c[0], 0, 0, 0))
        stay_b = pl.BlockSpec(block, lambda i, c: (c[1], 0, 0, 0))
        leave_b = pl.BlockSpec(block, lambda i, c: (1 - c[1], 0, 0, 0))
        specs += [stay_a] * 2 + [leave_a] * 2 + [stay_b] * 2 + [leave_b] * 2
        ins += [keep_a, got_a] * 2 + [keep_b, got_b] * 2
    shape = (half, rows, sum(widths))
    return pl.pallas_call(
        partial(second_add_kernel, widths),
        grid_spec=pltpu.PrefetchScalarGridSpec(
            num_scalar_prefetch=1,
            grid=(1,),
            in_specs=specs,
            out_specs=[pl.BlockSpec(shape, lambda i, c: (0, 0, 0))] * 4,
        ),
        out_shape=[struct(shape, BF)] * 4,
        compiler_params=params(),
        cost_estimate=cost(
            4 * half * rows * shape[2], 24 * half * rows * shape[2], times=times
        ),
        name="reduce_over_first_link",
    )(place.coords, *ins)


def third_add_kernel(coords, keep_a, got_a, keep_b, got_b, keep, send):
    own = lax.rem(coords[2], 2)
    for out, which in ((keep, own), (send, 1 - own)):
        out[0] = rounded_sum(keep_a[which], got_a[which])
        out[1] = rounded_sum(keep_b[which], got_b[which])


def spread_add_kernel(coords, keep_a, got_a, keep_b, got_b, *outs):
    half = keep_a.shape[0]
    for step, out in enumerate(outs):
        target = lax.rem(coords[2] + step, 2 * half)
        inner = lax.rem(target, half)
        near = keep_a[inner].astype(F32) + got_a[inner].astype(F32)
        far = keep_b[inner].astype(F32) + got_b[inner].astype(F32)
        out[...] = jnp.where(target < half, near, far).astype(BF)


def fourth_add_kernel(coords, keep, got, keep_out, send):
    own = lax.div(coords[2], 2)
    keep_out[...] = rounded_sum(keep[own], got[own])
    send[...] = rounded_sum(keep[1 - own], got[1 - own])


def small_add(place, kernel, ins, shape, name, times=10**6, outs=2):
    inside = pl.BlockSpec(memory_space=pltpu.VMEM)
    return pl.pallas_call(
        kernel,
        in_specs=[pl.BlockSpec(memory_space=pltpu.SMEM)] + [inside] * len(ins),
        out_specs=[inside] * outs,
        out_shape=[struct(shape, BF)] * outs,
        compiler_params=params(),
        cost_estimate=cost(2 * ins[0].size, 6 * ins[0].size, times=times),
        name=name,
    )(place.coords, *ins)


class Reduction:
    def __init__(self, place):
        self.place = place
        self.parts = []

    def first(self, mine, got):
        place = self.place
        keep_a, send_a, keep_b, send_b = first_add(place, mine, got)
        self.parts.append((keep_a, place.swap_x(send_a), keep_b, place.swap_y(send_b)))
        return keep_a

    def second(self, times=10**6):
        place = self.place
        keep_a, send_a, keep_b, send_b = second_add(place, self.parts, times)
        self.sums = (keep_a, place.swap_y(send_a), keep_b, place.swap_x(send_b))
        return keep_a

    def third(self, times=10**6):
        place = self.place
        keep, send = small_add(
            place, third_add_kernel, self.sums, self.sums[0].shape, "reduce_over_second_link", times
        )
        self.sums = (keep, place.swap_z(send, 1))
        return keep

    def fourth(self, times=10**6):
        place = self.place
        keep, send = small_add(
            place, fourth_add_kernel, self.sums, self.sums[0].shape[1:], "reduce_over_z", times
        )
        self.sums = (keep, place.swap_z(send, 2))
        return keep

    def spread(self, times=10**6):
        place = self.place
        blocks = small_add(
            place, spread_add_kernel, self.sums, self.sums[0].shape[1:],
            "reduce_over_second_link", times, outs=place.depth,
        )
        self.sums = (blocks[0],) + tuple(
            place.shift_z(blocks[step], step) for step in range(1, place.depth)
        )
        return blocks[0]

    def result(self):
        total = self.sums[0].astype(F32)
        for part in self.sums[1:]:
            total = total + part.astype(F32)
        return total


def pack_kernel(coords, qkv, out, up, down, vector, qkv_wire, wire, line):
    rows, width = out.shape
    for which in range(3):
        qkv_wire[:, which * width : (which + 1) * width] = qkv[which].astype(BF)
    line[...] = jnp.zeros_like(line)
    line[0:1, 0 : vector.shape[1]] = vector[...]
    moved = pltpu.roll(line[...], 32 * (coords[4] % 4), 1)
    pieces = [moved[0:1, j * 128 : (j + 1) * 128] for j in range(4)]
    pieces.append(jnp.zeros((rows - 4, 128), F32))
    qkv_wire[:, 3 * width : 3 * width + 128] = jnp.concatenate(pieces, axis=0).astype(BF)
    wire[:, 0:width] = down[...].astype(BF)
    pieces = [up[:, j * width : (j + 1) * width] for j in range(4)]
    wire[:, width : 2 * width] = jnp.concatenate(pieces, axis=0).astype(BF)
    pieces = [out[:, j * 256 : (j + 1) * 256] for j in range(3)]
    pieces.append(jnp.zeros((rows, 256), F32))
    wire[:, 2 * width : 2 * width + 256] = jnp.concatenate(pieces, axis=0).astype(BF)


def pack(place, qkv, out, up, down, vector):
    rows, width = out.shape
    inside = pl.BlockSpec(memory_space=pltpu.VMEM)
    return pl.pallas_call(
        pack_kernel,
        in_specs=[pl.BlockSpec(memory_space=pltpu.SMEM)] + [inside] * 5,
        out_shape=(
            struct((rows, 3 * width + 128), BF),
            struct((4 * rows, 2 * width + 256), BF),
        ),
        scratch_shapes=[pltpu.VMEM((8, 512), F32)],
        compiler_params=params(),
        name="round_masters",
    )(place.coords, qkv, out, up, down, vector)


def qkv_kernel(depth, coords, frames, *refs):
    blocks = refs[:16]
    q_ref, k_ref, v_ref, vector_out, w_out, weights, windows, entries, sem = refs[16:]
    half = depth // 2
    rows = blocks[0].shape[1]
    width = weights.shape[2]
    outs = (q_ref, k_ref, v_ref)
    copy = pltpu.make_async_copy(weights, w_out, sem)

    @pl.when(pl.program_id(0) == 0)
    def assemble():
        first_core = coords[3] == 0
        for number in range(8):
            far = number // 4
            y = (coords[0] + (number // 2) % 2) % 2
            x = (coords[1] + number % 2) % 2
            for j in range(half):
                z = (coords[2] + depth - (far * half + j)) % depth
                chip = (y * 2 + x) * depth + z
                start = pl.multiple_of(chip * 2 * rows, 16)
                for which in range(3):
                    part = slice(which * width, (which + 1) * width)
                    own = blocks[number][j, :, part].astype(F32)
                    other = blocks[number + 8][j, :, part].astype(F32)
                    low = jnp.where(first_core, own, other)
                    high = jnp.where(first_core, other, own)
                    weights[which, pl.ds(start, 2 * rows), :] = jnp.concatenate(
                        [low, high], axis=0
                    ).astype(BF)
                part = slice(3 * width, 3 * width + 128)
                windows[chip * 2 + coords[3]] = blocks[number][j, :, part].astype(F32)[0:8]
                windows[chip * 2 + 1 - coords[3]] = blocks[number + 8][j, :, part].astype(F32)[0:8]
        copy.start()
        entries[...] = jnp.zeros_like(entries)
        for device in range(windows.shape[0]):
            first = 9 * (device // 4) + 2 * (device % 4)
            entries[first : first + 4, :] += windows[device, 0:4, :]
        vector_out[...] = jnp.zeros_like(vector_out)
        pieces = width // 128
        for row in range(12):
            for j in range(pieces):
                vector_out[row : row + 1, j * 128 : (j + 1) * 128] = entries[
                    row * pieces + j : row * pieces + j + 1, :
                ]

    for which in range(3):
        value = jnp.dot(frames[...], weights[which], preferred_element_type=F32)
        if which == 0:
            value = value + vector_out[0:1, :]
        if which == 2:
            value = value + vector_out[1:2, :]
        outs[which][...] = value.astype(BF)

    @pl.when(pl.program_id(0) == pl.num_programs(0) - 1)
    def finish():
        copy.wait()


def project_qkv(place, frames, blocks, tile=256):
    count, width = frames.shape
    low = struct((count, width), BF)
    row_tile = pl.BlockSpec((tile, width), lambda i: (i, 0))
    anywhere = pl.BlockSpec(memory_space=pl.ANY)
    return pl.pallas_call(
        partial(qkv_kernel, place.depth),
        grid=(count // tile,),
        in_specs=[pl.BlockSpec(memory_space=pltpu.SMEM), row_tile]
        + [pl.BlockSpec(block.shape, lambda i: (0, 0, 0)) for block in blocks],
        out_specs=[row_tile] * 3
        + [pl.BlockSpec((16, width), lambda i: (0, 0)), anywhere],
        out_shape=[low, low, low, struct((16, width), F32), struct((3, width, width), BF)],
        scratch_shapes=[
            pltpu.VMEM((3, width, width), BF),
            pltpu.VMEM((place.count, 8, 128), F32),
            pltpu.VMEM((80, 128), F32),
            pltpu.SemaphoreType.DMA,
        ],
        compiler_params=params(),
        cost_estimate=cost(6 * count * width * width, 10 * count * width, times=1),
        name="project_qkv",
    )(place.coords, frames, *blocks)


def attention_forward_kernel(q_ref, k_ref, v_ref, q_mark, k_mark, out_ref, weights_ref):
    count = q_ref.shape[0]
    valid = weights_ref.shape[2]
    values = v_ref[...].T
    lane = lax.broadcasted_iota(jnp.int32, (count, 128), 1)
    outs = []
    for head in (0, 1):
        own = (lane < 64) == (head == 0)
        keys = jnp.where(own, k_ref[...], k_mark[...])
        queries = jnp.where(own, q_ref[...] * BF(SCORE_SCALE), q_mark[...])
        scores = lax.dot_general(keys, queries, NT, preferred_element_type=F32)
        maximum = jnp.max(scores, axis=0, keepdims=True)
        raised = jnp.exp(scores - maximum)
        total = jnp.sum(raised, axis=0, keepdims=True)
        weights = (raised * (1.0 / total)).astype(BF)
        weights_ref[0, head] = weights[0:valid, :]
        rows = values[64 * head : 64 * head + 64, :]
        outs.append(jnp.dot(rows, weights, preferred_element_type=F32))
    out_ref[...] = jnp.concatenate(outs, axis=0).T.astype(BF)


def attention_forward(q, k, v, q_mark, k_mark, valid):
    count, width = q.shape
    pairs = width // 128
    column = pl.BlockSpec((count, 128), lambda i: (0, i))
    whole = pl.BlockSpec((count, 128), lambda i: (0, 0))
    return pl.pallas_call(
        attention_forward_kernel,
        grid=(pairs,),
        in_specs=[column] * 3 + [whole] * 2,
        out_specs=(column, pl.BlockSpec((1, 2, valid, count), lambda i: (i, 0, 0, 0))),
        out_shape=(struct((count, width), BF), struct((pairs, 2, valid, count), BF)),
        compiler_params=params(),
        cost_estimate=cost(
            16 * count * count * width, 8 * count * width, 12 * count * count, times=1
        ),
        name="attention_forward",
    )(q, k, v, q_mark, k_mark)


def attention_backward_kernel(
    valid, long_clip, lead_ref, q_ref, k_ref, v_ref, g_ref, weights_ref, grads_ref, sum_ref,
    dk_scr, dv_scr,
):
    count = q_ref.shape[0]

    def gradients(tiles, key_rows, query_rows):
        lane = lax.broadcasted_iota(jnp.int32, (count, 128), 1)
        keys_turned = k_ref[0:key_rows, :].T
        single = len(tiles) == 1
        if not single:
            dk_scr[...] = jnp.zeros_like(dk_scr)
            dv_scr[...] = jnp.zeros_like(dv_scr)
        masked = []
        for head in (0, 1):
            own = (lane < 64) == (head == 0)
            masked.append(
                (
                    jnp.where(own, q_ref[...] * BF(SCORE_SCALE), BF(0)),
                    jnp.where(own, g_ref[...], BF(0)),
                )
            )
        for queries, keys in tiles:
            turned = []
            dk = None
            for head in (0, 1):
                grads = masked[head][1][queries]
                weights_low = weights_ref[0, head, keys, queries]
                slopes = lax.dot_general(v_ref[keys, :], grads, NT, preferred_element_type=F32)
                weights = weights_low.astype(F32)
                inner = jnp.sum(weights * slopes, axis=0, keepdims=True)
                ds = (weights * (slopes - inner)).astype(BF)
                turned.append(
                    jnp.dot(
                        keys_turned[64 * head : 64 * head + 64, keys],
                        ds,
                        preferred_element_type=F32,
                    )
                    * SCORE_SCALE
                )
                dk_part = jnp.dot(ds, masked[head][0][queries], preferred_element_type=F32)
                dv_part = jnp.dot(weights_low, grads, preferred_element_type=F32)
                dk = dk_part if dk is None else dk + dk_part
                dv = dv_part if head == 0 else dv + dv_part
            dq = jnp.concatenate(turned, axis=0).T.astype(BF)
            grads_ref[0, queries, :] = dq
            sum_ref[0:1, :] += jnp.sum(dq.astype(F32), axis=0, keepdims=True)
            if not single:
                dk_scr[keys, :] += dk
                dv_scr[keys, :] += dv
        if not single:
            dk = dk_scr[0:key_rows, :]
            dv = dv_scr[0:key_rows, :]
        grads_ref[1, 0:key_rows, :] = dk.astype(BF)
        dv = dv.astype(BF)
        grads_ref[2, 0:key_rows, :] = dv
        sum_ref[1:2, :] += jnp.sum(dv.astype(F32), axis=0, keepdims=True)
        rest = jnp.zeros((count - key_rows, 128), BF)
        if key_rows < count:
            grads_ref[1, key_rows:count, :] = rest
            grads_ref[2, key_rows:count, :] = rest
        if query_rows < count:
            grads_ref[0, query_rows:count, :] = jnp.zeros((count - query_rows, 128), BF)

    sum_ref[...] = jnp.zeros_like(sum_ref)

    @pl.when(lead_ref[0] > 0)
    def one_long_clip():
        keys = -(-long_clip // 16) * 16
        queries = -(-long_clip // 128) * 128
        gradients([(slice(0, queries), slice(0, keys))], keys, queries)

    @pl.when(lead_ref[0] == 0)
    def short_clips():
        tiles = []
        for start in range(0, valid, 512):
            first = start // SHORT * SHORT // 128 * 128
            last = min(-(-(start + 512) // SHORT) * SHORT, valid)
            keys = slice(first, min(-(-last // 16) * 16, valid))
            tiles.append((slice(start, start + 512), keys))
        gradients(tiles, valid, count)


def attention_backward(lead, q, k, v, grads, weights, valid, first, pairs, earlier=()):
    count, width = q.shape
    column = pl.BlockSpec((count, 128), lambda i: (0, first + i))

    def kernel(*refs):
        attention_backward_kernel(valid, LONG, *refs[:6], *refs[6 + len(earlier) :])

    return pl.pallas_call(
        kernel,
        grid=(pairs,),
        in_specs=[pl.BlockSpec(memory_space=pltpu.SMEM)]
        + [column] * 4
        + [pl.BlockSpec((1, 2, valid, count), lambda i: (first + i, 0, 0, 0))]
        + [pl.BlockSpec(memory_space=pl.ANY)] * len(earlier),
        out_specs=(
            pl.BlockSpec((3, count, 128), lambda i: (0, 0, first + i)),
            pl.BlockSpec((8, 128), lambda i: (0, first + i)),
        ),
        out_shape=(struct((3, count, width), BF), struct((8, width), F32)),
        scratch_shapes=[pltpu.VMEM((valid, 128), F32)] * 2,
        input_output_aliases={6 + i: i for i in range(len(earlier))},
        compiler_params=params(),
        cost_estimate=cost(
            32 * count * count * 128 * pairs, 14 * count * 128 * pairs, 2 * count * count * pairs
        ),
        name="attention_backward",
    )(lead, q, k, v, grads, weights, *earlier)


def gelu_parts(value):
    upper = 0.5 + 0.5 * lax.erf(value * INV_SQRT2)
    fall = jnp.exp2(value * value * (-0.5 * LOG2_E))
    return value * upper, upper + value * fall * INV_SQRT_2PI


def normalize(hidden):
    mean = jnp.mean(hidden, axis=-1, keepdims=True)
    centred = hidden - mean
    variance = jnp.mean(centred * centred, axis=-1, keepdims=True)
    inverse = lax.rsqrt(variance + NORM_EPS)
    return centred * inverse, inverse


def norm_backward(grad_output, hat, inverse, gain):
    scaled = grad_output * gain
    return inverse * (
        scaled
        - jnp.mean(scaled, axis=-1, keepdims=True)
        - hat * jnp.mean(scaled * hat, axis=-1, keepdims=True)
    )


def column_sums(value):
    return jnp.sum(value, axis=0, keepdims=True)


def interleave(*works):
    works = list(works)
    while works:
        for work in list(works):
            try:
                next(work)
            except StopIteration:
                works.remove(work)


def middle_kernel(packed, last_rows, total_ref, frames, context, cotangent, vector, *refs):
    weight_refs = refs[: 1 if packed else 3]
    (
        result, normed_out, activated_out, down_g_out, up_g_out, first_g_out, attended_g_out,
        context_g_out, sums, up_w, down_w, out_w, raw_up, raw_out, slopes, first_hats,
        second_hats, inverses, down_total, grad_total, sems,
    ) = refs[len(weight_refs) :]
    step = pl.program_id(0)
    tiles = pl.num_programs(0) - 1
    tile, width = frames.shape
    hidden = up_w.shape[1]

    if packed:
        wire = weight_refs[0]
        copies = (
            pltpu.make_async_copy(wire.at[:, 2 * width : 2 * width + 256], raw_out, sems.at[0]),
            pltpu.make_async_copy(wire.at[:, width : 2 * width], raw_up, sems.at[1]),
            pltpu.make_async_copy(wire.at[:, 0:width], down_w, sems.at[2]),
        )
    else:
        copies = (
            pltpu.make_async_copy(weight_refs[0], out_w, sems.at[0]),
            pltpu.make_async_copy(weight_refs[1], up_w, sems.at[1]),
            pltpu.make_async_copy(weight_refs[2], down_w, sems.at[2]),
        )

    def unpack(raw, target, columns, pieces):
        rows = 24

        def pair(chip, carry):
            start = pl.multiple_of(chip * 8 * rows, 16)
            value = raw[pl.ds(start, 8 * rows), :].astype(F32)
            for j in range(pieces):
                both = jnp.concatenate(
                    [
                        value[j * rows : (j + 1) * rows],
                        value[(4 + j) * rows : (5 + j) * rows],
                    ],
                    axis=0,
                )
                to = pl.multiple_of(chip * 2 * rows, 16)
                target[pl.ds(to, 2 * rows), j * columns : (j + 1) * columns] = both.astype(BF)
            return carry

        lax.fori_loop(0, width // (2 * rows), pair, 0)

    def add_sum(row, value):
        sums[row : row + 1, :] += value

    def valid_rows(number, rows):
        position = number * tile + lax.broadcasted_iota(jnp.int32, (rows, 1), 0)
        return (position < total_ref[0]).astype(F32)

    def forward_start():
        attended = jnp.dot(context[...], out_w[...], preferred_element_type=F32) + vector[2:3, :]
        first_sum = frames[...].astype(F32) + attended
        first_hat, first_inverse = normalize(first_sum)
        normed_out[...] = (first_hat * vector[4:5, :] + vector[5:6, :]).astype(BF)
        first_hats[slot] = first_hat
        inverses[slot, 0] = jnp.broadcast_to(first_inverse, (tile, 128))
        valid = valid_rows(step, tile)
        add_sum(12, column_sums(valid * attended * attended))
        add_sum(13, column_sums(valid * first_sum * first_sum))
        add_sum(16, jnp.broadcast_to(column_sums(valid), (1, width)))
        down_total[...] = jnp.broadcast_to(vector[3:4, :], (tile, width))

    def forward_chunk(part, row):
        pre = jnp.dot(normed_out[...], up_w[:, part], preferred_element_type=F32)
        yield
        activated, slope = gelu_parts(pre + vector[pl.ds(row, 1), :])
        slopes[slot, :, part] = slope
        activated = activated.astype(BF)
        activated_out[:, part] = activated
        yield
        down_total[...] += jnp.dot(activated, down_w[part, :], preferred_element_type=F32)

    def forward_end():
        down_out = down_total[...]
        second_sum = normed_out[...].astype(F32) + down_out
        second_hat, second_inverse = normalize(second_sum)
        result[...] = (second_hat * vector[6:7, :] + vector[7:8, :]).astype(BF)
        second_hats[slot] = second_hat
        inverses[slot, 1] = jnp.broadcast_to(second_inverse, (tile, 128))
        valid = valid_rows(step, tile)
        add_sum(14, column_sums(valid * down_out * down_out))
        add_sum(15, column_sums(valid * second_sum * second_sum))

    def backward_start(rows):
        out_g = cotangent[0:rows, :].astype(F32) * valid_rows(step - 1, rows)
        second_hat = second_hats[other, 0:rows, :]
        grad_second = norm_backward(
            out_g, second_hat, inverses[other, 1, 0:rows, 0:1], vector[6:7, :]
        )
        add_sum(6, column_sums(out_g * second_hat))
        add_sum(7, column_sums(out_g))
        down_g = grad_second.astype(BF)
        down_g_out[0:rows, :] = down_g
        add_sum(3, column_sums(down_g.astype(F32)))
        grad_total[0:rows, :] = grad_second

    def backward_chunk(rows, part, row):
        grad = lax.dot_general(
            down_g_out[0:rows, :], down_w[part, :], NT, preferred_element_type=F32
        )
        yield
        up_g = (grad * slopes[other, 0:rows, part]).astype(BF)
        up_g_out[0:rows, part] = up_g
        sums[pl.ds(row, 1), :] += column_sums(up_g.astype(F32))
        yield
        grad_total[0:rows, :] += lax.dot_general(
            up_g, up_w[:, part], NT, preferred_element_type=F32
        )

    def backward_end(rows):
        grad_normed = grad_total[0:rows, :]
        first_hat = first_hats[other, 0:rows, :]
        grad_first = norm_backward(
            grad_normed, first_hat, inverses[other, 0, 0:rows, 0:1], vector[4:5, :]
        )
        add_sum(4, column_sums(grad_normed * first_hat))
        add_sum(5, column_sums(grad_normed))
        first_g_out[0:rows, :] = grad_first
        attended_g = grad_first.astype(BF)
        attended_g_out[0:rows, :] = attended_g
        add_sum(2, column_sums(attended_g.astype(F32)))
        context_g_out[0:rows, :] = lax.dot_general(
            attended_g, out_w[...], NT, preferred_element_type=F32
        ).astype(BF)

    def chunks(work, unroll):
        def body(j, carry):
            work(pl.ds(pl.multiple_of(j * width, width), width), 8 + j)
            return carry

        lax.fori_loop(0, hidden // width, body, 0, unroll=unroll)

    slot = lax.rem(step, 2)
    other = 1 - slot

    @pl.when(step == 0)
    def first_step():
        for copy in copies:
            copy.start()
        sums[...] = jnp.zeros_like(sums)
        copies[0].wait()
        if packed:
            unpack(raw_out, out_w, 256, 3)
        forward_start()
        copies[1].wait()
        if packed:
            unpack(raw_up, up_w, width, 4)
        copies[2].wait()
        chunks(lambda part, row: interleave(forward_chunk(part, row)), 2)
        forward_end()

    @pl.when((step > 0) & (step < tiles))
    def middle_step():
        forward_start()
        backward_start(tile)
        chunks(
            lambda part, row: interleave(
                backward_chunk(tile, part, row), forward_chunk(part, row)
            ),
            4,
        )
        forward_end()
        backward_end(tile)

    @pl.when(step == tiles)
    def last_step():
        backward_start(last_rows)
        chunks(lambda part, row: interleave(backward_chunk(last_rows, part, row)), 2)
        backward_end(last_rows)
        if last_rows < tile:
            for ref in (down_g_out, up_g_out, first_g_out, attended_g_out, context_g_out):
                ref[last_rows:tile, :] = jnp.zeros((tile - last_rows, ref.shape[1]), ref.dtype)


def middle(frames, context, cotangent, vector, total, weights, hidden, valid, tile=256):
    count, width = frames.shape
    packed = len(weights) == 1
    tiles = count // tile
    last_rows = min(tile, valid - (tiles - 1) * tile)

    def early(columns):
        return pl.BlockSpec((tile, columns), lambda i: (jnp.minimum(i, tiles - 1), 0))

    def late(columns):
        return pl.BlockSpec((tile, columns), lambda i: (jnp.maximum(i - 1, 0), 0))

    anywhere = pl.BlockSpec(memory_space=pl.ANY)
    low = struct((count, width), BF)
    wide = struct((count, hidden), BF)
    raw = hidden if packed else 16
    return pl.pallas_call(
        partial(middle_kernel, packed, last_rows),
        grid=(tiles + 1,),
        in_specs=[
            pl.BlockSpec(memory_space=pltpu.SMEM),
            early(width),
            early(width),
            late(width),
            pl.BlockSpec(vector.shape, lambda i: (0, 0)),
        ]
        + [anywhere] * len(weights),
        out_specs=[
            early(width), early(width), early(hidden), late(width), late(hidden), late(width),
            late(width), late(width), pl.BlockSpec((24, width), lambda i: (0, 0)),
        ],
        out_shape=[
            low, low, wide, low, wide, struct((count, width), F32), low, low,
            struct((24, width), F32),
        ],
        scratch_shapes=[
            pltpu.VMEM((width, hidden), BF),
            pltpu.VMEM((hidden, width), BF),
            pltpu.VMEM((width, width), BF),
            pltpu.VMEM((raw, width), BF),
            pltpu.VMEM((raw, 256), BF),
            pltpu.VMEM((2, tile, hidden), F32),
            pltpu.VMEM((2, tile, width), F32),
            pltpu.VMEM((2, tile, width), F32),
            pltpu.VMEM((2, 2, tile, 128), F32),
            pltpu.VMEM((tile, width), F32),
            pltpu.VMEM((tile, width), F32),
            pltpu.SemaphoreType.DMA((3,)),
        ],
        compiler_params=params(),
        cost_estimate=cost(
            2 * count * width * (4 * hidden + 2 * width),
            count * (14 * width + 4 * hidden) + 4 * width * hidden,
            2 * count * hidden,
        ),
        name="feed_forward",
    )(total, frames, context, cotangent, vector, *weights)


def split_by_core(value, rows, first, mine, theirs):
    for chip in range(value.shape[0] // (2 * rows)):
        low = value[2 * chip * rows : (2 * chip + 1) * rows, :]
        high = value[(2 * chip + 1) * rows : (2 * chip + 2) * rows, :]
        mine[chip] = jnp.where(first, low, high).astype(BF)
        theirs[chip] = jnp.where(first, high, low).astype(BF)


def down_grad_kernel(valid, rows, coords, left, right, mine, theirs):
    value = lax.dot_general(
        left[0:valid, :], right[0:valid, :], TN, preferred_element_type=F32
    )
    first = coords[3] == 0
    width = right.shape[1]
    for chip in range(mine.shape[0]):
        for j in range(4):
            lanes = slice(j * width, (j + 1) * width)
            start = 8 * chip * rows + j * rows
            low = value[start : start + rows, :]
            high = value[start + 4 * rows : start + 5 * rows, :]
            mine[chip, :, lanes] = jnp.where(first, low, high).astype(BF)
            theirs[chip, :, lanes] = jnp.where(first, high, low).astype(BF)


def down_grad(place, left, right, valid, chips=4):
    count, hidden = left.shape
    width = right.shape[1]
    rows = width // place.count
    tile = 8 * rows * chips
    out = pl.BlockSpec((chips, rows, 4 * width), lambda i, c: (i, 0, 0))
    outs = struct((place.count // 2, rows, 4 * width), BF)
    return pl.pallas_call(
        partial(down_grad_kernel, valid, rows),
        grid_spec=pltpu.PrefetchScalarGridSpec(
            num_scalar_prefetch=1,
            grid=(hidden // tile,),
            in_specs=[
                pl.BlockSpec((count, tile), lambda i, c: (0, i)),
                pl.BlockSpec((count, width), lambda i, c: (0, 0)),
            ],
            out_specs=[out, out],
        ),
        out_shape=[outs, outs],
        compiler_params=params(),
        cost_estimate=cost(2 * count * hidden * width, 2 * count * (hidden + width)),
        name="grad_down",
    )(place.coords, left, right)


def up_grad_kernel(
    valid, rows, coords, left, right, out_left, out_right, mine, theirs, lefts, rights, sems
):
    step = pl.program_id(0)
    last = pl.num_programs(0) - 1
    copies = (
        pltpu.make_async_copy(out_left, lefts, sems.at[0]),
        pltpu.make_async_copy(out_right, rights, sems.at[1]),
    )

    @pl.when(step == 0)
    def fetch():
        for copy in copies:
            copy.start()

    @pl.when(step < last)
    def up_part():
        value = lax.dot_general(
            left[0:valid, :], right[0:valid, :], TN, preferred_element_type=F32
        )
        split_by_core(value, rows, coords[3] == 0, mine, theirs)

    @pl.when(step == last)
    def out_part():
        for copy in copies:
            copy.wait()
        value = lax.dot_general(
            lefts[0:valid, :], rights[0:valid, :], TN, preferred_element_type=F32
        )
        split_by_core(value, rows, coords[3] == 0, mine, theirs)


def up_grad(place, left, right, out_left, out_right, valid):
    count, width = left.shape
    rows = width // place.count
    steps = right.shape[1] // width + 1
    anywhere = pl.BlockSpec(memory_space=pl.ANY)
    out = pl.BlockSpec((place.count // 2, rows, width), lambda i, c: (0, 0, i))
    outs = struct((place.count // 2, rows, steps * width), BF)
    return pl.pallas_call(
        partial(up_grad_kernel, valid, rows),
        grid_spec=pltpu.PrefetchScalarGridSpec(
            num_scalar_prefetch=1,
            grid=(steps,),
            in_specs=[
                pl.BlockSpec((count, width), lambda i, c: (0, 0)),
                pl.BlockSpec((count, width), lambda i, c: (0, jnp.minimum(i, steps - 2))),
                anywhere,
                anywhere,
            ],
            out_specs=[out, out],
            scratch_shapes=[
                pltpu.VMEM((count, width), BF),
                pltpu.VMEM((count, width), BF),
                pltpu.SemaphoreType.DMA((2,)),
            ],
        ),
        out_shape=[outs, outs],
        compiler_params=params(),
        cost_estimate=cost(
            2 * count * steps * width * width, 2 * (count + width) * (steps + 1) * width
        ),
        name="grad_up_and_out",
    )(place.coords, left, right, out_left, out_right)


def qkv_grad_kernel(
    valid, rows, coords, left, right, sums, more, mine, theirs, kept, sent, entries, sems
):
    step = pl.program_id(0)
    width = left.shape[1]
    first = coords[3] == 0

    def copies(start, size, number):
        lanes = pl.ds(start, size)
        return (
            pltpu.make_async_copy(kept.at[:, :, lanes], mine.at[:, :, lanes], sems.at[0, number]),
            pltpu.make_async_copy(sent.at[:, :, lanes], theirs.at[:, :, lanes], sems.at[1, number]),
        )

    for which in range(3):

        @pl.when(step == which)
        def part(which=which):
            lanes = slice(which * width, (which + 1) * width)
            value = lax.dot_general(
                left[0:valid, :], right[0, 0:valid, :], TN, preferred_element_type=F32
            )
            split_by_core(value, rows, first, kept.at[:, :, lanes], sent.at[:, :, lanes])
            for copy in copies(which * width, width, which):
                copy.start()

    @pl.when(step == 2)
    def vector_part():
        pieces = width // 128
        entries[...] = jnp.zeros_like(entries)
        for row in range(12):
            value = sums[row : row + 1, :]
            if row < 2:
                value = value + more[row : row + 1, :]
            for j in range(pieces):
                entries[row * pieces + j : row * pieces + j + 1, :] = value[
                    :, j * 128 : (j + 1) * 128
                ]
        blank = jnp.zeros((rows - 4, 128), F32)
        lanes = slice(3 * width, 3 * width + 128)
        for chip in range(kept.shape[0]):
            windows = []
            for device in (2 * chip, 2 * chip + 1):
                start = 9 * (device // 4) + 2 * (device % 4)
                windows.append(jnp.concatenate([entries[start : start + 4, :], blank], axis=0))
            kept[chip, :, lanes] = jnp.where(first, windows[0], windows[1]).astype(BF)
            sent[chip, :, lanes] = jnp.where(first, windows[1], windows[0]).astype(BF)
        for copy in copies(3 * width, 128, 3):
            copy.start()
        for which in range(3):
            for copy in copies(which * width, width, which):
                copy.wait()
        for copy in copies(3 * width, 128, 3):
            copy.wait()


def qkv_grad(place, left, right, sums, more, valid):
    count, width = left.shape
    rows = width // place.count
    wire = (place.count // 2, rows, 3 * width + 128)
    anywhere = pl.BlockSpec(memory_space=pl.ANY)
    return pl.pallas_call(
        partial(qkv_grad_kernel, valid, rows),
        grid_spec=pltpu.PrefetchScalarGridSpec(
            num_scalar_prefetch=1,
            grid=(3,),
            in_specs=[
                pl.BlockSpec((count, width), lambda i, c: (0, 0)),
                pl.BlockSpec((1, count, width), lambda i, c: (i, 0, 0)),
                pl.BlockSpec(sums.shape, lambda i, c: (0, 0)),
                pl.BlockSpec(more.shape, lambda i, c: (0, 0)),
            ],
            out_specs=[anywhere, anywhere],
            scratch_shapes=[
                pltpu.VMEM(wire, BF),
                pltpu.VMEM(wire, BF),
                pltpu.VMEM((80, 128), F32),
                pltpu.SemaphoreType.DMA((2, 4)),
            ],
        ),
        out_shape=[struct(wire, BF)] * 2,
        compiler_params=params(),
        cost_estimate=cost(6 * count * width * width, 8 * (count + width) * width),
        name="grad_qkv",
    )(place.coords, left, right, sums, more)


def frames_grad_kernel(first_g, grads, weights, out):
    value = first_g[...]
    for which in range(3):
        value = value + lax.dot_general(
            grads[which], weights[which], NT, preferred_element_type=F32
        )
    out[...] = value.astype(BF)


def frames_gradient(first_g, grads, weights, tile=256):
    count, width = first_g.shape
    row_tile = pl.BlockSpec((tile, width), lambda i: (i, 0))
    return pl.pallas_call(
        frames_grad_kernel,
        grid=(count // tile,),
        in_specs=[
            row_tile,
            pl.BlockSpec((3, tile, width), lambda i: (0, i, 0)),
            pl.BlockSpec(weights.shape, lambda i: (0, 0, 0)),
        ],
        out_specs=row_tile,
        out_shape=struct((count, width), BF),
        compiler_params=params(),
        cost_estimate=cost(6 * count * width * width, 12 * count * width + 6 * width * width),
        name="frames_gradient",
    )(first_g, grads, weights)


def adam_update(master, first, second, gradient, step_rate, decay_rate):
    first_new = BETA_FIRST * first + (1.0 - BETA_FIRST) * gradient
    second_new = BETA_SECOND * second + (1.0 - BETA_SECOND) * gradient * gradient
    first_hat = first_new / (1.0 - BETA_FIRST**STEP)
    second_hat = second_new / (1.0 - BETA_SECOND**STEP)
    updated = master - step_rate * (
        first_hat / (jnp.sqrt(second_hat) + ADAM_EPS) + decay_rate * master
    )
    return (first_new, second_new, updated, updated.astype(BF))


def segment_marks(length_row, frame_count):
    clip_ends = jnp.cumsum(length_row)
    position = jnp.arange(frame_count, dtype=jnp.int32)
    segment = jnp.sum((clip_ends[None, :] <= position[:, None]).astype(jnp.int32), axis=1)
    lane = jnp.arange(128, dtype=jnp.int32)[None, :] % 64
    same = lane == segment[:, None]
    q_mark = jnp.where(same, 1.0, 0.0).astype(BF)
    k_mark = jnp.where(same | (lane >= 8), 0.0, -MASKED).astype(BF)
    return q_mark, k_mark, clip_ends[-1:].astype(jnp.int32)


def gather_vector(place, shard):
    blank = jnp.zeros((place.count, shard.shape[0]), BF)
    own = lax.dynamic_update_slice(blank, shard[None, :], (place.index, 0))
    return place.total(own)


def after(values, things):
    return lax.optimization_barrier((values, things))[0]


def shards(n_dp, n_fsdp, *arrays):
    (
        frames, cotangent, lengths, qkv_master, out_master, up_master, down_master, vector_master,
        qkv_first, qkv_second, out_first, out_second, up_first, up_second, down_first,
        down_second, vector_first, vector_second,
    ) = arrays
    place = Place(n_dp, n_fsdp)
    frame_count, width = frames.shape
    hidden = up_master.shape[1]
    rows = out_master.shape[0]
    valid = min(frame_count, -(-MOST_VALID // 16) * 16)
    fast = n_dp == 4 and place.depth == 4 and rows == 24

    q_mark, k_mark, total = segment_marks(lengths[0], frame_count)
    if fast:
        qkv_wire, wire_low = pack(
            place, qkv_master, out_master, up_master, down_master, vector_master[None, :]
        )
        wire = lax.all_gather(wire_low, AXES, axis=0, tiled=True)
        blocks = gather_blocks(place, qkv_wire)
        queries, keys, values, vector, qkv_full = project_qkv(place, frames, blocks)
        weights = (wire,)
    else:
        vector = gather_vector(place, vector_master.astype(BF)).astype(F32).reshape(-1, width)
        qkv_full = lax.all_gather(qkv_master.astype(BF), AXES, axis=1, tiled=True)
        projected = jnp.einsum("fd,cde->cfe", frames, qkv_full, preferred_element_type=F32)
        queries = (projected[0] + vector[0]).astype(BF)
        keys = projected[1].astype(BF)
        values = (projected[2] + vector[1]).astype(BF)
        weights = tuple(
            lax.all_gather(w.astype(BF), AXES, axis=0, tiled=True)
            for w in (out_master, up_master, down_master)
        )

    context, attention = attention_forward(queries, keys, values, q_mark, k_mark, valid)
    (
        result, normed, activated, down_g, up_g, first_g, attended_g, context_g, sums,
    ) = middle(frames, context, cotangent, vector, total, weights, hidden, valid)

    def attention_part(first, pairs, start, earlier=()):
        return attention_backward(
            lengths[0, 0:1], start, keys, values, context_g, attention, valid, first, pairs, earlier
        )

    if fast:
        down_mine, theirs = down_grad(place, activated, down_g, valid)
        down_got = place.swap_core(theirs)
        up_mine, theirs = up_grad(
            place, after(normed, down_mine), up_g, context, attended_g, valid
        )
        up_got = place.swap_core(theirs)
        all_sums = lax.all_gather(sums, AXES, axis=0)
        most = Reduction(place)
        done = most.first(after(down_mine, up_mine), down_got)
        grads = attention_part(0, 2, after(queries, done))
        done = most.first(after(up_mine, grads[1]), up_got)
        qkv_g, bias_sums = attention_part(2, 4, after(queries, done), grads)
        most.parts[0], all_sums = after((most.parts[0], all_sums), bias_sums)
        done = most.second()
        mine, theirs = qkv_grad(
            place, after(frames, (done, all_sums)), qkv_g, sums, bias_sums, valid
        )
        got = place.swap_core(theirs)
        squares = jnp.sum(after(all_sums, mine)[:, 12:17], axis=(0, 2))
        layer_rms = jnp.sqrt(squares[0:4] / squares[4])
        most.sums = after(most.sums, (mine, layer_rms))
        done = most.third()
        last = Reduction(place)
        done = last.first(after(mine, done), got)
        frames_grad = frames_gradient(after(first_g, done), qkv_g, qkv_full)
        most.sums = after(most.sums, frames_grad)
        done = most.fourth(0)
        last.parts[0] = after(last.parts[0], done)
        last.second(1000)
        done = last.spread(1000)
        most.sums = after(most.sums, done)
        grad_most = most.result()
        grad_qkv = last.result()
        grad_down = grad_most[:, : 4 * width].reshape(rows, 4, width)
        grad_down = grad_down.transpose(1, 0, 2).reshape(4 * rows, width)
        grad_up = grad_most[:, 4 * width : 8 * width]
        grad_out = grad_most[:, 8 * width :]
        window = grad_qkv[0:4, 3 * width :].reshape(-1)
        grad_vector = lax.dynamic_slice(
            window, (32 * (place.index % 4),), (vector_master.shape[0],)
        )
        grad_qkv = grad_qkv[:, : 3 * width].reshape(rows, 3, width).transpose(1, 0, 2)
    else:
        def scatter(value, dimension):
            return lax.psum_scatter(value, AXES, scatter_dimension=dimension, tiled=True)

        def product(left, right):
            return lax.dot_general(left, right, TN, preferred_element_type=F32)

        qkv_g, bias_sums = attention_part(0, HEADS // 2, queries)
        grad_down = scatter(product(activated, down_g), 0)
        grad_up = scatter(product(normed, up_g), 0)
        grad_out = scatter(product(context, attended_g), 0)
        grad_qkv = scatter(jnp.stack([product(frames, qkv_g[i]) for i in range(3)]), 1)
        frames_grad = frames_gradient(first_g, qkv_g, qkv_full)
        sums = place.total(sums + jnp.pad(bias_sums, ((0, 16), (0, 0))))
        grad_vector = lax.dynamic_slice(
            sums[0:12].reshape(-1),
            (place.index * vector_master.shape[0],),
            (vector_master.shape[0],),
        )
        layer_rms = jnp.sqrt(jnp.sum(sums[12:16], axis=1) / jnp.sum(sums[16]))

    down_new = adam_update(
        down_master, down_first, down_second, grad_down, MATRIX_RATE, WEIGHT_DECAY
    )
    up_new = adam_update(up_master, up_first, up_second, grad_up, MATRIX_RATE, WEIGHT_DECAY)
    out_new = adam_update(out_master, out_first, out_second, grad_out, MATRIX_RATE, WEIGHT_DECAY)
    qkv_new = adam_update(qkv_master, qkv_first, qkv_second, grad_qkv, MATRIX_RATE, WEIGHT_DECAY)
    vector_new = adam_update(
        vector_master, vector_first, vector_second, grad_vector, VECTOR_RATE, 0.0
    )
    return (
        (result, frames_grad, layer_rms) + qkv_new + out_new + up_new + down_new + vector_new
    )


def solution(mesh):
    rows = P(AXES, None)
    middle_rows = P(None, AXES, None)
    entries = P(AXES)
    return jax.shard_map(
        partial(shards, mesh.shape["dp"], mesh.shape["fsdp"]),
        mesh=mesh,
        in_specs=(
            rows, rows, rows, middle_rows, rows, rows, rows, entries,
            middle_rows, middle_rows, rows, rows, rows, rows, rows, rows, entries, entries,
        ),
        out_specs=(rows, rows, P())
        + (middle_rows,) * 4
        + (rows,) * 12
        + (entries,) * 4,
        check_vma=False,
    )
```

```python
from functools import partial

import jax
import jax.numpy as jnp
from jax import lax
from jax.experimental import pallas as pl
from jax.experimental.pallas import tpu as pltpu
from jax.sharding import PartitionSpec as P

HEADS = 12
STEP = 10
LONG = 780
SHORT = 150
MOST_VALID = 900

MASKED = 1e30
NORM_EPS = 1e-05
SCORE_SCALE = 0.125
BETA_FIRST = 0.9
BETA_SECOND = 0.98
ADAM_EPS = 1e-06
MATRIX_RATE = 0.05
VECTOR_RATE = 0.3
WEIGHT_DECAY = 0.01
AXES = ("dp", "fsdp")
BF = jnp.bfloat16
F32 = jnp.float32
NT = (((1,), (1,)), ((), ()))
TN = (((0,), (0,)), ((), ()))
VMEM_LIMIT = 60 * 2**20
INV_SQRT2 = 0.7071067811865476
INV_SQRT_2PI = 0.3989422804014327
LOG2_E = 1.4426950408889634


def struct(shape, dtype):
    return jax.ShapeDtypeStruct(shape, dtype)


def params(**more):
    return pltpu.CompilerParams(vmem_limit_bytes=VMEM_LIMIT, **more)


def cost(flops, bytes_accessed, transcendentals=0, times=1000):
    return pl.CostEstimate(
        flops=int(flops) * times,
        bytes_accessed=int(bytes_accessed) * times,
        transcendentals=int(transcendentals) * times,
    )


class Place:
    def __init__(self, n_dp, n_fsdp):
        self.n_dp = n_dp
        self.n_fsdp = n_fsdp
        self.depth = n_fsdp // 2
        self.count = n_dp * n_fsdp
        dp = lax.axis_index("dp")
        fsdp = lax.axis_index("fsdp")
        self.index = dp * n_fsdp + fsdp
        self.coords = jnp.stack([dp // 2, dp % 2, fsdp // 2, fsdp % 2, self.index])

    def swap_x(self, value):
        return lax.ppermute(value, "dp", [(i, i ^ 1) for i in range(self.n_dp)])

    def swap_y(self, value):
        return lax.ppermute(value, "dp", [(i, i ^ 2) for i in range(self.n_dp)])

    def swap_core(self, value):
        return lax.ppermute(value, "fsdp", [(i, i ^ 1) for i in range(self.n_fsdp)])

    def shift_z(self, value, step):
        depth = self.depth
        pairs = [(i, ((i // 2 + step) % depth) * 2 + i % 2) for i in range(self.n_fsdp)]
        return lax.ppermute(value, "fsdp", pairs)

    def swap_z(self, value, bit):
        pairs = [(i, i ^ (2 * bit)) for i in range(self.n_fsdp)]
        return lax.ppermute(value, "fsdp", pairs)

    def total(self, value):
        for axis, size in (("fsdp", self.n_fsdp), ("dp", self.n_dp)):
            bit = 1
            while bit < size:
                other = lax.ppermute(value, axis, [(i, i ^ bit) for i in range(size)])
                value = value + other
                bit *= 2
        return value


def gather_blocks(place, block):
    depth = place.depth
    column = [block] + [place.shift_z(block, step) for step in range(1, depth)]
    near = jnp.stack(column[: depth // 2])
    far = jnp.stack(column[depth // 2 :])
    near_x = place.swap_x(near)
    far_y = place.swap_y(far)
    halves = [
        [near, near_x, place.swap_y(near), place.swap_y(near_x)],
        [far, place.swap_x(far), far_y, place.swap_x(far_y)],
    ]
    own = halves[0] + halves[1]
    return own + [place.swap_core(value) for value in own]


def rounded_sum(left, right):
    return (left.astype(F32) + right.astype(F32)).astype(BF)


def first_add_kernel(coords, *refs):
    for number, out in enumerate(refs[8:]):
        out[0] = rounded_sum(refs[2 * number][0, 0], refs[2 * number + 1][0, 0])


def first_add(place, mine, got):
    half = place.depth // 2
    rows, columns = mine.shape[1:]
    shape = (2, 2, place.depth, rows, columns)
    mine = mine.reshape(shape)
    got = got.reshape(shape)
    block = (1, 1, half, rows, columns)
    specs = [
        pl.BlockSpec(block, lambda i, c: (i, c[1], 0, 0, 0)),
        pl.BlockSpec(block, lambda i, c: (i, 1 - c[1], 0, 0, 0)),
        pl.BlockSpec(block, lambda i, c: (c[0], i, 1, 0, 0)),
        pl.BlockSpec(block, lambda i, c: (1 - c[0], i, 1, 0, 0)),
    ]
    out = pl.BlockSpec((1, half, rows, columns), lambda i, c: (i, 0, 0, 0))
    return pl.pallas_call(
        first_add_kernel,
        grid_spec=pltpu.PrefetchScalarGridSpec(
            num_scalar_prefetch=1,
            grid=(2,),
            in_specs=[spec for spec in specs for _ in range(2)],
            out_specs=[out] * 4,
        ),
        out_shape=[struct((2, half, rows, columns), BF)] * 4,
        compiler_params=params(),
        cost_estimate=cost(mine.size, 6 * mine.size, times=10**6),
        name="reduce_over_core",
    )(place.coords, *([mine, got] * 4))


def second_add_kernel(widths, coords, *refs):
    outs = refs[8 * len(widths) :]
    start = 0
    for part, width in enumerate(widths):
        ins = refs[8 * part : 8 * part + 8]
        for number, out in enumerate(outs):
            out[:, :, start : start + width] = rounded_sum(
                ins[2 * number][0], ins[2 * number + 1][0]
            )
        start += width


def second_add(place, parts, times):
    half, rows = parts[0][0].shape[1:3]
    widths = [part[0].shape[3] for part in parts]
    specs = []
    ins = []
    for (keep_a, got_a, keep_b, got_b), width in zip(parts, widths):
        block = (1, half, rows, width)
        stay_a = pl.BlockSpec(block, lambda i, c: (c[0], 0, 0, 0))
        leave_a = pl.BlockSpec(block, lambda i, c: (1 - c[0], 0, 0, 0))
        stay_b = pl.BlockSpec(block, lambda i, c: (c[1], 0, 0, 0))
        leave_b = pl.BlockSpec(block, lambda i, c: (1 - c[1], 0, 0, 0))
        specs += [stay_a] * 2 + [leave_a] * 2 + [stay_b] * 2 + [leave_b] * 2
        ins += [keep_a, got_a] * 2 + [keep_b, got_b] * 2
    shape = (half, rows, sum(widths))
    return pl.pallas_call(
        partial(second_add_kernel, widths),
        grid_spec=pltpu.PrefetchScalarGridSpec(
            num_scalar_prefetch=1,
            grid=(1,),
            in_specs=specs,
            out_specs=[pl.BlockSpec(shape, lambda i, c: (0, 0, 0))] * 4,
        ),
        out_shape=[struct(shape, BF)] * 4,
        compiler_params=params(),
        cost_estimate=cost(
            4 * half * rows * shape[2], 24 * half * rows * shape[2], times=times
        ),
        name="reduce_over_first_link",
    )(place.coords, *ins)


def third_add_kernel(coords, keep_a, got_a, keep_b, got_b, keep, send):
    own = lax.rem(coords[2], 2)
    for out, which in ((keep, own), (send, 1 - own)):
        out[0] = rounded_sum(keep_a[which], got_a[which])
        out[1] = rounded_sum(keep_b[which], got_b[which])


def spread_add_kernel(coords, keep_a, got_a, keep_b, got_b, *outs):
    half = keep_a.shape[0]
    for step, out in enumerate(outs):
        target = lax.rem(coords[2] + step, 2 * half)
        inner = lax.rem(target, half)
        near = keep_a[inner].astype(F32) + got_a[inner].astype(F32)
        far = keep_b[inner].astype(F32) + got_b[inner].astype(F32)
        out[...] = jnp.where(target < half, near, far).astype(BF)


def fourth_add_kernel(coords, keep, got, keep_out, send):
    own = lax.div(coords[2], 2)
    keep_out[...] = rounded_sum(keep[own], got[own])
    send[...] = rounded_sum(keep[1 - own], got[1 - own])


def small_add(place, kernel, ins, shape, name, times=10**6, outs=2):
    inside = pl.BlockSpec(memory_space=pltpu.VMEM)
    return pl.pallas_call(
        kernel,
        in_specs=[pl.BlockSpec(memory_space=pltpu.SMEM)] + [inside] * len(ins),
        out_specs=[inside] * outs,
        out_shape=[struct(shape, BF)] * outs,
        compiler_params=params(),
        cost_estimate=cost(2 * ins[0].size, 6 * ins[0].size, times=times),
        name=name,
    )(place.coords, *ins)


class Reduction:
    def __init__(self, place):
        self.place = place
        self.parts = []

    def first(self, mine, got):
        place = self.place
        keep_a, send_a, keep_b, send_b = first_add(place, mine, got)
        self.parts.append((keep_a, place.swap_x(send_a), keep_b, place.swap_y(send_b)))
        return keep_a

    def second(self, times=10**6):
        place = self.place
        keep_a, send_a, keep_b, send_b = second_add(place, self.parts, times)
        self.sums = (keep_a, place.swap_y(send_a), keep_b, place.swap_x(send_b))
        return keep_a

    def third(self, times=10**6):
        place = self.place
        keep, send = small_add(
            place, third_add_kernel, self.sums, self.sums[0].shape, "reduce_over_second_link", times
        )
        self.sums = (keep, place.swap_z(send, 1))
        return keep

    def fourth(self, times=10**6):
        place = self.place
        keep, send = small_add(
            place, fourth_add_kernel, self.sums, self.sums[0].shape[1:], "reduce_over_z", times
        )
        self.sums = (keep, place.swap_z(send, 2))
        return keep

    def spread(self, times=10**6):
        place = self.place
        blocks = small_add(
            place, spread_add_kernel, self.sums, self.sums[0].shape[1:],
            "reduce_over_second_link", times, outs=place.depth,
        )
        self.sums = (blocks[0],) + tuple(
            place.shift_z(blocks[step], step) for step in range(1, place.depth)
        )
        return blocks[0]

    def result(self):
        total = self.sums[0].astype(F32)
        for part in self.sums[1:]:
            total = total + part.astype(F32)
        return total


def pack_kernel(coords, qkv, out, up, down, vector, qkv_wire, wire, line):
    rows, width = out.shape
    for which in range(3):
        qkv_wire[:, which * width : (which + 1) * width] = qkv[which].astype(BF)
    line[...] = jnp.zeros_like(line)
    line[0:1, 0 : vector.shape[1]] = vector[...]
    moved = pltpu.roll(line[...], 32 * (coords[4] % 4), 1)
    pieces = [moved[0:1, j * 128 : (j + 1) * 128] for j in range(4)]
    pieces.append(jnp.zeros((rows - 4, 128), F32))
    qkv_wire[:, 3 * width : 3 * width + 128] = jnp.concatenate(pieces, axis=0).astype(BF)
    wire[:, 0:width] = down[...].astype(BF)
    pieces = [up[:, j * width : (j + 1) * width] for j in range(4)]
    wire[:, width : 2 * width] = jnp.concatenate(pieces, axis=0).astype(BF)
    pieces = [out[:, j * 256 : (j + 1) * 256] for j in range(3)]
    pieces.append(jnp.zeros((rows, 256), F32))
    wire[:, 2 * width : 2 * width + 256] = jnp.concatenate(pieces, axis=0).astype(BF)


def pack(place, qkv, out, up, down, vector):
    rows, width = out.shape
    inside = pl.BlockSpec(memory_space=pltpu.VMEM)
    return pl.pallas_call(
        pack_kernel,
        in_specs=[pl.BlockSpec(memory_space=pltpu.SMEM)] + [inside] * 5,
        out_shape=(
            struct((rows, 3 * width + 128), BF),
            struct((4 * rows, 2 * width + 256), BF),
        ),
        scratch_shapes=[pltpu.VMEM((8, 512), F32)],
        compiler_params=params(),
        name="round_masters",
    )(place.coords, qkv, out, up, down, vector)


def qkv_kernel(depth, coords, frames, *refs):
    blocks = refs[:16]
    q_ref, k_ref, v_ref, vector_out, w_out, weights, windows, entries, sem = refs[16:]
    half = depth // 2
    rows = blocks[0].shape[1]
    width = weights.shape[2]
    outs = (q_ref, k_ref, v_ref)
    copy = pltpu.make_async_copy(weights, w_out, sem)

    @pl.when(pl.program_id(0) == 0)
    def assemble():
        first_core = coords[3] == 0
        for number in range(8):
            far = number // 4
            y = (coords[0] + (number // 2) % 2) % 2
            x = (coords[1] + number % 2) % 2
            for j in range(half):
                z = (coords[2] + depth - (far * half + j)) % depth
                chip = (y * 2 + x) * depth + z
                start = pl.multiple_of(chip * 2 * rows, 16)
                for which in range(3):
                    part = slice(which * width, (which + 1) * width)
                    own = blocks[number][j, :, part].astype(F32)
                    other = blocks[number + 8][j, :, part].astype(F32)
                    low = jnp.where(first_core, own, other)
                    high = jnp.where(first_core, other, own)
                    weights[which, pl.ds(start, 2 * rows), :] = jnp.concatenate(
                        [low, high], axis=0
                    ).astype(BF)
                part = slice(3 * width, 3 * width + 128)
                windows[chip * 2 + coords[3]] = blocks[number][j, :, part].astype(F32)[0:8]
                windows[chip * 2 + 1 - coords[3]] = blocks[number + 8][j, :, part].astype(F32)[0:8]
        copy.start()
        entries[...] = jnp.zeros_like(entries)
        for device in range(windows.shape[0]):
            first = 9 * (device // 4) + 2 * (device % 4)
            entries[first : first + 4, :] += windows[device, 0:4, :]
        vector_out[...] = jnp.zeros_like(vector_out)
        pieces = width // 128
        for row in range(12):
            for j in range(pieces):
                vector_out[row : row + 1, j * 128 : (j + 1) * 128] = entries[
                    row * pieces + j : row * pieces + j + 1, :
                ]

    for which in range(3):
        value = jnp.dot(frames[...], weights[which], preferred_element_type=F32)
        if which == 0:
            value = value + vector_out[0:1, :]
        if which == 2:
            value = value + vector_out[1:2, :]
        outs[which][...] = value.astype(BF)

    @pl.when(pl.program_id(0) == pl.num_programs(0) - 1)
    def finish():
        copy.wait()


def project_qkv(place, frames, blocks, tile=256):
    count, width = frames.shape
    low = struct((count, width), BF)
    row_tile = pl.BlockSpec((tile, width), lambda i: (i, 0))
    anywhere = pl.BlockSpec(memory_space=pl.ANY)
    return pl.pallas_call(
        partial(qkv_kernel, place.depth),
        grid=(count // tile,),
        in_specs=[pl.BlockSpec(memory_space=pltpu.SMEM), row_tile]
        + [pl.BlockSpec(block.shape, lambda i: (0, 0, 0)) for block in blocks],
        out_specs=[row_tile] * 3
        + [pl.BlockSpec((16, width), lambda i: (0, 0)), anywhere],
        out_shape=[low, low, low, struct((16, width), F32), struct((3, width, width), BF)],
        scratch_shapes=[
            pltpu.VMEM((3, width, width), BF),
            pltpu.VMEM((place.count, 8, 128), F32),
            pltpu.VMEM((80, 128), F32),
            pltpu.SemaphoreType.DMA,
        ],
        compiler_params=params(),
        cost_estimate=cost(6 * count * width * width, 10 * count * width, times=1),
        name="project_qkv",
    )(place.coords, frames, *blocks)


def attention_forward_kernel(q_ref, k_ref, v_ref, q_mark, k_mark, out_ref, weights_ref):
    count = q_ref.shape[0]
    valid = weights_ref.shape[2]
    values = v_ref[...].T
    lane = lax.broadcasted_iota(jnp.int32, (count, 128), 1)
    outs = []
    for head in (0, 1):
        own = (lane < 64) == (head == 0)
        keys = jnp.where(own, k_ref[...], k_mark[...])
        queries = jnp.where(own, q_ref[...] * BF(SCORE_SCALE), q_mark[...])
        scores = lax.dot_general(keys, queries, NT, preferred_element_type=F32)
        maximum = jnp.max(scores, axis=0, keepdims=True)
        raised = jnp.exp(scores - maximum)
        total = jnp.sum(raised, axis=0, keepdims=True)
        weights = (raised * (1.0 / total)).astype(BF)
        weights_ref[0, head] = weights[0:valid, :]
        rows = values[64 * head : 64 * head + 64, :]
        outs.append(jnp.dot(rows, weights, preferred_element_type=F32))
    out_ref[...] = jnp.concatenate(outs, axis=0).T.astype(BF)


def attention_forward(q, k, v, q_mark, k_mark, valid):
    count, width = q.shape
    pairs = width // 128
    column = pl.BlockSpec((count, 128), lambda i: (0, i))
    whole = pl.BlockSpec((count, 128), lambda i: (0, 0))
    return pl.pallas_call(
        attention_forward_kernel,
        grid=(pairs,),
        in_specs=[column] * 3 + [whole] * 2,
        out_specs=(column, pl.BlockSpec((1, 2, valid, count), lambda i: (i, 0, 0, 0))),
        out_shape=(struct((count, width), BF), struct((pairs, 2, valid, count), BF)),
        compiler_params=params(),
        cost_estimate=cost(
            16 * count * count * width, 8 * count * width, 12 * count * count, times=1
        ),
        name="attention_forward",
    )(q, k, v, q_mark, k_mark)


def attention_backward_kernel(
    valid, long_clip, lead_ref, q_ref, k_ref, v_ref, g_ref, weights_ref, grads_ref, sum_ref,
    dk_scr, dv_scr,
):
    count = q_ref.shape[0]

    def gradients(tiles, key_rows, query_rows):
        lane = lax.broadcasted_iota(jnp.int32, (count, 128), 1)
        keys_turned = k_ref[0:key_rows, :].T
        single = len(tiles) == 1
        if not single:
            dk_scr[...] = jnp.zeros_like(dk_scr)
            dv_scr[...] = jnp.zeros_like(dv_scr)
        masked = []
        for head in (0, 1):
            own = (lane < 64) == (head == 0)
            masked.append(
                (
                    jnp.where(own, q_ref[...] * BF(SCORE_SCALE), BF(0)),
                    jnp.where(own, g_ref[...], BF(0)),
                )
            )
        for queries, keys in tiles:
            turned = []
            dk = None
            for head in (0, 1):
                grads = masked[head][1][queries]
                weights_low = weights_ref[0, head, keys, queries]
                slopes = lax.dot_general(v_ref[keys, :], grads, NT, preferred_element_type=F32)
                weights = weights_low.astype(F32)
                inner = jnp.sum(weights * slopes, axis=0, keepdims=True)
                ds = (weights * (slopes - inner)).astype(BF)
                turned.append(
                    jnp.dot(
                        keys_turned[64 * head : 64 * head + 64, keys],
                        ds,
                        preferred_element_type=F32,
                    )
                    * SCORE_SCALE
                )
                dk_part = jnp.dot(ds, masked[head][0][queries], preferred_element_type=F32)
                dv_part = jnp.dot(weights_low, grads, preferred_element_type=F32)
                dk = dk_part if dk is None else dk + dk_part
                dv = dv_part if head == 0 else dv + dv_part
            dq = jnp.concatenate(turned, axis=0).T.astype(BF)
            grads_ref[0, queries, :] = dq
            sum_ref[0:1, :] += jnp.sum(dq.astype(F32), axis=0, keepdims=True)
            if not single:
                dk_scr[keys, :] += dk
                dv_scr[keys, :] += dv
        if not single:
            dk = dk_scr[0:key_rows, :]
            dv = dv_scr[0:key_rows, :]
        grads_ref[1, 0:key_rows, :] = dk.astype(BF)
        dv = dv.astype(BF)
        grads_ref[2, 0:key_rows, :] = dv
        sum_ref[1:2, :] += jnp.sum(dv.astype(F32), axis=0, keepdims=True)
        rest = jnp.zeros((count - key_rows, 128), BF)
        if key_rows < count:
            grads_ref[1, key_rows:count, :] = rest
            grads_ref[2, key_rows:count, :] = rest
        if query_rows < count:
            grads_ref[0, query_rows:count, :] = jnp.zeros((count - query_rows, 128), BF)

    sum_ref[...] = jnp.zeros_like(sum_ref)

    @pl.when(lead_ref[0] > 0)
    def one_long_clip():
        keys = -(-long_clip // 16) * 16
        queries = -(-long_clip // 128) * 128
        gradients([(slice(0, queries), slice(0, keys))], keys, queries)

    @pl.when(lead_ref[0] == 0)
    def short_clips():
        tiles = []
        for start in range(0, valid, 512):
            first = start // SHORT * SHORT // 128 * 128
            last = min(-(-(start + 512) // SHORT) * SHORT, valid)
            keys = slice(first, min(-(-last // 16) * 16, valid))
            tiles.append((slice(start, start + 512), keys))
        gradients(tiles, valid, count)


def attention_backward(lead, q, k, v, grads, weights, valid, first, pairs, earlier=()):
    count, width = q.shape
    column = pl.BlockSpec((count, 128), lambda i: (0, first + i))

    def kernel(*refs):
        attention_backward_kernel(valid, LONG, *refs[:6], *refs[6 + len(earlier) :])

    return pl.pallas_call(
        kernel,
        grid=(pairs,),
        in_specs=[pl.BlockSpec(memory_space=pltpu.SMEM)]
        + [column] * 4
        + [pl.BlockSpec((1, 2, valid, count), lambda i: (first + i, 0, 0, 0))]
        + [pl.BlockSpec(memory_space=pl.ANY)] * len(earlier),
        out_specs=(
            pl.BlockSpec((3, count, 128), lambda i: (0, 0, first + i)),
            pl.BlockSpec((8, 128), lambda i: (0, first + i)),
        ),
        out_shape=(struct((3, count, width), BF), struct((8, width), F32)),
        scratch_shapes=[pltpu.VMEM((valid, 128), F32)] * 2,
        input_output_aliases={6 + i: i for i in range(len(earlier))},
        compiler_params=params(),
        cost_estimate=cost(
            32 * count * count * 128 * pairs, 14 * count * 128 * pairs, 2 * count * count * pairs
        ),
        name="attention_backward",
    )(lead, q, k, v, grads, weights, *earlier)


def gelu_parts(value):
    upper = 0.5 + 0.5 * lax.erf(value * INV_SQRT2)
    fall = jnp.exp2(value * value * (-0.5 * LOG2_E))
    return value * upper, upper + value * fall * INV_SQRT_2PI


def normalize(hidden):
    mean = jnp.mean(hidden, axis=-1, keepdims=True)
    centred = hidden - mean
    variance = jnp.mean(centred * centred, axis=-1, keepdims=True)
    inverse = lax.rsqrt(variance + NORM_EPS)
    return centred * inverse, inverse


def norm_backward(grad_output, hat, inverse, gain):
    scaled = grad_output * gain
    return inverse * (
        scaled
        - jnp.mean(scaled, axis=-1, keepdims=True)
        - hat * jnp.mean(scaled * hat, axis=-1, keepdims=True)
    )


def column_sums(value):
    return jnp.sum(value, axis=0, keepdims=True)


def interleave(*works):
    works = list(works)
    while works:
        for work in list(works):
            try:
                next(work)
            except StopIteration:
                works.remove(work)


def middle_kernel(packed, last_rows, total_ref, frames, context, cotangent, vector, *refs):
    weight_refs = refs[: 1 if packed else 3]
    (
        result, normed_out, activated_out, down_g_out, up_g_out, first_g_out, attended_g_out,
        context_g_out, sums, up_w, down_w, out_w, raw_up, raw_out, slopes, first_hats,
        second_hats, inverses, down_total, grad_total, sems,
    ) = refs[len(weight_refs) :]
    step = pl.program_id(0)
    tiles = pl.num_programs(0) - 1
    tile, width = frames.shape
    hidden = up_w.shape[1]

    if packed:
        wire = weight_refs[0]
        copies = (
            pltpu.make_async_copy(wire.at[:, 2 * width : 2 * width + 256], raw_out, sems.at[0]),
            pltpu.make_async_copy(wire.at[:, width : 2 * width], raw_up, sems.at[1]),
            pltpu.make_async_copy(wire.at[:, 0:width], down_w, sems.at[2]),
        )
    else:
        copies = (
            pltpu.make_async_copy(weight_refs[0], out_w, sems.at[0]),
            pltpu.make_async_copy(weight_refs[1], up_w, sems.at[1]),
            pltpu.make_async_copy(weight_refs[2], down_w, sems.at[2]),
        )

    def unpack(raw, target, columns, pieces):
        rows = 24

        def pair(chip, carry):
            start = pl.multiple_of(chip * 8 * rows, 16)
            value = raw[pl.ds(start, 8 * rows), :].astype(F32)
            for j in range(pieces):
                both = jnp.concatenate(
                    [
                        value[j * rows : (j + 1) * rows],
                        value[(4 + j) * rows : (5 + j) * rows],
                    ],
                    axis=0,
                )
                to = pl.multiple_of(chip * 2 * rows, 16)
                target[pl.ds(to, 2 * rows), j * columns : (j + 1) * columns] = both.astype(BF)
            return carry

        lax.fori_loop(0, width // (2 * rows), pair, 0)

    def add_sum(row, value):
        sums[row : row + 1, :] += value

    def valid_rows(number, rows):
        position = number * tile + lax.broadcasted_iota(jnp.int32, (rows, 1), 0)
        return (position < total_ref[0]).astype(F32)

    def forward_start():
        attended = jnp.dot(context[...], out_w[...], preferred_element_type=F32) + vector[2:3, :]
        first_sum = frames[...].astype(F32) + attended
        first_hat, first_inverse = normalize(first_sum)
        normed_out[...] = (first_hat * vector[4:5, :] + vector[5:6, :]).astype(BF)
        first_hats[slot] = first_hat
        inverses[slot, 0] = jnp.broadcast_to(first_inverse, (tile, 128))
        valid = valid_rows(step, tile)
        add_sum(12, column_sums(valid * attended * attended))
        add_sum(13, column_sums(valid * first_sum * first_sum))
        add_sum(16, jnp.broadcast_to(column_sums(valid), (1, width)))
        down_total[...] = jnp.broadcast_to(vector[3:4, :], (tile, width))

    def forward_chunk(part, row):
        pre = jnp.dot(normed_out[...], up_w[:, part], preferred_element_type=F32)
        yield
        activated, slope = gelu_parts(pre + vector[pl.ds(row, 1), :])
        slopes[slot, :, part] = slope
        activated = activated.astype(BF)
        activated_out[:, part] = activated
        yield
        down_total[...] += jnp.dot(activated, down_w[part, :], preferred_element_type=F32)

    def forward_end():
        down_out = down_total[...]
        second_sum = normed_out[...].astype(F32) + down_out
        second_hat, second_inverse = normalize(second_sum)
        result[...] = (second_hat * vector[6:7, :] + vector[7:8, :]).astype(BF)
        second_hats[slot] = second_hat
        inverses[slot, 1] = jnp.broadcast_to(second_inverse, (tile, 128))
        valid = valid_rows(step, tile)
        add_sum(14, column_sums(valid * down_out * down_out))
        add_sum(15, column_sums(valid * second_sum * second_sum))

    def backward_start(rows):
        out_g = cotangent[0:rows, :].astype(F32) * valid_rows(step - 1, rows)
        second_hat = second_hats[other, 0:rows, :]
        grad_second = norm_backward(
            out_g, second_hat, inverses[other, 1, 0:rows, 0:1], vector[6:7, :]
        )
        add_sum(6, column_sums(out_g * second_hat))
        add_sum(7, column_sums(out_g))
        down_g = grad_second.astype(BF)
        down_g_out[0:rows, :] = down_g
        add_sum(3, column_sums(down_g.astype(F32)))
        grad_total[0:rows, :] = grad_second

    def backward_chunk(rows, part, row):
        grad = lax.dot_general(
            down_g_out[0:rows, :], down_w[part, :], NT, preferred_element_type=F32
        )
        yield
        up_g = (grad * slopes[other, 0:rows, part]).astype(BF)
        up_g_out[0:rows, part] = up_g
        sums[pl.ds(row, 1), :] += column_sums(up_g.astype(F32))
        yield
        grad_total[0:rows, :] += lax.dot_general(
            up_g, up_w[:, part], NT, preferred_element_type=F32
        )

    def backward_end(rows):
        grad_normed = grad_total[0:rows, :]
        first_hat = first_hats[other, 0:rows, :]
        grad_first = norm_backward(
            grad_normed, first_hat, inverses[other, 0, 0:rows, 0:1], vector[4:5, :]
        )
        add_sum(4, column_sums(grad_normed * first_hat))
        add_sum(5, column_sums(grad_normed))
        first_g_out[0:rows, :] = grad_first
        attended_g = grad_first.astype(BF)
        attended_g_out[0:rows, :] = attended_g
        add_sum(2, column_sums(attended_g.astype(F32)))
        context_g_out[0:rows, :] = lax.dot_general(
            attended_g, out_w[...], NT, preferred_element_type=F32
        ).astype(BF)

    def chunks(work, unroll):
        def body(j, carry):
            work(pl.ds(pl.multiple_of(j * width, width), width), 8 + j)
            return carry

        lax.fori_loop(0, hidden // width, body, 0, unroll=unroll)

    slot = lax.rem(step, 2)
    other = 1 - slot

    @pl.when(step == 0)
    def first_step():
        for copy in copies:
            copy.start()
        sums[...] = jnp.zeros_like(sums)
        copies[0].wait()
        if packed:
            unpack(raw_out, out_w, 256, 3)
        forward_start()
        copies[1].wait()
        if packed:
            unpack(raw_up, up_w, width, 4)
        copies[2].wait()
        chunks(lambda part, row: interleave(forward_chunk(part, row)), 2)
        forward_end()

    @pl.when((step > 0) & (step < tiles))
    def middle_step():
        forward_start()
        backward_start(tile)
        chunks(
            lambda part, row: interleave(
                backward_chunk(tile, part, row), forward_chunk(part, row)
            ),
            4,
        )
        forward_end()
        backward_end(tile)

    @pl.when(step == tiles)
    def last_step():
        backward_start(last_rows)
        chunks(lambda part, row: interleave(backward_chunk(last_rows, part, row)), 2)
        backward_end(last_rows)
        if last_rows < tile:
            for ref in (down_g_out, up_g_out, first_g_out, attended_g_out, context_g_out):
                ref[last_rows:tile, :] = jnp.zeros((tile - last_rows, ref.shape[1]), ref.dtype)


def middle(frames, context, cotangent, vector, total, weights, hidden, valid, tile=256):
    count, width = frames.shape
    packed = len(weights) == 1
    tiles = count // tile
    last_rows = min(tile, valid - (tiles - 1) * tile)

    def early(columns):
        return pl.BlockSpec((tile, columns), lambda i: (jnp.minimum(i, tiles - 1), 0))

    def late(columns):
        return pl.BlockSpec((tile, columns), lambda i: (jnp.maximum(i - 1, 0), 0))

    anywhere = pl.BlockSpec(memory_space=pl.ANY)
    low = struct((count, width), BF)
    wide = struct((count, hidden), BF)
    raw = hidden if packed else 16
    return pl.pallas_call(
        partial(middle_kernel, packed, last_rows),
        grid=(tiles + 1,),
        in_specs=[
            pl.BlockSpec(memory_space=pltpu.SMEM),
            early(width),
            early(width),
            late(width),
            pl.BlockSpec(vector.shape, lambda i: (0, 0)),
        ]
        + [anywhere] * len(weights),
        out_specs=[
            early(width), early(width), early(hidden), late(width), late(hidden), late(width),
            late(width), late(width), pl.BlockSpec((24, width), lambda i: (0, 0)),
        ],
        out_shape=[
            low, low, wide, low, wide, struct((count, width), F32), low, low,
            struct((24, width), F32),
        ],
        scratch_shapes=[
            pltpu.VMEM((width, hidden), BF),
            pltpu.VMEM((hidden, width), BF),
            pltpu.VMEM((width, width), BF),
            pltpu.VMEM((raw, width), BF),
            pltpu.VMEM((raw, 256), BF),
            pltpu.VMEM((2, tile, hidden), F32),
            pltpu.VMEM((2, tile, width), F32),
            pltpu.VMEM((2, tile, width), F32),
            pltpu.VMEM((2, 2, tile, 128), F32),
            pltpu.VMEM((tile, width), F32),
            pltpu.VMEM((tile, width), F32),
            pltpu.SemaphoreType.DMA((3,)),
        ],
        compiler_params=params(),
        cost_estimate=cost(
            2 * count * width * (4 * hidden + 2 * width),
            count * (14 * width + 4 * hidden) + 4 * width * hidden,
            2 * count * hidden,
        ),
        name="feed_forward",
    )(total, frames, context, cotangent, vector, *weights)


def split_by_core(value, rows, first, mine, theirs):
    for chip in range(value.shape[0] // (2 * rows)):
        low = value[2 * chip * rows : (2 * chip + 1) * rows, :]
        high = value[(2 * chip + 1) * rows : (2 * chip + 2) * rows, :]
        mine[chip] = jnp.where(first, low, high).astype(BF)
        theirs[chip] = jnp.where(first, high, low).astype(BF)


def down_grad_kernel(valid, rows, coords, left, right, mine, theirs):
    value = lax.dot_general(
        left[0:valid, :], right[0:valid, :], TN, preferred_element_type=F32
    )
    first = coords[3] == 0
    width = right.shape[1]
    for chip in range(mine.shape[0]):
        for j in range(4):
            lanes = slice(j * width, (j + 1) * width)
            start = 8 * chip * rows + j * rows
            low = value[start : start + rows, :]
            high = value[start + 4 * rows : start + 5 * rows, :]
            mine[chip, :, lanes] = jnp.where(first, low, high).astype(BF)
            theirs[chip, :, lanes] = jnp.where(first, high, low).astype(BF)


def down_grad(place, left, right, valid, chips=4):
    count, hidden = left.shape
    width = right.shape[1]
    rows = width // place.count
    tile = 8 * rows * chips
    out = pl.BlockSpec((chips, rows, 4 * width), lambda i, c: (i, 0, 0))
    outs = struct((place.count // 2, rows, 4 * width), BF)
    return pl.pallas_call(
        partial(down_grad_kernel, valid, rows),
        grid_spec=pltpu.PrefetchScalarGridSpec(
            num_scalar_prefetch=1,
            grid=(hidden // tile,),
            in_specs=[
                pl.BlockSpec((count, tile), lambda i, c: (0, i)),
                pl.BlockSpec((count, width), lambda i, c: (0, 0)),
            ],
            out_specs=[out, out],
        ),
        out_shape=[outs, outs],
        compiler_params=params(),
        cost_estimate=cost(2 * count * hidden * width, 2 * count * (hidden + width)),
        name="grad_down",
    )(place.coords, left, right)


def up_grad_kernel(
    valid, rows, coords, left, right, out_left, out_right, mine, theirs, lefts, rights, sems
):
    step = pl.program_id(0)
    last = pl.num_programs(0) - 1
    copies = (
        pltpu.make_async_copy(out_left, lefts, sems.at[0]),
        pltpu.make_async_copy(out_right, rights, sems.at[1]),
    )

    @pl.when(step == 0)
    def fetch():
        for copy in copies:
            copy.start()

    @pl.when(step < last)
    def up_part():
        value = lax.dot_general(
            left[0:valid, :], right[0:valid, :], TN, preferred_element_type=F32
        )
        split_by_core(value, rows, coords[3] == 0, mine, theirs)

    @pl.when(step == last)
    def out_part():
        for copy in copies:
            copy.wait()
        value = lax.dot_general(
            lefts[0:valid, :], rights[0:valid, :], TN, preferred_element_type=F32
        )
        split_by_core(value, rows, coords[3] == 0, mine, theirs)


def up_grad(place, left, right, out_left, out_right, valid):
    count, width = left.shape
    rows = width // place.count
    steps = right.shape[1] // width + 1
    anywhere = pl.BlockSpec(memory_space=pl.ANY)
    out = pl.BlockSpec((place.count // 2, rows, width), lambda i, c: (0, 0, i))
    outs = struct((place.count // 2, rows, steps * width), BF)
    return pl.pallas_call(
        partial(up_grad_kernel, valid, rows),
        grid_spec=pltpu.PrefetchScalarGridSpec(
            num_scalar_prefetch=1,
            grid=(steps,),
            in_specs=[
                pl.BlockSpec((count, width), lambda i, c: (0, 0)),
                pl.BlockSpec((count, width), lambda i, c: (0, jnp.minimum(i, steps - 2))),
                anywhere,
                anywhere,
            ],
            out_specs=[out, out],
            scratch_shapes=[
                pltpu.VMEM((count, width), BF),
                pltpu.VMEM((count, width), BF),
                pltpu.SemaphoreType.DMA((2,)),
            ],
        ),
        out_shape=[outs, outs],
        compiler_params=params(),
        cost_estimate=cost(
            2 * count * steps * width * width, 2 * (count + width) * (steps + 1) * width
        ),
        name="grad_up_and_out",
    )(place.coords, left, right, out_left, out_right)


def qkv_grad_kernel(
    valid, rows, coords, left, right, sums, more, mine, theirs, kept, sent, entries, sems
):
    step = pl.program_id(0)
    width = left.shape[1]
    first = coords[3] == 0

    def copies(start, size, number):
        lanes = pl.ds(start, size)
        return (
            pltpu.make_async_copy(kept.at[:, :, lanes], mine.at[:, :, lanes], sems.at[0, number]),
            pltpu.make_async_copy(sent.at[:, :, lanes], theirs.at[:, :, lanes], sems.at[1, number]),
        )

    for which in range(3):

        @pl.when(step == which)
        def part(which=which):
            lanes = slice(which * width, (which + 1) * width)
            value = lax.dot_general(
                left[0:valid, :], right[0, 0:valid, :], TN, preferred_element_type=F32
            )
            split_by_core(value, rows, first, kept.at[:, :, lanes], sent.at[:, :, lanes])
            for copy in copies(which * width, width, which):
                copy.start()

    @pl.when(step == 2)
    def vector_part():
        pieces = width // 128
        entries[...] = jnp.zeros_like(entries)
        for row in range(12):
            value = sums[row : row + 1, :]
            if row < 2:
                value = value + more[row : row + 1, :]
            for j in range(pieces):
                entries[row * pieces + j : row * pieces + j + 1, :] = value[
                    :, j * 128 : (j + 1) * 128
                ]
        blank = jnp.zeros((rows - 4, 128), F32)
        lanes = slice(3 * width, 3 * width + 128)
        for chip in range(kept.shape[0]):
            windows = []
            for device in (2 * chip, 2 * chip + 1):
                start = 9 * (device // 4) + 2 * (device % 4)
                windows.append(jnp.concatenate([entries[start : start + 4, :], blank], axis=0))
            kept[chip, :, lanes] = jnp.where(first, windows[0], windows[1]).astype(BF)
            sent[chip, :, lanes] = jnp.where(first, windows[1], windows[0]).astype(BF)
        for copy in copies(3 * width, 128, 3):
            copy.start()
        for which in range(3):
            for copy in copies(which * width, width, which):
                copy.wait()
        for copy in copies(3 * width, 128, 3):
            copy.wait()


def qkv_grad(place, left, right, sums, more, valid):
    count, width = left.shape
    rows = width // place.count
    wire = (place.count // 2, rows, 3 * width + 128)
    anywhere = pl.BlockSpec(memory_space=pl.ANY)
    return pl.pallas_call(
        partial(qkv_grad_kernel, valid, rows),
        grid_spec=pltpu.PrefetchScalarGridSpec(
            num_scalar_prefetch=1,
            grid=(3,),
            in_specs=[
                pl.BlockSpec((count, width), lambda i, c: (0, 0)),
                pl.BlockSpec((1, count, width), lambda i, c: (i, 0, 0)),
                pl.BlockSpec(sums.shape, lambda i, c: (0, 0)),
                pl.BlockSpec(more.shape, lambda i, c: (0, 0)),
            ],
            out_specs=[anywhere, anywhere],
            scratch_shapes=[
                pltpu.VMEM(wire, BF),
                pltpu.VMEM(wire, BF),
                pltpu.VMEM((80, 128), F32),
                pltpu.SemaphoreType.DMA((2, 4)),
            ],
        ),
        out_shape=[struct(wire, BF)] * 2,
        compiler_params=params(),
        cost_estimate=cost(6 * count * width * width, 8 * (count + width) * width),
        name="grad_qkv",
    )(place.coords, left, right, sums, more)


def frames_grad_kernel(first_g, grads, weights, out):
    value = first_g[...]
    for which in range(3):
        value = value + lax.dot_general(
            grads[which], weights[which], NT, preferred_element_type=F32
        )
    out[...] = value.astype(BF)


def frames_gradient(first_g, grads, weights, tile=256):
    count, width = first_g.shape
    row_tile = pl.BlockSpec((tile, width), lambda i: (i, 0))
    return pl.pallas_call(
        frames_grad_kernel,
        grid=(count // tile,),
        in_specs=[
            row_tile,
            pl.BlockSpec((3, tile, width), lambda i: (0, i, 0)),
            pl.BlockSpec(weights.shape, lambda i: (0, 0, 0)),
        ],
        out_specs=row_tile,
        out_shape=struct((count, width), BF),
        compiler_params=params(),
        cost_estimate=cost(6 * count * width * width, 12 * count * width + 6 * width * width),
        name="frames_gradient",
    )(first_g, grads, weights)


def adam_update(master, first, second, gradient, step_rate, decay_rate):
    first_new = BETA_FIRST * first + (1.0 - BETA_FIRST) * gradient
    second_new = BETA_SECOND * second + (1.0 - BETA_SECOND) * gradient * gradient
    first_hat = first_new / (1.0 - BETA_FIRST**STEP)
    second_hat = second_new / (1.0 - BETA_SECOND**STEP)
    updated = master - step_rate * (
        first_hat / (jnp.sqrt(second_hat) + ADAM_EPS) + decay_rate * master
    )
    return (first_new, second_new, updated, updated.astype(BF))


def segment_marks(length_row, frame_count):
    clip_ends = jnp.cumsum(length_row)
    position = jnp.arange(frame_count, dtype=jnp.int32)
    segment = jnp.sum((clip_ends[None, :] <= position[:, None]).astype(jnp.int32), axis=1)
    lane = jnp.arange(128, dtype=jnp.int32)[None, :] % 64
    same = lane == segment[:, None]
    q_mark = jnp.where(same, 1.0, 0.0).astype(BF)
    k_mark = jnp.where(same | (lane >= 8), 0.0, -MASKED).astype(BF)
    return q_mark, k_mark, clip_ends[-1:].astype(jnp.int32)


def gather_vector(place, shard):
    blank = jnp.zeros((place.count, shard.shape[0]), BF)
    own = lax.dynamic_update_slice(blank, shard[None, :], (place.index, 0))
    return place.total(own)


def after(values, things):
    return lax.optimization_barrier((values, things))[0]


def shards(n_dp, n_fsdp, *arrays):
    (
        frames, cotangent, lengths, qkv_master, out_master, up_master, down_master, vector_master,
        qkv_first, qkv_second, out_first, out_second, up_first, up_second, down_first,
        down_second, vector_first, vector_second,
    ) = arrays
    place = Place(n_dp, n_fsdp)
    frame_count, width = frames.shape
    hidden = up_master.shape[1]
    rows = out_master.shape[0]
    valid = min(frame_count, -(-MOST_VALID // 16) * 16)
    fast = n_dp == 4 and place.depth == 4 and rows == 24

    q_mark, k_mark, total = segment_marks(lengths[0], frame_count)
    if fast:
        qkv_wire, wire_low = pack(
            place, qkv_master, out_master, up_master, down_master, vector_master[None, :]
        )
        wire = lax.all_gather(wire_low, AXES, axis=0, tiled=True)
        blocks = gather_blocks(place, qkv_wire)
        queries, keys, values, vector, qkv_full = project_qkv(place, frames, blocks)
        weights = (wire,)
    else:
        vector = gather_vector(place, vector_master.astype(BF)).astype(F32).reshape(-1, width)
        qkv_full = lax.all_gather(qkv_master.astype(BF), AXES, axis=1, tiled=True)
        projected = jnp.einsum("fd,cde->cfe", frames, qkv_full, preferred_element_type=F32)
        queries = (projected[0] + vector[0]).astype(BF)
        keys = projected[1].astype(BF)
        values = (projected[2] + vector[1]).astype(BF)
        weights = tuple(
            lax.all_gather(w.astype(BF), AXES, axis=0, tiled=True)
            for w in (out_master, up_master, down_master)
        )

    context, attention = attention_forward(queries, keys, values, q_mark, k_mark, valid)
    (
        result, normed, activated, down_g, up_g, first_g, attended_g, context_g, sums,
    ) = middle(frames, context, cotangent, vector, total, weights, hidden, valid)

    def attention_part(first, pairs, start, earlier=()):
        return attention_backward(
            lengths[0, 0:1], start, keys, values, context_g, attention, valid, first, pairs, earlier
        )

    if fast:
        down_mine, theirs = down_grad(place, activated, down_g, valid)
        down_got = place.swap_core(theirs)
        up_mine, theirs = up_grad(
            place, after(normed, down_mine), up_g, context, attended_g, valid
        )
        up_got = place.swap_core(theirs)
        all_sums = lax.all_gather(sums, AXES, axis=0)
        most = Reduction(place)
        done = most.first(after(down_mine, up_mine), down_got)
        grads = attention_part(0, 2, after(queries, done))
        done = most.first(after(up_mine, grads[1]), up_got)
        grads = attention_part(2, 3, after(queries, done), grads)
        most.parts[0] = after(most.parts[0], grads[1])
        done = most.second()
        qkv_g, bias_sums = attention_part(5, 1, after(queries, done), grads)
        mine, theirs = qkv_grad(place, frames, qkv_g, sums, bias_sums, valid)
        got = place.swap_core(theirs)
        most.sums, all_sums = after((most.sums, all_sums), mine)
        done = most.third()
        last = Reduction(place)
        done = last.first(after(mine, done), got)
        frames_grad = frames_gradient(after(first_g, done), qkv_g, qkv_full)
        most.sums = after(most.sums, frames_grad)
        done = most.fourth(0)
        last.parts[0] = after(last.parts[0], done)
        done = last.second(1000)
        squares = jnp.sum(after(all_sums, done)[:, 12:17], axis=(0, 2))
        layer_rms = jnp.sqrt(squares[0:4] / squares[4])
        last.sums = after(last.sums, layer_rms)
        done = last.spread(1000)
        most.sums = after(most.sums, done)
        grad_most = most.result()
        grad_qkv = last.result()
        grad_down = grad_most[:, : 4 * width].reshape(rows, 4, width)
        grad_down = grad_down.transpose(1, 0, 2).reshape(4 * rows, width)
        grad_up = grad_most[:, 4 * width : 8 * width]
        grad_out = grad_most[:, 8 * width :]
        window = grad_qkv[0:4, 3 * width :].reshape(-1)
        grad_vector = lax.dynamic_slice(
            window, (32 * (place.index % 4),), (vector_master.shape[0],)
        )
        grad_qkv = grad_qkv[:, : 3 * width].reshape(rows, 3, width).transpose(1, 0, 2)
    else:
        def scatter(value, dimension):
            return lax.psum_scatter(value, AXES, scatter_dimension=dimension, tiled=True)

        def product(left, right):
            return lax.dot_general(left, right, TN, preferred_element_type=F32)

        qkv_g, bias_sums = attention_part(0, HEADS // 2, queries)
        grad_down = scatter(product(activated, down_g), 0)
        grad_up = scatter(product(normed, up_g), 0)
        grad_out = scatter(product(context, attended_g), 0)
        grad_qkv = scatter(jnp.stack([product(frames, qkv_g[i]) for i in range(3)]), 1)
        frames_grad = frames_gradient(first_g, qkv_g, qkv_full)
        sums = place.total(sums + jnp.pad(bias_sums, ((0, 16), (0, 0))))
        grad_vector = lax.dynamic_slice(
            sums[0:12].reshape(-1),
            (place.index * vector_master.shape[0],),
            (vector_master.shape[0],),
        )
        layer_rms = jnp.sqrt(jnp.sum(sums[12:16], axis=1) / jnp.sum(sums[16]))

    down_new = adam_update(
        down_master, down_first, down_second, grad_down, MATRIX_RATE, WEIGHT_DECAY
    )
    up_new = adam_update(up_master, up_first, up_second, grad_up, MATRIX_RATE, WEIGHT_DECAY)
    out_new = adam_update(out_master, out_first, out_second, grad_out, MATRIX_RATE, WEIGHT_DECAY)
    qkv_new = adam_update(qkv_master, qkv_first, qkv_second, grad_qkv, MATRIX_RATE, WEIGHT_DECAY)
    vector_new = adam_update(
        vector_master, vector_first, vector_second, grad_vector, VECTOR_RATE, 0.0
    )
    return (
        (result, frames_grad, layer_rms) + qkv_new + out_new + up_new + down_new + vector_new
    )


def solution(mesh):
    rows = P(AXES, None)
    middle_rows = P(None, AXES, None)
    entries = P(AXES)
    return jax.shard_map(
        partial(shards, mesh.shape["dp"], mesh.shape["fsdp"]),
        mesh=mesh,
        in_specs=(
            rows, rows, rows, middle_rows, rows, rows, rows, entries,
            middle_rows, middle_rows, rows, rows, rows, rows, rows, rows, entries, entries,
        ),
        out_specs=(rows, rows, P())
        + (middle_rows,) * 4
        + (rows,) * 12
        + (entries,) * 4,
        check_vma=False,
    )
```
